256 devices in a mesh: cfg: 2 (over core), seq: 16 (over x, z_hi), dp: 8 (over y, z_lo).
Axes of the slice: x: 4, y: 4, z: 8 (z_hi: 4, z_lo: 2; z = z_hi * 2 + z_lo), core: 2. Of those that a mesh axis runs over, the one named last changes fastest.
Arguments:
- image_projections: bfloat16 [2, 16, 2048, 6144], P('cfg', 'dp', 'seq'), may hold values from -8 to 8
- text_projections: bfloat16 [2, 16, 512, 4096], P('cfg', 'dp', 'seq'), may hold values from -6 to 6
- output_weight: bfloat16 [2048, 3072], P('seq', 'dp'), may hold values from -0.125 to 0.125
- image_state: bfloat16 [2, 16, 2048, 3072], P('cfg', 'dp', 'seq'), may hold values from -6 to 6
- modulation: bfloat16 [2, 16, 3, 3072], P('cfg', 'dp'), may hold values from -4 to 4
- final_weight: bfloat16 [3072, 64], replicated, may hold values from -0.109375 to 0.109375
- latent: float32 [16, 2048, 64], P('dp', 'seq'), may hold values from -6 to 6
- next_latent: float32 [16, 2048, 64], P('dp', 'seq'), may hold values from -8 to 8
- timestep: float32 [16], P('dp'), may hold values from 0.3 to 0.8
- rewards: float32 [16], P('dp'), may hold values from -5 to 5
- group_index: int32 [16], P('dp'), may hold values from 0 to 7, as said below
Outputs:
- grad_final_weight: float32 [3072, 64], P('dp')
- log_prob: float32 [16], P('dp')
The draws below stay inside these ranges and needn't reach their ends.
Inputs may be any that keep to these rules, and one draw needn't show every extreme that they name: `group_index`: each of the 8 prompts has exactly 2 rollouts; rollout 0 shares its prompt with one of the last 2 rollouts.
All inputs are finite; a program needn't handle non-finite values.
Results may differ from the reference program's by a relative error of at most 0.00053.
Values may be sent and summed in bfloat16 or wider, within the bound.
No kernel may reach another device: no remote copies, remote signals or barrier semaphores. Data moves between devices by JAX's collectives and lax.ppermute only.
A program may use at most 64 MiB of HBM per device.

```python
import math
import jax
import jax.numpy as jnp
from jax import lax

D = 3072
C = 64
HD = 128
RPD = 2
GROUP_SIZE = 2
HEADS = 16
HW = 2048
IMG = 2048
TXT = 512
ROLLOUTS = 16
GROUPS = 8


def draw_image_projections(key, part):
    key = jax.random.fold_in(key, 11)
    base_key = jax.random.fold_in(key, 0)
    shape = (2, ROLLOUTS, IMG, 3, HW)
    values = jax.random.normal(base_key, shape, jnp.float32)
    factor = jnp.array([2.5, 1.0, 1.0], jnp.float32).reshape(1, 1, 1, 3, 1)
    values = jnp.clip(values * factor, -8.0, 8.0)
    return values.reshape(2, ROLLOUTS, IMG, 3 * HW).astype(jnp.bfloat16)


def latent_base(key):
    return jnp.clip(jax.random.normal(key, (ROLLOUTS, IMG, C), jnp.float32), -6.0, 6.0)


def draw_latent(key, part):
    return latent_base(key)


def draw_next_latent(key, part):
    base = latent_base(key)
    key = jax.random.fold_in(key, 23)
    return jnp.clip(base + 0.15 * jax.random.normal(key, base.shape, jnp.float32), -8.0, 8.0)


def draw_group_index(key, part):
    key = jax.random.fold_in(key, 31)
    pick_key, order_key, label_key = jax.random.split(key, 3)
    chosen = ROLLOUTS - RPD + jax.random.randint(pick_key, (), 0, RPD).astype(jnp.int32)
    candidates = jnp.arange(1, ROLLOUTS - 1, dtype=jnp.int32)
    remaining = jnp.where(candidates >= chosen, candidates + 1, candidates)
    shuffled = jax.random.permutation(order_key, remaining)
    groups = jnp.zeros((ROLLOUTS,), jnp.int32)
    groups = groups.at[shuffled].set(1 + jnp.arange(ROLLOUTS - 2, dtype=jnp.int32) // 2)
    groups = groups.at[0].set(0)
    groups = groups.at[chosen].set(0)
    labels = jax.random.permutation(label_key, GROUPS).astype(jnp.int32)
    return labels[groups].astype(jnp.int32)


def block_scale(key, shape, cuts, least, high):
    def one(axis_at, shards_of):
        draws = jax.random.uniform(jax.random.fold_in(jax.random.fold_in(key, 6), axis_at), (shards_of,), jnp.float32, least / len(cuts), high / len(cuts))
        return jnp.repeat(jnp.exp(draws), shape[axis_at] // shards_of).reshape((-1,) + (1,) * (len(shape) - axis_at - 1))

    factor_of = one(*cuts[0])
    for cut in cuts[1:]:
        factor_of = factor_of * one(*cut)
    return factor_of


def gaussian(stream_key, shape, scale, bound, shards=(), kind=jnp.bfloat16):
    level = block_scale(stream_key, shape, shards, -0.22, 0.18) if shards else 1.0
    result = jax.random.normal(stream_key, shape, jnp.float32) * scale * level
    return jnp.minimum(jnp.maximum(result, -bound), bound).astype(kind)


def setup_inputs(seed: int = 0) -> dict:
    arg_keys = jax.random.split(jax.random.key(seed), 12)
    image_projections = draw_image_projections(jax.random.fold_in(arg_keys[11], 71), 0)
    text_projections = gaussian(arg_keys[1], (2, ROLLOUTS, TXT, 2 * HW), 1.0, 6.0, ((0, 2), (1, 8), (2, 16)))
    output_weight = gaussian(arg_keys[2], (HW, D), HW ** -0.5, 0.125, ((0, 16), (1, 8)))
    image_state = gaussian(arg_keys[3], (2, ROLLOUTS, IMG, D), 1.0, 6.0, ((0, 2), (1, 8), (2, 16)))
    modulation = gaussian(arg_keys[4], (2, ROLLOUTS, 3, D), 0.8, 4.0, ((0, 2), (1, 8)))
    final_weight = gaussian(arg_keys[5], (D, C), D ** -0.5, 0.109375)
    latent = draw_latent(jax.random.fold_in(arg_keys[11], 71), 0)
    next_latent = draw_next_latent(jax.random.fold_in(arg_keys[11], 71), 0)
    timestep = jnp.clip(0.3 + 0.5 * jax.random.uniform(arg_keys[8], (ROLLOUTS,), jnp.float32) ** block_scale(arg_keys[8], (ROLLOUTS,), ((0, 8),), -0.2, 0.2), 0.3, 0.8)
    rewards = gaussian(arg_keys[9], (ROLLOUTS,), 1.0, 5.0, ((0, 8),), jnp.float32)
    group_index = draw_group_index(jax.random.fold_in(arg_keys[11], 71), 0)
    return {"image_projections": image_projections, "text_projections": text_projections, "output_weight": output_weight, "image_state": image_state, "modulation": modulation, "final_weight": final_weight, "latent": latent, "next_latent": next_latent, "timestep": timestep, "rewards": rewards, "group_index": group_index}


cfg_scale = 4.5
noise_level = 0.7
step_width = 0.02
norm_eps = 1e-06

def attend(query, key_rows, value_rows):
    scores = jnp.dot(query.astype(jnp.float32), key_rows.astype(jnp.float32).T) * (1.0 / math.sqrt(HD))
    highest = lax.optimization_barrier(jnp.max(scores, axis=1, keepdims=True))
    powered = jnp.exp(scores - highest)
    weights = (powered / lax.optimization_barrier(jnp.sum(powered, axis=1, keepdims=True))).astype(jnp.bfloat16)
    return jnp.dot(weights.astype(jnp.float32), value_rows.astype(jnp.float32)).astype(jnp.bfloat16)

def modulate(mixed_rows, modulation_rows):
    center = lax.optimization_barrier(jnp.sum(mixed_rows, axis=1, keepdims=True)) / D
    square = lax.optimization_barrier(jnp.sum(mixed_rows * mixed_rows, axis=1, keepdims=True)) / D
    normed = (mixed_rows - center) * lax.rsqrt(square - center * center + norm_eps)
    scale_rows = modulation_rows[2][None, :].astype(jnp.float32)
    shift_rows = modulation_rows[1][None, :].astype(jnp.float32)
    return (normed * (1.0 + scale_rows) + shift_rows).astype(jnp.bfloat16)

def final_hidden(image_rows, text_rows, state_rows, modulation_rows, output_weight):
    queries = image_rows[:, :HW].reshape(IMG, HEADS, HD).transpose(1, 0, 2)
    key_rows = jnp.concatenate([image_rows[:, HW:2 * HW], text_rows[:, :HW]], 0)
    key_rows = key_rows.reshape(IMG + TXT, HEADS, HD).transpose(1, 0, 2)
    value_rows = jnp.concatenate([image_rows[:, 2 * HW:], text_rows[:, HW:]], 0)
    value_rows = value_rows.reshape(IMG + TXT, HEADS, HD).transpose(1, 0, 2)

    def per_head(triple):
        return attend(triple[0], triple[1], triple[2])
    mixed_heads = lax.map(per_head, (queries, key_rows, value_rows))
    attention = mixed_heads.transpose(1, 0, 2).reshape(IMG, HW)
    projected = jnp.dot(attention, output_weight, preferred_element_type=jnp.float32)
    gate_rows = modulation_rows[0][None, :].astype(jnp.float32)
    mixed_rows = state_rows.astype(jnp.float32) + gate_rows * projected
    return modulate(mixed_rows, modulation_rows)

def step_terms(conditional, unconditional, latent, next_latent, timestep, advantage, rollouts):
    guided = unconditional + cfg_scale * (conditional - unconditional)
    moment = timestep[:, None, None]
    spread = noise_level * jnp.sqrt(moment / (1.0 - moment))
    drift_gain = 1.0 + spread * spread * (1.0 - moment) / (2.0 * moment)
    step_mean = latent * (1.0 - spread * spread / (2.0 * moment) * step_width) - guided * drift_gain * step_width
    deviation = spread * math.sqrt(step_width)
    residue = next_latent - step_mean
    density = -residue * residue / (2.0 * deviation * deviation) - jnp.log(deviation) - 0.5 * math.log(2.0 * math.pi)
    slopes = advantage[:, None, None] / (rollouts * C) * drift_gain * step_width / (deviation * deviation) * residue
    return (density, slopes)

def reference(image_projections, text_projections, output_weight, image_state, modulation, final_weight, latent, next_latent, timestep, rewards, group_index):
    flat_image = image_projections.reshape(2 * ROLLOUTS, IMG, 3 * HW)
    flat_text = text_projections.reshape(2 * ROLLOUTS, TXT, 2 * HW)
    flat_state = image_state.reshape(2 * ROLLOUTS, IMG, D)
    flat_mod = modulation.reshape(2 * ROLLOUTS, 3, D)

    def per_pass(pieces):
        return final_hidden(pieces[0], pieces[1], pieces[2], pieces[3], output_weight)
    hidden = lax.map(per_pass, (flat_image, flat_text, flat_state, flat_mod))
    velocity = jnp.dot(hidden.reshape(-1, D), final_weight, preferred_element_type=jnp.float32)
    velocity = velocity.reshape(2, ROLLOUTS, IMG, C)
    member = (group_index[:, None] == jnp.arange(GROUPS, dtype=jnp.int32)[None, :]).astype(jnp.float32)
    totals = lax.optimization_barrier(jnp.sum(member * rewards[:, None], axis=0))
    advantage = rewards - lax.optimization_barrier(jnp.sum(member * totals[None, :], axis=1)) / GROUP_SIZE
    density, slopes = step_terms(velocity[0], velocity[1], latent, next_latent, timestep, advantage, ROLLOUTS)
    log_prob = lax.optimization_barrier(jnp.sum(density, axis=(1, 2))) / (IMG * C)
    cond_slopes = (cfg_scale * slopes).astype(jnp.bfloat16)
    uncond_slopes = ((1.0 - cfg_scale) * slopes).astype(jnp.bfloat16)
    gradient = jnp.dot(hidden[:ROLLOUTS].reshape(-1, D).T, cond_slopes.reshape(-1, C), preferred_element_type=jnp.float32)
    gradient = gradient + jnp.dot(hidden[ROLLOUTS:].reshape(-1, D).T, uncond_slopes.reshape(-1, C), preferred_element_type=jnp.float32)
    return (gradient, log_prob)
```

```python
import math

import jax
import jax.numpy as jnp
from jax import lax
from jax.experimental import pallas as pl
from jax.experimental.pallas import tpu as pltpu
from jax.sharding import PartitionSpec as P

C = 64
HD = 128
GROUP_SIZE = 2

cfg_scale = 4.5
noise_level = 0.7
step_width = 0.02
norm_eps = 1e-06

X, ZH, Y, ZL = 4, 4, 4, 2
VMEM_BYTES = 56 * 1024 * 1024


def from_x(value, d):
    pairs = [(((x + d) % X) * ZH + z, x * ZH + z) for x in range(X) for z in range(ZH)]
    return lax.ppermute(value, "seq", pairs)


def from_zh(value, d):
    pairs = [(x * ZH + (z + d) % ZH, x * ZH + z) for x in range(X) for z in range(ZH)]
    return lax.ppermute(value, "seq", pairs)


def from_y(value, d):
    pairs = [(((y + d) % Y) * ZL + z, y * ZL + z) for y in range(Y) for z in range(ZL)]
    return lax.ppermute(value, "dp", pairs)


def from_zl(value):
    pairs = [(y * ZL + 1 - z, y * ZL + z) for y in range(Y) for z in range(ZL)]
    return lax.ppermute(value, "dp", pairs)


def from_cfg(value):
    return lax.ppermute(value, "cfg", [(0, 1), (1, 0)])


def ring_sum(value, fetch):
    first, second, third = (fetch(value, d) for d in (1, 2, 3))
    return (value + second) + (first + third)


def pack_kernel(q_ref, k_ref, v_ref, kt_ref, vt_ref, out_ref):
    rows, text = q_ref.shape[2], kt_ref.shape[2]
    for h in range(out_ref.shape[0]):
        cols = slice(h * HD, (h + 1) * HD)
        out_ref[h, 0:rows, :] = q_ref[0, 0, :, cols]
        out_ref[h, rows : 2 * rows, :] = k_ref[0, 0, :, cols]
        out_ref[h, 2 * rows : 2 * rows + text, :] = kt_ref[0, 0, :, cols]
        out_ref[h, 2 * rows + text : 3 * rows + text, :] = v_ref[0, 0, :, cols]
        out_ref[h, 3 * rows + text : 3 * rows + 2 * text, :] = vt_ref[0, 0, :, cols]


def pack(image_projections, text_projections, r):
    rows, text = image_projections.shape[2], text_projections.shape[2]
    heads = image_projections.shape[3] // (3 * HD)
    per = 4
    steps = heads // per
    total = 3 * rows + 2 * text

    def spec(count, part):
        return pl.BlockSpec((1, 1, count, per * HD), lambda h: (0, r, 0, part * steps + h))

    return pl.pallas_call(
        pack_kernel,
        grid=(steps,),
        in_specs=[spec(rows, 0), spec(rows, 1), spec(rows, 2), spec(text, 0), spec(text, 1)],
        out_specs=pl.BlockSpec((per, total, HD), lambda h: (h, 0, 0)),
        out_shape=jax.ShapeDtypeStruct((heads, total, HD), jnp.bfloat16),
        compiler_params=pltpu.CompilerParams(vmem_limit_bytes=32 * 1024 * 1024),
        cost_estimate=pl.CostEstimate(
            flops=0, bytes_accessed=2 * heads * total * HD * 2, transcendentals=0
        ),
        name=f"pack{r}",
    )(image_projections, image_projections, image_projections, text_projections, text_projections)


def attention_kernel(parts_ref, out_ref, keys, values):
    peers = parts_ref.shape[0]
    per_step, rows = out_ref.shape[0], out_ref.shape[1]
    kv_rows = keys.shape[0] // peers
    step = pl.program_id(0)

    @pl.when(step == 0)
    def _():
        ones = jnp.ones((kv_rows, HD), jnp.bfloat16)
        for s in range(peers):
            at = slice(s * kv_rows, (s + 1) * kv_rows)
            keys[at, :] = parts_ref[s, rows : rows + kv_rows, :]
            values[at, 0:HD] = parts_ref[s, rows + kv_rows : rows + 2 * kv_rows, :]
            values[at, HD : 2 * HD] = ones

    factor = math.log2(math.e) / math.sqrt(HD)
    queries = parts_ref[pl.ds(step * per_step, per_step), 0:rows, :].reshape(per_step * rows, HD)
    scores = lax.dot_general(
        queries, keys[...], (((1,), (1,)), ((), ())), preferred_element_type=jnp.float32
    )
    highest = jnp.max(scores, axis=1, keepdims=True)
    powered = jnp.exp2((scores - highest) * factor).astype(jnp.bfloat16)
    sums = jnp.dot(powered, values[...], preferred_element_type=jnp.float32)
    result = sums[:, 0:HD] / sums[:, HD : HD + 1]
    out_ref[...] = result.astype(jnp.bfloat16).reshape(per_step, rows, HD)


def attention(parts, rows, per_step=2):
    peers, total, _ = parts.shape
    kv_rows = (total - rows) // 2
    return pl.pallas_call(
        attention_kernel,
        grid=(peers // per_step,),
        in_specs=[pl.BlockSpec((peers, total, HD), lambda i: (0, 0, 0))],
        out_specs=pl.BlockSpec((per_step, rows, HD), lambda i: (i, 0, 0)),
        out_shape=jax.ShapeDtypeStruct((peers, rows, HD), jnp.bfloat16),
        scratch_shapes=[
            pltpu.VMEM((peers * kv_rows, HD), jnp.bfloat16),
            pltpu.VMEM((peers * kv_rows, 2 * HD), jnp.bfloat16),
        ],
        compiler_params=pltpu.CompilerParams(vmem_limit_bytes=VMEM_BYTES),
        cost_estimate=pl.CostEstimate(
            flops=8 * peers * rows * peers * kv_rows * HD,
            bytes_accessed=2 * peers * total * HD,
            transcendentals=peers * rows * peers * kv_rows,
        ),
        name="attention",
    )(parts)


def hidden_kernel(place, heads_ref, state_ref, mods_ref, final_ref, *rest):
    pieces, (hidden_ref, velocity_ref, flat, mixed, weights, sems) = rest[:10], rest[10:]
    x_at, zh_at, y_at, c_at = place[0], place[1], place[2], place[3]
    heads = heads_ref.shape[0]
    depth = heads * HD
    width = weights.shape[2]
    half = heads // 2
    spans = ((0, 0, heads), (1, 0, heads), (3, 0, heads), (2, 0, half), (2, half, half))
    copies = []
    for core in range(2):
        for n, (turn, first, count) in enumerate(spans):
            copy = pltpu.make_async_copy(
                pieces[core * 5 + n],
                weights.at[core * 4 + turn, pl.ds(first * HD, count * HD)],
                sems.at[core * 5 + n],
            )
            copy.start()
            copies.append(copy)
    for i in range(X):
        for j in range(ZH):
            head = lax.rem(x_at + i, X) * ZH + lax.rem(zh_at + j, ZH)
            k = i * ZH + j
            flat[:, k * HD : (k + 1) * HD] = heads_ref[head]
    rows = flat.shape[0]
    row_sum = jnp.zeros((rows, 1), jnp.float32)
    square_sum = jnp.zeros((rows, 1), jnp.float32)
    for core in range(2):
        core_at = c_at if core == 0 else 1 - c_at
        for turn, needed in ((0, (0,)), (1, (1,)), (3, (2,)), (2, (3, 4))):
            for n in needed:
                copies[core * 5 + n].wait()
            at = pl.ds(pl.multiple_of((lax.rem(y_at + turn, Y) * ZL + core_at) * width, 128), width)
            projected = jnp.dot(
                flat[...], weights[core * 4 + turn], preferred_element_type=jnp.float32
            )
            gate = mods_ref[0, 0:1, at].astype(jnp.float32)
            block = state_ref[0, 0, :, at].astype(jnp.float32) + gate * projected
            mixed[:, at] = block
            row_sum = row_sum + jnp.sum(block, axis=1, keepdims=True)
            square_sum = square_sum + jnp.sum(block * block, axis=1, keepdims=True)
    width_all = mixed.shape[1]
    center = row_sum / width_all
    square = square_sum / width_all
    inverse = lax.rsqrt(square - center * center + norm_eps)
    scale = 1.0 + mods_ref[0, 2:3, :].astype(jnp.float32)
    shift = mods_ref[0, 1:2, :].astype(jnp.float32)
    hidden = ((mixed[...] - center) * inverse * scale + shift).astype(jnp.bfloat16)
    hidden_ref[...] = hidden
    velocity_ref[...] = jnp.dot(hidden, final_ref[...], preferred_element_type=jnp.float32)


def hidden_rows(place, heads_part, image_state, modulation, final_weight, pieces, r):
    heads, rows, _ = heads_part.shape
    width_all = image_state.shape[3]
    width = pieces[0].shape[1]
    whole = pl.BlockSpec(memory_space=pltpu.VMEM)
    return pl.pallas_call(
        hidden_kernel,
        grid=(1,),
        in_specs=[
            pl.BlockSpec(memory_space=pltpu.SMEM),
            pl.BlockSpec((heads, rows, HD), lambda i: (0, 0, 0)),
            pl.BlockSpec((1, 1, rows, width_all), lambda i: (0, r, 0, 0)),
            pl.BlockSpec((1, 3, width_all), lambda i: (r, 0, 0)),
            pl.BlockSpec((width_all, C), lambda i: (0, 0)),
        ]
        + [pl.BlockSpec(memory_space=pl.ANY)] * 10,
        out_specs=[
            pl.BlockSpec((rows, width_all), lambda i: (0, 0)),
            pl.BlockSpec((rows, C), lambda i: (0, 0)),
        ],
        out_shape=[
            jax.ShapeDtypeStruct((rows, width_all), jnp.bfloat16),
            jax.ShapeDtypeStruct((rows, C), jnp.float32),
        ],
        scratch_shapes=[
            pltpu.VMEM((rows, heads * HD), jnp.bfloat16),
            pltpu.VMEM((rows, width_all), jnp.float32),
            pltpu.VMEM((8, heads * HD, width), jnp.bfloat16),
            pltpu.SemaphoreType.DMA((10,)),
        ],
        compiler_params=pltpu.CompilerParams(vmem_limit_bytes=VMEM_BYTES),
        cost_estimate=pl.CostEstimate(
            flops=2 * rows * heads * HD * width_all,
            bytes_accessed=2 * heads * HD * width_all,
            transcendentals=0,
        ),
        name=f"hidden{r}",
    )(place, heads_part, image_state, modulation, final_weight, *pieces)


def gather_weight(output_weight, zl_at, c_at):
    depth, width = output_weight.shape
    mine = jnp.where(zl_at == c_at, output_weight, from_zl(output_weight))
    column = jnp.concatenate([mine] + [from_zh(mine, d) for d in range(1, ZH)], axis=0)
    plane = jnp.concatenate([column] + [from_x(column, d) for d in range(1, X)], axis=0)
    cut = plane.shape[0] // 2
    ahead = from_y(plane, 1)
    behind = from_y(plane, -1)
    far_first = from_y(ahead[:cut], 1)
    far_second = from_y(behind[cut:], -1)
    own = [plane, ahead, behind, far_first, far_second]
    return own + [from_cfg(piece) for piece in own]


def step_terms(conditional, unconditional, latent, next_latent, timestep, advantage, rollouts):
    guided = unconditional + cfg_scale * (conditional - unconditional)
    moment = timestep[:, None, None]
    spread = noise_level * jnp.sqrt(moment / (1.0 - moment))
    drift_gain = 1.0 + spread * spread * (1.0 - moment) / (2.0 * moment)
    step_mean = (
        latent * (1.0 - spread * spread / (2.0 * moment) * step_width)
        - guided * drift_gain * step_width
    )
    deviation = spread * math.sqrt(step_width)
    residue = next_latent - step_mean
    density = (
        -residue * residue / (2.0 * deviation * deviation)
        - jnp.log(deviation)
        - 0.5 * math.log(2.0 * math.pi)
    )
    slopes = (
        advantage[:, None, None]
        / (rollouts * C)
        * drift_gain
        * step_width
        / (deviation * deviation)
        * residue
    )
    return (density, slopes)


def exchange(send):
    return lax.all_to_all(send, "seq", split_axis=0, concat_axis=0, tiled=True)


def per_device(
    image_projections,
    text_projections,
    output_weight,
    image_state,
    modulation,
    final_weight,
    latent,
    next_latent,
    timestep,
    rewards,
    group_index,
):
    seq_count = lax.axis_size("seq")
    data_count = lax.axis_size("dp")
    per_dev = image_projections.shape[1]
    image_count = image_projections.shape[2]
    width_all = image_state.shape[3]
    rollouts = per_dev * data_count
    seq_at, dp_at, c_at = lax.axis_index("seq"), lax.axis_index("dp"), lax.axis_index("cfg")
    x_at, zh_at, y_at, zl_at = seq_at // ZH, seq_at % ZH, dp_at // ZL, dp_at % ZL
    place = jnp.stack([x_at, zh_at, y_at, c_at]).astype(jnp.int32)

    parts = [
        exchange(pack(image_projections, text_projections, r)) for r in range(per_dev)
    ]
    pieces = gather_weight(output_weight, zl_at, c_at)

    group_count = rollouts // GROUP_SIZE
    member = (group_index[:, None] == jnp.arange(group_count, dtype=jnp.int32)[None, :]).astype(
        jnp.float32
    )
    totals = jnp.sum(member * rewards[:, None], axis=0)
    totals = totals + from_zl(totals)
    totals = ring_sum(totals, from_y)
    advantage = rewards - jnp.sum(member * totals[None, :], axis=1) / GROUP_SIZE

    returned = [exchange(attention(part, image_count)) for part in parts]
    mods_local = modulation[0]
    rows = [
        hidden_rows(place, returned[r], image_state, mods_local, final_weight, pieces, r)
        for r in range(per_dev)
    ]
    hidden = jnp.concatenate([row[0] for row in rows], axis=0)
    velocity = jnp.stack([row[1] for row in rows])
    partner = from_cfg(velocity)
    is_first = c_at == 0
    cond_velocity = jnp.where(is_first, velocity, partner)
    unconditional = jnp.where(is_first, partner, velocity)
    density, slopes = step_terms(
        cond_velocity, unconditional, latent, next_latent, timestep, advantage, rollouts
    )
    factor = jnp.where(is_first, cfg_scale, 1.0 - cfg_scale)
    own_slopes = (factor * slopes).astype(jnp.bfloat16)
    log_sums = jnp.sum(density, axis=(1, 2))

    partial = lax.dot_general(
        own_slopes.reshape(-1, C), hidden, (((0,), (0,)), ((), ())), preferred_element_type=jnp.float32
    )
    col_count = width_all // data_count
    half = C // 2
    partial = partial.reshape(2, half, data_count, col_count).transpose(0, 2, 1, 3)
    kept = jnp.where(is_first, partial[0], partial[1]) + from_cfg(
        jnp.where(is_first, partial[1], partial[0])
    )
    spread_parts = lax.all_to_all(kept, "dp", split_axis=0, concat_axis=0, tiled=True)
    share = jnp.sum(spread_parts, axis=0)
    share = share.reshape(half * col_count // 128, 128)
    tail = jnp.concatenate(
        [jnp.broadcast_to(log_sums[:, None], (per_dev, 128)), jnp.zeros((8 - per_dev, 128), jnp.float32)]
    )
    share = jnp.concatenate([share, tail], axis=0)
    share = ring_sum(ring_sum(share, from_zh), from_x)
    log_sum = share[-8 : per_dev - 8, 0]
    log_prob = log_sum / (seq_count * image_count * C)
    share = share[:-8].reshape(half, col_count)
    other = from_cfg(share)
    first = jnp.where(is_first, share, other)
    second = jnp.where(is_first, other, share)
    gradient = jnp.concatenate([first, second], axis=0).T
    return (gradient, log_prob)


def solution(mesh):
    in_specs = (
        P("cfg", "dp", "seq", None),
        P("cfg", "dp", "seq", None),
        P("seq", "dp"),
        P("cfg", "dp", "seq", None),
        P("cfg", "dp", None, None),
        P(),
        P("dp", "seq", None),
        P("dp", "seq", None),
        P("dp"),
        P("dp"),
        P("dp"),
    )
    out_specs = (P("dp", None), P("dp"))
    return jax.shard_map(
        per_device, mesh=mesh, in_specs=in_specs, out_specs=out_specs, check_vma=False
    )
```

```python
import functools
import math

import jax
import jax.numpy as jnp
from jax import lax
from jax.experimental import pallas as pl
from jax.experimental.pallas import tpu as pltpu
from jax.sharding import PartitionSpec as P

C = 64
HD = 128
GROUP_SIZE = 2

cfg_scale = 4.5
noise_level = 0.7
step_width = 0.02
norm_eps = 1e-06

X, ZH, Y, ZL = 4, 4, 4, 2
VMEM_BYTES = 56 * 1024 * 1024


def from_x(value, d):
    pairs = [(((x + d) % X) * ZH + z, x * ZH + z) for x in range(X) for z in range(ZH)]
    return lax.ppermute(value, "seq", pairs)


def from_zh(value, d):
    pairs = [(x * ZH + (z + d) % ZH, x * ZH + z) for x in range(X) for z in range(ZH)]
    return lax.ppermute(value, "seq", pairs)


def from_y(value, d):
    pairs = [(((y + d) % Y) * ZL + z, y * ZL + z) for y in range(Y) for z in range(ZL)]
    return lax.ppermute(value, "dp", pairs)


def from_zl(value):
    pairs = [(y * ZL + 1 - z, y * ZL + z) for y in range(Y) for z in range(ZL)]
    return lax.ppermute(value, "dp", pairs)


def from_cfg(value):
    return lax.ppermute(value, "cfg", [(0, 1), (1, 0)])


def after(value, *others):
    return lax.optimization_barrier((value,) + others)[0]


def ring_sum(value, fetch):
    first, second, third = (fetch(value, d) for d in (1, 2, 3))
    return (value + second) + (first + third)


def pack_kernel(k_ref, v_ref, kt_ref, vt_ref, q_ref, out_ref):
    rows, text = k_ref.shape[2], kt_ref.shape[2]
    for h in range(out_ref.shape[0]):
        cols = slice(h * HD, (h + 1) * HD)
        at = 0
        for r in range(k_ref.shape[1]):
            for ref, count in ((k_ref, rows), (kt_ref, text), (v_ref, rows), (vt_ref, text)):
                out_ref[h, at : at + count, :] = ref[0, r, :, cols]
                at += count
        out_ref[h, at : at + rows, :] = q_ref[0, 0, :, cols]


def pack_queries_kernel(q_ref, out_ref):
    for h in range(out_ref.shape[0]):
        out_ref[h] = q_ref[0, 0, :, h * HD : (h + 1) * HD]


def pack(image_projections, text_projections):
    _, per_dev, rows, width = image_projections.shape
    text = text_projections.shape[2]
    heads = width // (3 * HD)
    per = 4
    steps = heads // per
    total = per_dev * 2 * (rows + text) + rows

    def spec(rollouts, count, part):
        return pl.BlockSpec((1, rollouts, count, per * HD), lambda h: (0, 0, 0, part * steps + h))

    return pl.pallas_call(
        pack_kernel,
        grid=(steps,),
        in_specs=[
            spec(per_dev, rows, 1),
            spec(per_dev, rows, 2),
            spec(per_dev, text, 0),
            spec(per_dev, text, 1),
            spec(1, rows, 0),
        ],
        out_specs=pl.BlockSpec((per, total, HD), lambda h: (h, 0, 0)),
        out_shape=jax.ShapeDtypeStruct((heads, total, HD), jnp.bfloat16),
        compiler_params=pltpu.CompilerParams(vmem_limit_bytes=32 * 1024 * 1024),
        cost_estimate=pl.CostEstimate(
            flops=0, bytes_accessed=2 * heads * total * HD * 2, transcendentals=0
        ),
        name="pack",
    )(image_projections, image_projections, text_projections, text_projections, image_projections)


def pack_queries(image_projections, r):
    _, _, rows, width = image_projections.shape
    heads = width // (3 * HD)
    return pl.pallas_call(
        pack_queries_kernel,
        grid=(1,),
        in_specs=[pl.BlockSpec((1, 1, rows, heads * HD), lambda i: (0, r, 0, 0))],
        out_specs=pl.BlockSpec((heads, rows, HD), lambda i: (0, 0, 0)),
        out_shape=jax.ShapeDtypeStruct((heads, rows, HD), jnp.bfloat16),
        compiler_params=pltpu.CompilerParams(vmem_limit_bytes=32 * 1024 * 1024),
        cost_estimate=pl.CostEstimate(
            flops=0, bytes_accessed=2 * heads * rows * HD * 2, transcendentals=0
        ),
        name="pack_queries",
    )(image_projections)


def attention_kernel(q_ref, kv_ref, out_ref, keys, values):
    peers, kv_rows = kv_ref.shape[0], kv_ref.shape[1] // 2
    ones = jnp.ones((kv_rows, HD), jnp.bfloat16)
    for s in range(peers):
        at = slice(s * kv_rows, (s + 1) * kv_rows)
        keys[at, :] = kv_ref[s, 0:kv_rows, :]
        values[at, 0:HD] = kv_ref[s, kv_rows : 2 * kv_rows, :]
        values[at, HD : 2 * HD] = ones

    factor = math.log2(math.e) / math.sqrt(HD)
    for n in range(peers):
        scores = lax.dot_general(
            q_ref[n], keys[...], (((1,), (1,)), ((), ())), preferred_element_type=jnp.float32
        )
        highest = jnp.max(scores, axis=1, keepdims=True)
        powered = jnp.exp2((scores - highest) * factor).astype(jnp.bfloat16)
        sums = jnp.dot(powered, values[...], preferred_element_type=jnp.float32)
        out_ref[n] = (sums[:, 0:HD] / sums[:, HD : HD + 1]).astype(jnp.bfloat16)


def attention(queries, q_at, key_values, kv_at, rows, kv_rows):
    peers = queries.shape[0]
    return pl.pallas_call(
        attention_kernel,
        grid=(1,),
        in_specs=[
            pl.BlockSpec((peers, rows, HD), lambda i: (0, q_at, 0)),
            pl.BlockSpec((peers, 2 * kv_rows, HD), lambda i: (0, kv_at, 0)),
        ],
        out_specs=pl.BlockSpec((peers, rows, HD), lambda i: (0, 0, 0)),
        out_shape=jax.ShapeDtypeStruct((peers, rows, HD), jnp.bfloat16),
        scratch_shapes=[
            pltpu.VMEM((peers * kv_rows, HD), jnp.bfloat16),
            pltpu.VMEM((peers * kv_rows, 2 * HD), jnp.bfloat16),
        ],
        compiler_params=pltpu.CompilerParams(vmem_limit_bytes=VMEM_BYTES),
        cost_estimate=pl.CostEstimate(
            flops=8 * peers * rows * peers * kv_rows * HD,
            bytes_accessed=2 * peers * (2 * rows + 2 * kv_rows) * HD,
            transcendentals=peers * rows * peers * kv_rows,
        ),
        name="attention",
    )(queries, key_values)


def hidden_kernel(r, place, heads_ref, state_ref, mods_ref, final_ref, *rest):
    pieces, (hidden_ref, velocity_ref, flat, mixed, weights, sems) = rest[:10], rest[10:]
    x_at, zh_at, y_at, c_at = place[0], place[1], place[2], place[3]
    heads = heads_ref.shape[0]
    depth = heads * HD
    width = weights.shape[2]
    half = heads // 2
    spans = ((0, 0, heads), (1, 0, heads), (3, 0, heads), (2, 0, half), (2, half, half))
    copies = []
    for core in range(2):
        for n, (turn, first, count) in enumerate(spans):
            copy = pltpu.make_async_copy(
                pieces[core * 5 + n],
                weights.at[core * 4 + turn, pl.ds(first * HD, count * HD)],
                sems.at[core * 5 + n],
            )
            copy.start()
            copies.append(copy)
    for i in range(X):
        for j in range(ZH):
            head = lax.rem(x_at + i, X) * ZH + lax.rem(zh_at + j, ZH)
            k = i * ZH + j
            flat[:, k * HD : (k + 1) * HD] = heads_ref[head]
    rows = flat.shape[0]
    row_sum = jnp.zeros((rows, 1), jnp.float32)
    square_sum = jnp.zeros((rows, 1), jnp.float32)
    for core in range(2):
        core_at = c_at if core == 0 else 1 - c_at
        for turn, needed in ((0, (0,)), (1, (1,)), (3, (2,)), (2, (3, 4))):
            for n in needed:
                copies[core * 5 + n].wait()
            at = pl.ds(pl.multiple_of((lax.rem(y_at + turn, Y) * ZL + core_at) * width, 128), width)
            projected = jnp.dot(
                flat[...], weights[core * 4 + turn], preferred_element_type=jnp.float32
            )
            gate = mods_ref[0, r : r + 1, at].astype(jnp.float32)
            block = state_ref[0, 0, :, at].astype(jnp.float32) + gate * projected
            mixed[:, at] = block
            row_sum = row_sum + jnp.sum(block, axis=1, keepdims=True)
            square_sum = square_sum + jnp.sum(block * block, axis=1, keepdims=True)
    width_all = mixed.shape[1]
    center = row_sum / width_all
    square = square_sum / width_all
    inverse = lax.rsqrt(square - center * center + norm_eps)
    scale = 1.0 + mods_ref[2, r : r + 1, :].astype(jnp.float32)
    shift = mods_ref[1, r : r + 1, :].astype(jnp.float32)
    hidden = ((mixed[...] - center) * inverse * scale + shift).astype(jnp.bfloat16)
    hidden_ref[...] = hidden
    velocity_ref[...] = lax.dot_general(
        final_ref[...], hidden, (((1,), (1,)), ((), ())), preferred_element_type=jnp.float32
    )


def hidden_rows(place, heads_part, image_state, modulation, final_weight, pieces, r):
    heads, rows, _ = heads_part.shape
    width_all = image_state.shape[3]
    width = pieces[0].shape[1]
    whole = pl.BlockSpec(memory_space=pltpu.VMEM)
    return pl.pallas_call(
        functools.partial(hidden_kernel, r),
        grid=(1,),
        in_specs=[
            pl.BlockSpec(memory_space=pltpu.SMEM),
            pl.BlockSpec((heads, rows, HD), lambda i: (0, 0, 0)),
            pl.BlockSpec((1, 1, rows, width_all), lambda i: (0, r, 0, 0)),
            whole,
            whole,
        ]
        + [pl.BlockSpec(memory_space=pl.ANY)] * 10,
        out_specs=[
            pl.BlockSpec((rows, width_all), lambda i: (0, 0)),
            pl.BlockSpec((C, rows), lambda i: (0, 0)),
        ],
        out_shape=[
            jax.ShapeDtypeStruct((rows, width_all), jnp.bfloat16),
            jax.ShapeDtypeStruct((C, rows), jnp.float32),
        ],
        scratch_shapes=[
            pltpu.VMEM((rows, heads * HD), jnp.bfloat16),
            pltpu.VMEM((rows, width_all), jnp.float32),
            pltpu.VMEM((8, heads * HD, width), jnp.bfloat16),
            pltpu.SemaphoreType.DMA((10,)),
        ],
        compiler_params=pltpu.CompilerParams(vmem_limit_bytes=VMEM_BYTES),
        cost_estimate=pl.CostEstimate(
            flops=2 * rows * heads * HD * width_all,
            bytes_accessed=2 * heads * HD * width_all,
            transcendentals=0,
        ),
        name=f"hidden{r}",
    )(place, heads_part, image_state, modulation, final_weight, *pieces)


def step_kernel(place, terms, own_ref, partner_ref, latent_ref, next_ref, hidden_ref, *rest):
    earlier, (keep_ref, send_ref, squares_ref) = rest[:-3], rest[-3:]
    r = 1 if earlier else 0
    first = place[3] == 0
    own, partner = own_ref[...], partner_ref[...]
    conditional = jnp.where(first, own, partner)
    unconditional = jnp.where(first, partner, own)
    guided = unconditional + cfg_scale * (conditional - unconditional)
    step_mean = latent_ref[0] * terms[0, r] - guided * terms[1, r]
    residue = next_ref[0] - step_mean
    total = jnp.sum(residue * residue)
    slopes = terms[2, r] * residue
    own_slopes = jnp.where(first, cfg_scale, 1.0 - cfg_scale) * slopes
    half = own_slopes.shape[0] // 2
    low, high = own_slopes[:half], own_slopes[half:]
    ordered = jnp.concatenate([jnp.where(first, low, high), jnp.where(first, high, low)], axis=0)
    partial = jnp.dot(
        ordered.astype(jnp.bfloat16), hidden_ref[...], preferred_element_type=jnp.float32
    )
    width = keep_ref.shape[2]
    for n in range(keep_ref.shape[0]):
        cols = slice(n * width, (n + 1) * width)
        if earlier:
            keep_ref[n] = earlier[0][n] + partial[:half, cols]
            send_ref[n] = earlier[1][n] + partial[half:, cols]
        else:
            keep_ref[n] = partial[:half, cols]
            send_ref[n] = partial[half:, cols]
    row = lax.broadcasted_iota(jnp.int32, squares_ref.shape, 0)
    before = earlier[2][...] if earlier else jnp.zeros(squares_ref.shape, jnp.float32)
    squares_ref[...] = jnp.where(row == r, total, before)


def step(place, terms, own, partner, latent, next_latent, hidden, earlier, data_count):
    rows, width_all = hidden.shape
    r = 1 if earlier else 0
    cut = (data_count, C // 2, width_all // data_count)
    smem = pl.BlockSpec(memory_space=pltpu.SMEM)
    vmem = pl.BlockSpec(memory_space=pltpu.VMEM)
    return pl.pallas_call(
        step_kernel,
        grid=(1,),
        in_specs=[smem, smem]
        + [pl.BlockSpec((C, rows), lambda i: (0, 0))] * 2
        + [pl.BlockSpec((1, C, rows), lambda i: (r, 0, 0))] * 2
        + [pl.BlockSpec((rows, width_all), lambda i: (0, 0))]
        + [vmem] * len(earlier),
        out_specs=[vmem] * 3,
        out_shape=[
            jax.ShapeDtypeStruct(cut, jnp.float32),
            jax.ShapeDtypeStruct(cut, jnp.float32),
            jax.ShapeDtypeStruct((8, 128), jnp.float32),
        ],
        compiler_params=pltpu.CompilerParams(vmem_limit_bytes=VMEM_BYTES),
        cost_estimate=pl.CostEstimate(
            flops=2 * rows * C * width_all, bytes_accessed=2 * rows * width_all, transcendentals=0
        ),
        name=f"step{r}",
    )(place, terms, own, partner, latent, next_latent, hidden, *earlier)


def fold_kernel(parts_ref, squares_ref, out_ref):
    count, width = parts_ref.shape[1], parts_ref.shape[2]
    out_ref[0:count, :] = jnp.sum(parts_ref[...], axis=0)
    out_ref[count : count + 8, 128:width] = jnp.zeros((8, width - 128), jnp.float32)
    out_ref[count : count + 8, 0:128] = squares_ref[...]


def fold(parts, squares):
    _, count, width = parts.shape
    vmem = pl.BlockSpec(memory_space=pltpu.VMEM)
    return pl.pallas_call(
        fold_kernel,
        in_specs=[vmem] * 2,
        out_specs=vmem,
        out_shape=jax.ShapeDtypeStruct((count + 8, width), jnp.float32),
        name="fold",
    )(parts, squares)


def finish_kernel(place, own_ref, other_ref, out_ref):
    first = place[3] == 0
    half = out_ref.shape[0] // 2
    own, other = own_ref[0:half, :], other_ref[0:half, :]
    out_ref[0:half, :] = jnp.where(first, own, other)
    out_ref[half : 2 * half, :] = jnp.where(first, other, own)


def finish(place, own, other):
    vmem = pl.BlockSpec(memory_space=pltpu.VMEM)
    return pl.pallas_call(
        finish_kernel,
        in_specs=[pl.BlockSpec(memory_space=pltpu.SMEM), vmem, vmem],
        out_specs=vmem,
        out_shape=jax.ShapeDtypeStruct((C, own.shape[1]), jnp.float32),
        name="finish",
    )(place, own, other)


def exchange(send):
    return lax.all_to_all(send, "seq", split_axis=0, concat_axis=0, tiled=True)


def per_device(
    image_projections,
    text_projections,
    output_weight,
    image_state,
    modulation,
    final_weight,
    latent,
    next_latent,
    timestep,
    rewards,
    group_index,
):
    seq_count = lax.axis_size("seq")
    data_count = lax.axis_size("dp")
    per_dev = image_projections.shape[1]
    image_count = image_projections.shape[2]
    width_all = image_state.shape[3]
    rollouts = per_dev * data_count
    seq_at, dp_at, c_at = lax.axis_index("seq"), lax.axis_index("dp"), lax.axis_index("cfg")
    x_at, zh_at, y_at, zl_at = seq_at // ZH, seq_at % ZH, dp_at // ZL, dp_at % ZL
    place = jnp.stack([x_at, zh_at, y_at, c_at]).astype(jnp.int32)

    kv_rows = image_count + text_projections.shape[2]

    mine = jnp.where(zl_at == c_at, output_weight, from_zl(output_weight))
    column = jnp.concatenate([mine] + [from_zh(mine, d) for d in range(1, ZH)], axis=0)
    first_part = exchange(after(pack(image_projections, text_projections), column))
    plane = jnp.concatenate([column] + [from_x(column, d) for d in range(1, X)], axis=0)
    cut = plane.shape[0] // 2
    ahead = from_y(plane, 1)
    behind = from_y(plane, -1)
    plane_other = from_cfg(plane)

    group_count = rollouts // GROUP_SIZE
    member = (group_index[:, None] == jnp.arange(group_count, dtype=jnp.int32)[None, :]).astype(
        jnp.float32
    )
    totals = jnp.sum(member * rewards[:, None], axis=0)
    totals = totals + from_zl(totals)
    totals = ring_sum(totals, from_y)
    advantage = rewards - jnp.sum(member * totals[None, :], axis=1) / GROUP_SIZE

    spread = noise_level * jnp.sqrt(timestep / (1.0 - timestep))
    drift_gain = 1.0 + spread * spread * (1.0 - timestep) / (2.0 * timestep)
    deviation = spread * math.sqrt(step_width)
    terms = jnp.stack(
        [
            1.0 - spread * spread / (2.0 * timestep) * step_width,
            drift_gain * step_width,
            advantage / (rollouts * C) * drift_gain * step_width / (deviation * deviation),
        ]
    )

    second_part = exchange(
        after(pack_queries(image_projections, 1), ahead, behind, plane_other, totals)
    )
    far_first = from_y(ahead[:cut], 1)
    far_second = from_y(behind[cut:], -1)
    ahead_other, behind_other = from_cfg(ahead), from_cfg(behind)
    pieces = [plane, ahead, behind, far_first, far_second]
    pieces += [plane_other, ahead_other, behind_other, from_cfg(far_first), from_cfg(far_second)]

    queries_at = per_dev * 2 * kv_rows // image_count
    attended = [
        attention(first_part, queries_at, first_part, 0, image_count, kv_rows),
        attention(second_part, 0, first_part, 1, image_count, kv_rows),
    ]
    attended[0] = after(attended[0], far_first, far_second, ahead_other, behind_other)
    returned = [exchange(value) for value in attended]
    returned[0] = after(returned[0], attended[1], terms)
    mods_local = modulation[0].transpose(1, 0, 2)
    final_across = final_weight.T
    latent_across, next_across = latent.transpose(0, 2, 1), next_latent.transpose(0, 2, 1)
    sums = ()
    for r in range(per_dev):
        if sums:
            returned[r] = after(returned[r], *sums)
        hidden, velocity = hidden_rows(
            place, returned[r], image_state, mods_local, final_across, pieces, r
        )
        sums = step(
            place,
            terms,
            velocity,
            from_cfg(velocity),
            latent_across,
            next_across,
            hidden,
            tuple(sums),
            data_count,
        )
    keep, send, squares = sums

    kept = keep + from_cfg(send)
    share = fold(lax.all_to_all(kept, "dp", split_axis=0, concat_axis=0, tiled=True), squares)
    share = ring_sum(ring_sum(share, from_zh), from_x)
    gradient = finish(place, share, from_cfg(share)).T
    square_mean = share[C // 2 : C // 2 + per_dev, 0] / (seq_count * image_count * C)
    log_prob = (
        -square_mean / (2.0 * deviation * deviation)
        - jnp.log(deviation)
        - 0.5 * math.log(2.0 * math.pi)
    )
    return (gradient, log_prob)


def solution(mesh):
    in_specs = (
        P("cfg", "dp", "seq", None),
        P("cfg", "dp", "seq", None),
        P("seq", "dp"),
        P("cfg", "dp", "seq", None),
        P("cfg", "dp", None, None),
        P(),
        P("dp", "seq", None),
        P("dp", "seq", None),
        P("dp"),
        P("dp"),
        P("dp"),
    )
    out_specs = (P("dp", None), P("dp"))
    return jax.shard_map(
        per_device, mesh=mesh, in_specs=in_specs, out_specs=out_specs, check_vma=False
    )
```

```python
import functools
import math

import jax
import jax.numpy as jnp
from jax import lax
from jax.experimental import pallas as pl
from jax.experimental.pallas import tpu as pltpu
from jax.sharding import PartitionSpec as P

C = 64
HD = 128
GROUP_SIZE = 2

cfg_scale = 4.5
noise_level = 0.7
step_width = 0.02
norm_eps = 1e-06

X, ZH, Y, ZL = 4, 4, 4, 2
VMEM_BYTES = 56 * 1024 * 1024


def from_x(value, d):
    pairs = [(((x + d) % X) * ZH + z, x * ZH + z) for x in range(X) for z in range(ZH)]
    return lax.ppermute(value, "seq", pairs)


def from_column(value, d):
    def at(core, x, z, y, zl):
        return ((core * X + x) * ZH + z) * (Y * ZL) + y * ZL + zl

    pairs = [
        (at(core if zl == core else 1 - core, x, (z + d) % ZH, y, core), at(core, x, z, y, zl))
        for core in range(2)
        for x in range(X)
        for z in range(ZH)
        for y in range(Y)
        for zl in range(ZL)
    ]
    return lax.ppermute(value, ("cfg", "seq", "dp"), pairs)


def from_zh(value, d):
    pairs = [(x * ZH + (z + d) % ZH, x * ZH + z) for x in range(X) for z in range(ZH)]
    return lax.ppermute(value, "seq", pairs)


def from_y(value, d):
    pairs = [(((y + d) % Y) * ZL + z, y * ZL + z) for y in range(Y) for z in range(ZL)]
    return lax.ppermute(value, "dp", pairs)


def from_zl(value):
    pairs = [(y * ZL + 1 - z, y * ZL + z) for y in range(Y) for z in range(ZL)]
    return lax.ppermute(value, "dp", pairs)


def from_cfg(value):
    return lax.ppermute(value, "cfg", [(0, 1), (1, 0)])


def after(value, *others):
    return lax.optimization_barrier((value,) + others)[0]


def ring_sum(value, fetch):
    first, second, third = (fetch(value, d) for d in (1, 2, 3))
    return (value + second) + (first + third)


def pack_kernel(k_ref, v_ref, kt_ref, vt_ref, q_ref, out_ref):
    rows, text = k_ref.shape[2], kt_ref.shape[2]
    for h in range(out_ref.shape[0]):
        cols = slice(h * HD, (h + 1) * HD)
        at = 0
        for r in range(k_ref.shape[1]):
            for ref, count in ((k_ref, rows), (kt_ref, text), (v_ref, rows), (vt_ref, text)):
                out_ref[h, at : at + count, :] = ref[0, r, :, cols]
                at += count
        out_ref[h, at : at + rows, :] = q_ref[0, 0, :, cols]


def pack_queries_kernel(q_ref, out_ref):
    for h in range(out_ref.shape[0]):
        out_ref[h] = q_ref[0, 0, :, h * HD : (h + 1) * HD]


def pack(image_projections, text_projections):
    _, per_dev, rows, width = image_projections.shape
    text = text_projections.shape[2]
    heads = width // (3 * HD)
    per = 4
    steps = heads // per
    total = per_dev * 2 * (rows + text) + rows

    def spec(rollouts, count, part):
        return pl.BlockSpec((1, rollouts, count, per * HD), lambda h: (0, 0, 0, part * steps + h))

    return pl.pallas_call(
        pack_kernel,
        grid=(steps,),
        in_specs=[
            spec(per_dev, rows, 1),
            spec(per_dev, rows, 2),
            spec(per_dev, text, 0),
            spec(per_dev, text, 1),
            spec(1, rows, 0),
        ],
        out_specs=pl.BlockSpec((per, total, HD), lambda h: (h, 0, 0)),
        out_shape=jax.ShapeDtypeStruct((heads, total, HD), jnp.bfloat16),
        compiler_params=pltpu.CompilerParams(vmem_limit_bytes=32 * 1024 * 1024),
        cost_estimate=pl.CostEstimate(
            flops=0, bytes_accessed=2 * heads * total * HD * 2, transcendentals=0
        ),
        name="pack",
    )(image_projections, image_projections, text_projections, text_projections, image_projections)


def pack_queries(image_projections, r):
    _, _, rows, width = image_projections.shape
    heads = width // (3 * HD)
    return pl.pallas_call(
        pack_queries_kernel,
        grid=(1,),
        in_specs=[pl.BlockSpec((1, 1, rows, heads * HD), lambda i: (0, r, 0, 0))],
        out_specs=pl.BlockSpec((heads, rows, HD), lambda i: (0, 0, 0)),
        out_shape=jax.ShapeDtypeStruct((heads, rows, HD), jnp.bfloat16),
        compiler_params=pltpu.CompilerParams(vmem_limit_bytes=32 * 1024 * 1024),
        cost_estimate=pl.CostEstimate(
            flops=0, bytes_accessed=2 * heads * rows * HD * 2, transcendentals=0
        ),
        name="pack_queries",
    )(image_projections)


def attention_kernel(q_ref, kv_ref, out_ref, keys, values):
    peers, kv_rows = kv_ref.shape[0], kv_ref.shape[1] // 2
    ones = jnp.ones((kv_rows, HD), jnp.bfloat16)
    for s in range(peers):
        at = slice(s * kv_rows, (s + 1) * kv_rows)
        keys[at, :] = kv_ref[s, 0:kv_rows, :]
        values[at, 0:HD] = kv_ref[s, kv_rows : 2 * kv_rows, :]
        values[at, HD : 2 * HD] = ones

    factor = math.log2(math.e) / math.sqrt(HD)
    for n in range(peers):
        scores = lax.dot_general(
            q_ref[n], keys[...], (((1,), (1,)), ((), ())), preferred_element_type=jnp.float32
        )
        highest = jnp.max(scores, axis=1, keepdims=True)
        powered = jnp.exp2((scores - highest) * factor).astype(jnp.bfloat16)
        sums = jnp.dot(powered, values[...], preferred_element_type=jnp.float32)
        out_ref[n] = (sums[:, 0:HD] / sums[:, HD : HD + 1]).astype(jnp.bfloat16)


def attention(queries, q_at, key_values, kv_at, rows, kv_rows):
    peers = queries.shape[0]
    return pl.pallas_call(
        attention_kernel,
        grid=(1,),
        in_specs=[
            pl.BlockSpec((peers, rows, HD), lambda i: (0, q_at, 0)),
            pl.BlockSpec((peers, 2 * kv_rows, HD), lambda i: (0, kv_at, 0)),
        ],
        out_specs=pl.BlockSpec((peers, rows, HD), lambda i: (0, 0, 0)),
        out_shape=jax.ShapeDtypeStruct((peers, rows, HD), jnp.bfloat16),
        scratch_shapes=[
            pltpu.VMEM((peers * kv_rows, HD), jnp.bfloat16),
            pltpu.VMEM((peers * kv_rows, 2 * HD), jnp.bfloat16),
        ],
        compiler_params=pltpu.CompilerParams(vmem_limit_bytes=VMEM_BYTES),
        cost_estimate=pl.CostEstimate(
            flops=8 * peers * rows * peers * kv_rows * HD,
            bytes_accessed=2 * peers * (2 * rows + 2 * kv_rows) * HD,
            transcendentals=peers * rows * peers * kv_rows,
        ),
        name="attention",
    )(queries, key_values)


def hidden_kernel(r, place, heads_ref, state_ref, mods_ref, final_ref, *rest):
    pieces, (hidden_ref, velocity_ref, flat, mixed, weights, sems) = rest[:10], rest[10:]
    x_at, zh_at, y_at, c_at = place[0], place[1], place[2], place[3]
    heads = heads_ref.shape[0]
    depth = heads * HD
    width = weights.shape[2]
    half = heads // 2
    spans = ((0, 0, heads), (1, 0, heads), (3, 0, heads), (2, 0, half), (2, half, half))
    copies = []
    for core in range(2):
        for n, (turn, first, count) in enumerate(spans):
            copy = pltpu.make_async_copy(
                pieces[core * 5 + n],
                weights.at[core * 4 + turn, pl.ds(first * HD, count * HD)],
                sems.at[core * 5 + n],
            )
            copy.start()
            copies.append(copy)
    for i in range(X):
        for j in range(ZH):
            head = lax.rem(x_at + i, X) * ZH + lax.rem(zh_at + j, ZH)
            k = i * ZH + j
            flat[:, k * HD : (k + 1) * HD] = heads_ref[head]
    rows = flat.shape[0]
    row_sum = jnp.zeros((rows, 1), jnp.float32)
    square_sum = jnp.zeros((rows, 1), jnp.float32)
    for core in range(2):
        core_at = c_at if core == 0 else 1 - c_at
        for turn, needed in ((0, (0,)), (1, (1,)), (3, (2,)), (2, (3, 4))):
            for n in needed:
                copies[core * 5 + n].wait()
            at = pl.ds(pl.multiple_of((lax.rem(y_at + turn, Y) * ZL + core_at) * width, 128), width)
            projected = jnp.dot(
                flat[...], weights[core * 4 + turn], preferred_element_type=jnp.float32
            )
            gate = mods_ref[0, r : r + 1, at].astype(jnp.float32)
            block = state_ref[0, 0, :, at].astype(jnp.float32) + gate * projected
            mixed[:, at] = block
            row_sum = row_sum + jnp.sum(block, axis=1, keepdims=True)
            square_sum = square_sum + jnp.sum(block * block, axis=1, keepdims=True)
    width_all = mixed.shape[1]
    center = row_sum / width_all
    square = square_sum / width_all
    inverse = lax.rsqrt(square - center * center + norm_eps)
    scale = 1.0 + mods_ref[2, r : r + 1, :].astype(jnp.float32)
    shift = mods_ref[1, r : r + 1, :].astype(jnp.float32)
    hidden = ((mixed[...] - center) * inverse * scale + shift).astype(jnp.bfloat16)
    hidden_ref[...] = hidden
    velocity_ref[...] = lax.dot_general(
        final_ref[...], hidden, (((1,), (1,)), ((), ())), preferred_element_type=jnp.float32
    )


def hidden_rows(place, heads_part, image_state, modulation, final_weight, pieces, r):
    heads, rows, _ = heads_part.shape
    width_all = image_state.shape[3]
    width = pieces[0].shape[1]
    whole = pl.BlockSpec(memory_space=pltpu.VMEM)
    return pl.pallas_call(
        functools.partial(hidden_kernel, r),
        grid=(1,),
        in_specs=[
            pl.BlockSpec(memory_space=pltpu.SMEM),
            pl.BlockSpec((heads, rows, HD), lambda i: (0, 0, 0)),
            pl.BlockSpec((1, 1, rows, width_all), lambda i: (0, r, 0, 0)),
            whole,
            whole,
        ]
        + [pl.BlockSpec(memory_space=pl.ANY)] * 10,
        out_specs=[
            pl.BlockSpec((rows, width_all), lambda i: (0, 0)),
            pl.BlockSpec((C, rows), lambda i: (0, 0)),
        ],
        out_shape=[
            jax.ShapeDtypeStruct((rows, width_all), jnp.bfloat16),
            jax.ShapeDtypeStruct((C, rows), jnp.float32),
        ],
        scratch_shapes=[
            pltpu.VMEM((rows, heads * HD), jnp.bfloat16),
            pltpu.VMEM((rows, width_all), jnp.float32),
            pltpu.VMEM((8, heads * HD, width), jnp.bfloat16),
            pltpu.SemaphoreType.DMA((10,)),
        ],
        compiler_params=pltpu.CompilerParams(vmem_limit_bytes=VMEM_BYTES),
        cost_estimate=pl.CostEstimate(
            flops=2 * rows * heads * HD * width_all,
            bytes_accessed=2 * heads * HD * width_all,
            transcendentals=0,
        ),
        name=f"hidden{r}",
    )(place, heads_part, image_state, modulation, final_weight, *pieces)


def step_kernel(place, terms, own_ref, partner_ref, latent_ref, next_ref, hidden_ref, *rest):
    earlier, (keep_ref, send_ref, squares_ref) = rest[:-3], rest[-3:]
    r = 1 if earlier else 0
    first = place[3] == 0
    own, partner = own_ref[...], partner_ref[...]
    conditional = jnp.where(first, own, partner)
    unconditional = jnp.where(first, partner, own)
    guided = unconditional + cfg_scale * (conditional - unconditional)
    step_mean = latent_ref[0] * terms[0, r] - guided * terms[1, r]
    residue = next_ref[0] - step_mean
    total = jnp.sum(residue * residue)
    slopes = terms[2, r] * residue
    own_slopes = jnp.where(first, cfg_scale, 1.0 - cfg_scale) * slopes
    half = own_slopes.shape[0] // 2
    low, high = own_slopes[:half], own_slopes[half:]
    ordered = jnp.concatenate([jnp.where(first, low, high), jnp.where(first, high, low)], axis=0)
    partial = jnp.dot(
        ordered.astype(jnp.bfloat16), hidden_ref[...], preferred_element_type=jnp.float32
    )
    width = keep_ref.shape[2]
    for n in range(keep_ref.shape[0]):
        cols = slice(n * width, (n + 1) * width)
        if earlier:
            keep_ref[n] = earlier[0][n] + partial[:half, cols]
            send_ref[n] = earlier[1][n] + partial[half:, cols]
        else:
            keep_ref[n] = partial[:half, cols]
            send_ref[n] = partial[half:, cols]
    row = lax.broadcasted_iota(jnp.int32, squares_ref.shape, 0)
    before = earlier[2][...] if earlier else jnp.zeros(squares_ref.shape, jnp.float32)
    squares_ref[...] = jnp.where(row == r, total, before)


def step(place, terms, own, partner, latent, next_latent, hidden, earlier, data_count):
    rows, width_all = hidden.shape
    r = 1 if earlier else 0
    cut = (data_count, C // 2, width_all // data_count)
    smem = pl.BlockSpec(memory_space=pltpu.SMEM)
    vmem = pl.BlockSpec(memory_space=pltpu.VMEM)
    return pl.pallas_call(
        step_kernel,
        grid=(1,),
        in_specs=[smem, smem]
        + [pl.BlockSpec((C, rows), lambda i: (0, 0))] * 2
        + [pl.BlockSpec((1, C, rows), lambda i: (r, 0, 0))] * 2
        + [pl.BlockSpec((rows, width_all), lambda i: (0, 0))]
        + [vmem] * len(earlier),
        out_specs=[vmem] * 3,
        out_shape=[
            jax.ShapeDtypeStruct(cut, jnp.float32),
            jax.ShapeDtypeStruct(cut, jnp.float32),
            jax.ShapeDtypeStruct((8, 128), jnp.float32),
        ],
        compiler_params=pltpu.CompilerParams(vmem_limit_bytes=VMEM_BYTES),
        cost_estimate=pl.CostEstimate(
            flops=2 * rows * C * width_all, bytes_accessed=2 * rows * width_all, transcendentals=0
        ),
        name=f"step{r}",
    )(place, terms, own, partner, latent, next_latent, hidden, *earlier)


def fold_kernel(parts_ref, squares_ref, out_ref):
    count, width = parts_ref.shape[1], parts_ref.shape[2]
    out_ref[0:count, :] = jnp.sum(parts_ref[...], axis=0)
    out_ref[count : count + 8, 128:width] = jnp.zeros((8, width - 128), jnp.float32)
    out_ref[count : count + 8, 0:128] = squares_ref[...]


def fold(parts, squares):
    _, count, width = parts.shape
    vmem = pl.BlockSpec(memory_space=pltpu.VMEM)
    return pl.pallas_call(
        fold_kernel,
        in_specs=[vmem] * 2,
        out_specs=vmem,
        out_shape=jax.ShapeDtypeStruct((count + 8, width), jnp.float32),
        name="fold",
    )(parts, squares)


def finish_kernel(place, own_ref, other_ref, out_ref):
    first = place[3] == 0
    half = out_ref.shape[0] // 2
    own, other = own_ref[0:half, :], other_ref[0:half, :]
    out_ref[0:half, :] = jnp.where(first, own, other)
    out_ref[half : 2 * half, :] = jnp.where(first, other, own)


def finish(place, own, other):
    vmem = pl.BlockSpec(memory_space=pltpu.VMEM)
    return pl.pallas_call(
        finish_kernel,
        in_specs=[pl.BlockSpec(memory_space=pltpu.SMEM), vmem, vmem],
        out_specs=vmem,
        out_shape=jax.ShapeDtypeStruct((C, own.shape[1]), jnp.float32),
        name="finish",
    )(place, own, other)


def exchange(send):
    return lax.all_to_all(send, "seq", split_axis=0, concat_axis=0, tiled=True)


def per_device(
    image_projections,
    text_projections,
    output_weight,
    image_state,
    modulation,
    final_weight,
    latent,
    next_latent,
    timestep,
    rewards,
    group_index,
):
    seq_count = lax.axis_size("seq")
    data_count = lax.axis_size("dp")
    per_dev = image_projections.shape[1]
    image_count = image_projections.shape[2]
    width_all = image_state.shape[3]
    rollouts = per_dev * data_count
    seq_at, dp_at, c_at = lax.axis_index("seq"), lax.axis_index("dp"), lax.axis_index("cfg")
    x_at, zh_at, y_at = seq_at // ZH, seq_at % ZH, dp_at // ZL
    place = jnp.stack([x_at, zh_at, y_at, c_at]).astype(jnp.int32)

    kv_rows = image_count + text_projections.shape[2]

    group_count = rollouts // GROUP_SIZE
    member = (group_index[:, None] == jnp.arange(group_count, dtype=jnp.int32)[None, :]).astype(
        jnp.float32
    )
    column = jnp.concatenate([from_column(output_weight, d) for d in range(ZH)], axis=0)
    totals = jnp.sum(member * rewards[:, None], axis=0)
    totals = totals + from_zl(totals)
    first_part = exchange(after(pack(image_projections, text_projections), column, totals))
    totals = ring_sum(totals, from_y)
    advantage = rewards - jnp.sum(member * totals[None, :], axis=1) / GROUP_SIZE
    column = after(column, totals)
    plane = jnp.concatenate([column] + [from_x(column, d) for d in range(1, X)], axis=0)
    cut = plane.shape[0] // 2
    ahead, behind = from_y(plane, 1), from_y(plane, -1)
    plane_other = from_cfg(plane)
    second_part = exchange(after(pack_queries(image_projections, 1), plane_other))
    far_first = from_y(ahead[:cut], 1)
    far_second = from_y(behind[cut:], -1)
    own = [plane, ahead, behind, far_first, far_second]
    pieces = own + [plane_other] + [from_cfg(piece) for piece in own[1:]]

    spread = noise_level * jnp.sqrt(timestep / (1.0 - timestep))
    drift_gain = 1.0 + spread * spread * (1.0 - timestep) / (2.0 * timestep)
    deviation = spread * math.sqrt(step_width)
    terms = jnp.stack(
        [
            1.0 - spread * spread / (2.0 * timestep) * step_width,
            drift_gain * step_width,
            advantage / (rollouts * C) * drift_gain * step_width / (deviation * deviation),
        ]
    )

    queries_at = per_dev * 2 * kv_rows // image_count
    attended = [
        attention(first_part, queries_at, first_part, 0, image_count, kv_rows),
        attention(second_part, 0, first_part, 1, image_count, kv_rows),
    ]
    attended[0] = after(attended[0], ahead, behind)
    returned = [exchange(value) for value in attended]
    returned[0] = after(returned[0], attended[1], terms)
    mods_local = modulation[0].transpose(1, 0, 2)
    final_across = final_weight.T
    latent_across, next_across = latent.transpose(0, 2, 1), next_latent.transpose(0, 2, 1)
    sums = ()
    for r in range(per_dev):
        if sums:
            returned[r] = after(returned[r], *sums)
        hidden, velocity = hidden_rows(
            place, returned[r], image_state, mods_local, final_across, pieces, r
        )
        sums = step(
            place,
            terms,
            velocity,
            from_cfg(velocity),
            latent_across,
            next_across,
            hidden,
            tuple(sums),
            data_count,
        )
    keep, send, squares = sums

    kept = keep + from_cfg(send)
    share = fold(lax.all_to_all(kept, "dp", split_axis=0, concat_axis=0, tiled=True), squares)
    share = ring_sum(ring_sum(share, from_zh), from_x)
    gradient = finish(place, share, from_cfg(share)).T
    square_mean = share[C // 2 : C // 2 + per_dev, 0] / (seq_count * image_count * C)
    log_prob = (
        -square_mean / (2.0 * deviation * deviation)
        - jnp.log(deviation)
        - 0.5 * math.log(2.0 * math.pi)
    )
    return (gradient, log_prob)


def solution(mesh):
    in_specs = (
        P("cfg", "dp", "seq", None),
        P("cfg", "dp", "seq", None),
        P("seq", "dp"),
        P("cfg", "dp", "seq", None),
        P("cfg", "dp", None, None),
        P(),
        P("dp", "seq", None),
        P("dp", "seq", None),
        P("dp"),
        P("dp"),
        P("dp"),
    )
    out_specs = (P("dp", None), P("dp"))
    return jax.shard_map(
        per_device, mesh=mesh, in_specs=in_specs, out_specs=out_specs, check_vma=False
    )
```

```python
import functools
import math

import jax
import jax.numpy as jnp
from jax import lax
from jax.experimental import pallas as pl
from jax.experimental.pallas import tpu as pltpu
from jax.sharding import PartitionSpec as P

C = 64
HD = 128
GROUP_SIZE = 2

cfg_scale = 4.5
noise_level = 0.7
step_width = 0.02
norm_eps = 1e-06

X, ZH, Y, ZL = 4, 4, 4, 2
VMEM_BYTES = 32 * 1024 * 1024
HIDDEN_VMEM_BYTES = 40 * 1024 * 1024
FULL_VMEM_BYTES = 61 * 1024 * 1024


def from_x(value, d):
    pairs = [(((x + d) % X) * ZH + z, x * ZH + z) for x in range(X) for z in range(ZH)]
    return lax.ppermute(value, "seq", pairs)


def from_column(value, d):
    def at(core, x, z, y, zl):
        return ((core * X + x) * ZH + z) * (Y * ZL) + y * ZL + zl

    pairs = [
        (at(core if zl == core else 1 - core, x, (z + d) % ZH, y, core), at(core, x, z, y, zl))
        for core in range(2)
        for x in range(X)
        for z in range(ZH)
        for y in range(Y)
        for zl in range(ZL)
    ]
    return lax.ppermute(value, ("cfg", "seq", "dp"), pairs)


def from_zh(value, d):
    pairs = [(x * ZH + (z + d) % ZH, x * ZH + z) for x in range(X) for z in range(ZH)]
    return lax.ppermute(value, "seq", pairs)


def from_y(value, d):
    pairs = [(((y + d) % Y) * ZL + z, y * ZL + z) for y in range(Y) for z in range(ZL)]
    return lax.ppermute(value, "dp", pairs)


def from_zl(value):
    pairs = [(y * ZL + 1 - z, y * ZL + z) for y in range(Y) for z in range(ZL)]
    return lax.ppermute(value, "dp", pairs)


def from_cfg(value):
    return lax.ppermute(value, "cfg", [(0, 1), (1, 0)])


def after(value, *others):
    return lax.optimization_barrier((value,) + others)[0]


def ring_sum(value, fetch):
    first, second, third = (fetch(value, d) for d in (1, 2, 3))
    return (value + second) + (first + third)


def pack_kernel(k_ref, v_ref, kt_ref, vt_ref, q_ref, out_ref):
    rows, text = k_ref.shape[2], kt_ref.shape[2]
    for h in range(out_ref.shape[0]):
        cols = slice(h * HD, (h + 1) * HD)
        at = 0
        for r in range(k_ref.shape[1]):
            for ref, count in ((k_ref, rows), (kt_ref, text), (v_ref, rows), (vt_ref, text)):
                out_ref[h, at : at + count, :] = ref[0, r, :, cols]
                at += count
        out_ref[h, at : at + rows, :] = q_ref[0, 0, :, cols]


def pack_queries_kernel(q_ref, out_ref):
    for h in range(out_ref.shape[0]):
        out_ref[h] = q_ref[0, 0, :, h * HD : (h + 1) * HD]


def pack(image_projections, text_projections):
    _, per_dev, rows, width = image_projections.shape
    text = text_projections.shape[2]
    heads = width // (3 * HD)
    per = 4
    steps = heads // per
    total = per_dev * 2 * (rows + text) + rows

    def spec(rollouts, count, part):
        return pl.BlockSpec((1, rollouts, count, per * HD), lambda h: (0, 0, 0, part * steps + h))

    return pl.pallas_call(
        pack_kernel,
        grid=(steps,),
        in_specs=[
            spec(per_dev, rows, 1),
            spec(per_dev, rows, 2),
            spec(per_dev, text, 0),
            spec(per_dev, text, 1),
            spec(1, rows, 0),
        ],
        out_specs=pl.BlockSpec((per, total, HD), lambda h: (h, 0, 0)),
        out_shape=jax.ShapeDtypeStruct((heads, total, HD), jnp.bfloat16),
        compiler_params=pltpu.CompilerParams(vmem_limit_bytes=FULL_VMEM_BYTES),
        cost_estimate=pl.CostEstimate(
            flops=0, bytes_accessed=2 * heads * total * HD * 2, transcendentals=0
        ),
        name="pack",
    )(image_projections, image_projections, text_projections, text_projections, image_projections)


def pack_queries(image_projections, r):
    _, _, rows, width = image_projections.shape
    heads = width // (3 * HD)
    return pl.pallas_call(
        pack_queries_kernel,
        grid=(1,),
        in_specs=[pl.BlockSpec((1, 1, rows, heads * HD), lambda i: (0, r, 0, 0))],
        out_specs=pl.BlockSpec((heads, rows, HD), lambda i: (0, 0, 0)),
        out_shape=jax.ShapeDtypeStruct((heads, rows, HD), jnp.bfloat16),
        compiler_params=pltpu.CompilerParams(vmem_limit_bytes=VMEM_BYTES),
        cost_estimate=pl.CostEstimate(
            flops=0, bytes_accessed=2 * heads * rows * HD * 2, transcendentals=0
        ),
        name="pack_queries",
    )(image_projections)


def attention_kernel(q_ref, kv_ref, *rest):
    out_ref, keys, values = rest[-3:]
    peers, kv_rows = kv_ref.shape[0], kv_ref.shape[1] // 2
    ones = jnp.ones((kv_rows, HD), jnp.bfloat16)
    for s in range(peers):
        at = slice(s * kv_rows, (s + 1) * kv_rows)
        keys[at, :] = kv_ref[s, 0:kv_rows, :]
        values[at, 0:HD] = kv_ref[s, kv_rows : 2 * kv_rows, :]
        values[at, HD : 2 * HD] = ones

    factor = math.log2(math.e) / math.sqrt(HD)
    for n in range(peers):
        scores = lax.dot_general(
            q_ref[n], keys[...], (((1,), (1,)), ((), ())), preferred_element_type=jnp.float32
        )
        highest = jnp.max(scores, axis=1, keepdims=True)
        powered = jnp.exp2((scores - highest) * factor).astype(jnp.bfloat16)
        sums = jnp.dot(powered, values[...], preferred_element_type=jnp.float32)
        out_ref[n] = (sums[:, 0:HD] / sums[:, HD : HD + 1]).astype(jnp.bfloat16)


def attention(queries, q_at, key_values, r, rows, kv_rows, per_dev, earlier=()):
    peers = queries.shape[0]
    return pl.pallas_call(
        attention_kernel,
        grid=(1,),
        in_specs=[
            pl.BlockSpec((peers, rows, HD), lambda i: (0, q_at, 0)),
            pl.BlockSpec((peers, 2 * kv_rows, HD), lambda i: (0, r, 0)),
        ]
        + [pl.BlockSpec(memory_space=pl.ANY)] * len(earlier),
        out_specs=pl.BlockSpec((peers, rows, HD), lambda i: (0, r, 0)),
        out_shape=jax.ShapeDtypeStruct((peers, per_dev * rows, HD), jnp.bfloat16),
        scratch_shapes=[
            pltpu.VMEM((peers * kv_rows, HD), jnp.bfloat16),
            pltpu.VMEM((peers * kv_rows, 2 * HD), jnp.bfloat16),
        ],
        input_output_aliases={2: 0} if earlier else {},
        compiler_params=pltpu.CompilerParams(vmem_limit_bytes=FULL_VMEM_BYTES),
        cost_estimate=pl.CostEstimate(
            flops=8 * peers * rows * peers * kv_rows * HD,
            bytes_accessed=2 * peers * (2 * rows + 2 * kv_rows) * HD,
            transcendentals=peers * rows * peers * kv_rows,
        ),
        name=f"attention{r}",
    )(queries, key_values, *earlier)


def hidden_kernel(place, heads_ref, state_ref, mods_ref, final_ref, *rest):
    pieces, (hidden_ref, velocity_ref, flat, mixed, weights, sems) = rest[:10], rest[10:]
    x_at, zh_at, y_at, c_at = place[0], place[1], place[2], place[3]
    per_dev, rows = state_ref.shape[1], state_ref.shape[2]
    width = weights.shape[2]
    depth = weights.shape[1]
    spans = ((0, 0), (1, 0), (3, 0), (2, 0), (2, depth // 2))
    copies = []
    for core in range(2):
        for n, (turn, at_row) in enumerate(spans):
            piece = pieces[core * 5 + n]
            copy = pltpu.make_async_copy(
                piece,
                weights.at[core * 4 + turn, pl.ds(at_row, piece.shape[0])],
                sems.at[core * 5 + n],
            )
            copy.start()
            copies.append(copy)
    for i in range(X):
        for j in range(ZH):
            head = lax.rem(x_at + i, X) * ZH + lax.rem(zh_at + j, ZH)
            k = i * ZH + j
            flat[:, k * HD : (k + 1) * HD] = heads_ref[head]
    row_sum = jnp.zeros((per_dev * rows, 1), jnp.float32)
    square_sum = jnp.zeros((per_dev * rows, 1), jnp.float32)
    for core in range(2):
        core_at = c_at if core == 0 else 1 - c_at
        for turn, needed in ((0, (0,)), (1, (1,)), (3, (2,)), (2, (3, 4))):
            for n in needed:
                copies[core * 5 + n].wait()
            at = pl.ds(pl.multiple_of((lax.rem(y_at + turn, Y) * ZL + core_at) * width, 128), width)
            projected = jnp.dot(
                flat[...], weights[core * 4 + turn], preferred_element_type=jnp.float32
            )
            for r in range(per_dev):
                gate = mods_ref[0, r : r + 1, at].astype(jnp.float32)
                mixed[r * rows : (r + 1) * rows, at] = (
                    state_ref[0, r, :, at].astype(jnp.float32)
                    + gate * projected[r * rows : (r + 1) * rows]
                )
            block = mixed[:, at]
            row_sum = row_sum + jnp.sum(block, axis=1, keepdims=True)
            square_sum = square_sum + jnp.sum(block * block, axis=1, keepdims=True)
    width_all = mixed.shape[1]
    center = row_sum / width_all
    square = square_sum / width_all
    inverse = lax.rsqrt(square - center * center + norm_eps)
    for r in range(per_dev):
        at = slice(r * rows, (r + 1) * rows)
        scale = 1.0 + mods_ref[2, r : r + 1, :].astype(jnp.float32)
        shift = mods_ref[1, r : r + 1, :].astype(jnp.float32)
        hidden_ref[at, :] = (
            (mixed[at, :] - center[at]) * inverse[at] * scale + shift
        ).astype(jnp.bfloat16)
    velocity_ref[...] = lax.dot_general(
        final_ref[...], hidden_ref[...], (((1,), (1,)), ((), ())), preferred_element_type=jnp.float32
    )


def hidden_rows(place, heads_part, image_state, modulation, final_weight, pieces):
    heads, all_rows, _ = heads_part.shape
    width_all = image_state.shape[3]
    vmem = pl.BlockSpec(memory_space=pltpu.VMEM)
    return pl.pallas_call(
        hidden_kernel,
        in_specs=[pl.BlockSpec(memory_space=pltpu.SMEM)]
        + [vmem] * 4
        + [pl.BlockSpec(memory_space=pl.ANY)] * 10,
        out_specs=[vmem] * 2,
        out_shape=[
            jax.ShapeDtypeStruct((all_rows, width_all), jnp.bfloat16),
            jax.ShapeDtypeStruct((C, all_rows), jnp.float32),
        ],
        scratch_shapes=[
            pltpu.VMEM((all_rows, heads * HD), jnp.bfloat16),
            pltpu.VMEM((all_rows, width_all), jnp.float32),
            pltpu.VMEM((8, heads * HD, pieces[0].shape[1]), jnp.bfloat16),
            pltpu.SemaphoreType.DMA((10,)),
        ],
        compiler_params=pltpu.CompilerParams(vmem_limit_bytes=HIDDEN_VMEM_BYTES),
        cost_estimate=pl.CostEstimate(
            flops=2 * all_rows * heads * HD * width_all,
            bytes_accessed=2 * heads * HD * width_all,
            transcendentals=0,
        ),
        name="hidden",
    )(place, heads_part, image_state, modulation, final_weight, *pieces)


def step_kernel(
    place, terms, own_ref, partner_ref, latent_ref, next_ref, hidden_ref, keep_ref, send_ref, squares_ref
):
    first = place[3] == 0
    own, partner = own_ref[...], partner_ref[...]
    conditional = jnp.where(first, own, partner)
    unconditional = jnp.where(first, partner, own)
    guided = unconditional + cfg_scale * (conditional - unconditional)
    per_dev, _, rows = latent_ref.shape
    row = lax.broadcasted_iota(jnp.int32, squares_ref.shape, 0)
    squares = jnp.zeros(squares_ref.shape, jnp.float32)
    slopes = []
    for r in range(per_dev):
        step_mean = (
            latent_ref[r] * terms[0, r] - guided[:, r * rows : (r + 1) * rows] * terms[1, r]
        )
        residue = next_ref[r] - step_mean
        squares = jnp.where(row == r, jnp.sum(residue * residue), squares)
        slopes.append(terms[2, r] * residue)
    squares_ref[...] = squares
    own_slopes = jnp.where(first, cfg_scale, 1.0 - cfg_scale) * jnp.concatenate(slopes, axis=1)
    half = own_slopes.shape[0] // 2
    low, high = own_slopes[:half], own_slopes[half:]
    ordered = jnp.concatenate([jnp.where(first, low, high), jnp.where(first, high, low)], axis=0)
    partial = jnp.dot(
        ordered.astype(jnp.bfloat16), hidden_ref[...], preferred_element_type=jnp.float32
    )
    width = keep_ref.shape[2]
    for n in range(keep_ref.shape[0]):
        cols = slice(n * width, (n + 1) * width)
        keep_ref[n] = partial[:half, cols]
        send_ref[n] = partial[half:, cols]


def step(place, terms, own, partner, latent, next_latent, hidden, data_count):
    rows, width_all = hidden.shape
    cut = (data_count, C // 2, width_all // data_count)
    smem = pl.BlockSpec(memory_space=pltpu.SMEM)
    vmem = pl.BlockSpec(memory_space=pltpu.VMEM)
    return pl.pallas_call(
        step_kernel,
        in_specs=[smem] * 2 + [vmem] * 5,
        out_specs=[vmem] * 3,
        out_shape=[
            jax.ShapeDtypeStruct(cut, jnp.float32),
            jax.ShapeDtypeStruct(cut, jnp.float32),
            jax.ShapeDtypeStruct((8, 128), jnp.float32),
        ],
        compiler_params=pltpu.CompilerParams(vmem_limit_bytes=VMEM_BYTES),
        cost_estimate=pl.CostEstimate(
            flops=2 * rows * C * width_all, bytes_accessed=2 * rows * width_all, transcendentals=0
        ),
        name="step",
    )(place, terms, own, partner, latent, next_latent, hidden)


def fold_kernel(parts_ref, squares_ref, out_ref):
    count, width = parts_ref.shape[1], parts_ref.shape[2]
    out_ref[0:count, :] = jnp.sum(parts_ref[...], axis=0)
    out_ref[count : count + 8, 128:width] = jnp.zeros((8, width - 128), jnp.float32)
    out_ref[count : count + 8, 0:128] = squares_ref[...]


def fold(parts, squares):
    _, count, width = parts.shape
    vmem = pl.BlockSpec(memory_space=pltpu.VMEM)
    return pl.pallas_call(
        fold_kernel,
        in_specs=[vmem] * 2,
        out_specs=vmem,
        out_shape=jax.ShapeDtypeStruct((count + 8, width), jnp.float32),
        name="fold",
    )(parts, squares)


def exchange(send):
    return lax.all_to_all(send, "seq", split_axis=0, concat_axis=0, tiled=True)


def per_device(
    image_projections,
    text_projections,
    output_weight,
    image_state,
    modulation,
    final_weight,
    latent,
    next_latent,
    timestep,
    rewards,
    group_index,
):
    seq_count = lax.axis_size("seq")
    data_count = lax.axis_size("dp")
    per_dev = image_projections.shape[1]
    image_count = image_projections.shape[2]
    width_all = image_state.shape[3]
    rollouts = per_dev * data_count
    seq_at, dp_at, c_at = lax.axis_index("seq"), lax.axis_index("dp"), lax.axis_index("cfg")
    x_at, zh_at, y_at = seq_at // ZH, seq_at % ZH, dp_at // ZL
    place = jnp.stack([x_at, zh_at, y_at, c_at]).astype(jnp.int32)

    kv_rows = image_count + text_projections.shape[2]

    group_count = rollouts // GROUP_SIZE
    member = (group_index[:, None] == jnp.arange(group_count, dtype=jnp.int32)[None, :]).astype(
        jnp.float32
    )
    column = jnp.concatenate([from_column(output_weight, d) for d in range(ZH)], axis=0)
    totals = jnp.sum(member * rewards[:, None], axis=0)
    first_part = exchange(after(pack(image_projections, text_projections), column))
    totals = ring_sum(totals, from_y)
    column = after(column, totals)
    totals = totals + from_zl(totals)
    advantage = rewards - jnp.sum(member * totals[None, :], axis=1) / GROUP_SIZE
    plane = jnp.concatenate([column] + [from_x(column, d) for d in range(1, X)], axis=0)
    cut = plane.shape[0] // 2
    ahead, behind = from_y(plane, 1), from_y(plane, -1)
    plane_other = from_cfg(plane)
    second_part = exchange(
        after(pack_queries(image_projections, 1), plane_other, first_part)
    )
    far_first = from_y(ahead[:cut], 1)
    far_second = from_y(behind[cut:], -1)
    own = [plane, ahead, behind, far_first, far_second]
    pieces = own + [plane_other] + [from_cfg(piece) for piece in own[1:]]

    spread = noise_level * jnp.sqrt(timestep / (1.0 - timestep))
    drift_gain = 1.0 + spread * spread * (1.0 - timestep) / (2.0 * timestep)
    deviation = spread * math.sqrt(step_width)
    terms = jnp.stack(
        [
            1.0 - spread * spread / (2.0 * timestep) * step_width,
            drift_gain * step_width,
            advantage / (rollouts * C) * drift_gain * step_width / (deviation * deviation),
        ]
    )

    queries_at = per_dev * 2 * kv_rows // image_count
    attended = attention(first_part, queries_at, first_part, 0, image_count, kv_rows, per_dev)
    attended = attention(
        after(second_part, ahead, behind), 0, first_part, 1, image_count, kv_rows, per_dev, (attended,)
    )
    returned = after(exchange(attended), terms)
    hidden, velocity = hidden_rows(
        place, returned, image_state, modulation[0].transpose(1, 0, 2), final_weight.T, pieces
    )
    keep, send, squares = step(
        place,
        terms,
        velocity,
        from_cfg(velocity),
        latent.transpose(0, 2, 1),
        next_latent.transpose(0, 2, 1),
        hidden,
        data_count,
    )

    kept = keep + from_cfg(send)
    share = fold(lax.all_to_all(kept, "dp", split_axis=0, concat_axis=0, tiled=True), squares)
    share = ring_sum(ring_sum(share, from_zh), from_x)
    other = from_cfg(share)
    first = c_at == 0
    half = C // 2
    gradient = jnp.concatenate(
        [jnp.where(first, share, other)[:half], jnp.where(first, other, share)[:half]], axis=0
    ).T
    square_mean = share[half : half + per_dev, 0] / (seq_count * image_count * C)
    log_prob = (
        -square_mean / (2.0 * deviation * deviation)
        - jnp.log(deviation)
        - 0.5 * math.log(2.0 * math.pi)
    )
    return (gradient, log_prob)


def solution(mesh):
    in_specs = (
        P("cfg", "dp", "seq", None),
        P("cfg", "dp", "seq", None),
        P("seq", "dp"),
        P("cfg", "dp", "seq", None),
        P("cfg", "dp", None, None),
        P(),
        P("dp", "seq", None),
        P("dp", "seq", None),
        P("dp"),
        P("dp"),
        P("dp"),
    )
    out_specs = (P("dp", None), P("dp"))
    return jax.shard_map(
        per_device, mesh=mesh, in_specs=in_specs, out_specs=out_specs, check_vma=False
    )
```

```python
import functools
import math

import jax
import jax.numpy as jnp
from jax import lax
from jax.experimental import pallas as pl
from jax.experimental.pallas import tpu as pltpu
from jax.sharding import PartitionSpec as P

C = 64
HD = 128
GROUP_SIZE = 2

cfg_scale = 4.5
noise_level = 0.7
step_width = 0.02
norm_eps = 1e-06

X, ZH, Y, ZL = 4, 4, 4, 2
VMEM_BYTES = 32 * 1024 * 1024
HIDDEN_VMEM_BYTES = 40 * 1024 * 1024
FULL_VMEM_BYTES = 61 * 1024 * 1024


def from_x(value, d):
    pairs = [(((x + d) % X) * ZH + z, x * ZH + z) for x in range(X) for z in range(ZH)]
    return lax.ppermute(value, "seq", pairs)


def from_column(value, d):
    def at(core, x, z, y, zl):
        return ((core * X + x) * ZH + z) * (Y * ZL) + y * ZL + zl

    pairs = [
        (at(core if zl == core else 1 - core, x, (z + d) % ZH, y, core), at(core, x, z, y, zl))
        for core in range(2)
        for x in range(X)
        for z in range(ZH)
        for y in range(Y)
        for zl in range(ZL)
    ]
    return lax.ppermute(value, ("cfg", "seq", "dp"), pairs)


def from_zh(value, d):
    pairs = [(x * ZH + (z + d) % ZH, x * ZH + z) for x in range(X) for z in range(ZH)]
    return lax.ppermute(value, "seq", pairs)


def from_y(value, d):
    pairs = [(((y + d) % Y) * ZL + z, y * ZL + z) for y in range(Y) for z in range(ZL)]
    return lax.ppermute(value, "dp", pairs)


def from_zl(value):
    pairs = [(y * ZL + 1 - z, y * ZL + z) for y in range(Y) for z in range(ZL)]
    return lax.ppermute(value, "dp", pairs)


def from_cfg(value):
    return lax.ppermute(value, "cfg", [(0, 1), (1, 0)])


def after(value, *others):
    return lax.optimization_barrier((value,) + others)[0]


def ring_sum(value, fetch):
    first, second, third = (fetch(value, d) for d in (1, 2, 3))
    return (value + second) + (first + third)


def pack_kernel(k_ref, v_ref, kt_ref, vt_ref, q_ref, out_ref):
    rows, text = k_ref.shape[2], kt_ref.shape[2]
    for h in range(out_ref.shape[0]):
        cols = slice(h * HD, (h + 1) * HD)
        at = 0
        for r in range(k_ref.shape[1]):
            for ref, count in ((k_ref, rows), (kt_ref, text), (v_ref, rows), (vt_ref, text)):
                out_ref[h, at : at + count, :] = ref[0, r, :, cols]
                at += count
        out_ref[h, at : at + rows, :] = q_ref[0, 0, :, cols]


def pack_queries_kernel(q_ref, out_ref):
    for h in range(out_ref.shape[0]):
        out_ref[h] = q_ref[0, 0, :, h * HD : (h + 1) * HD]


def pack(image_projections, text_projections):
    _, per_dev, rows, width = image_projections.shape
    text = text_projections.shape[2]
    heads = width // (3 * HD)
    per = 4
    steps = heads // per
    total = per_dev * 2 * (rows + text) + rows

    def spec(rollouts, count, part):
        return pl.BlockSpec((1, rollouts, count, per * HD), lambda h: (0, 0, 0, part * steps + h))

    return pl.pallas_call(
        pack_kernel,
        grid=(steps,),
        in_specs=[
            spec(per_dev, rows, 1),
            spec(per_dev, rows, 2),
            spec(per_dev, text, 0),
            spec(per_dev, text, 1),
            spec(1, rows, 0),
        ],
        out_specs=pl.BlockSpec((per, total, HD), lambda h: (h, 0, 0)),
        out_shape=jax.ShapeDtypeStruct((heads, total, HD), jnp.bfloat16),
        compiler_params=pltpu.CompilerParams(vmem_limit_bytes=FULL_VMEM_BYTES),
        cost_estimate=pl.CostEstimate(
            flops=0, bytes_accessed=2 * heads * total * HD * 2, transcendentals=0
        ),
        name="pack",
    )(image_projections, image_projections, text_projections, text_projections, image_projections)


def pack_queries(image_projections, r):
    _, _, rows, width = image_projections.shape
    heads = width // (3 * HD)
    return pl.pallas_call(
        pack_queries_kernel,
        grid=(1,),
        in_specs=[pl.BlockSpec((1, 1, rows, heads * HD), lambda i: (0, r, 0, 0))],
        out_specs=pl.BlockSpec((heads, rows, HD), lambda i: (0, 0, 0)),
        out_shape=jax.ShapeDtypeStruct((heads, rows, HD), jnp.bfloat16),
        compiler_params=pltpu.CompilerParams(vmem_limit_bytes=VMEM_BYTES),
        cost_estimate=pl.CostEstimate(
            flops=0, bytes_accessed=2 * heads * rows * HD * 2, transcendentals=0
        ),
        name="pack_queries",
    )(image_projections)


def attention_kernel(q_ref, kv_ref, *rest):
    out_ref, keys, values = rest[-3:]
    peers, kv_rows = kv_ref.shape[0], kv_ref.shape[1] // 2
    ones = jnp.ones((kv_rows, HD), jnp.bfloat16)
    for s in range(peers):
        at = slice(s * kv_rows, (s + 1) * kv_rows)
        keys[at, :] = kv_ref[s, 0:kv_rows, :]
        values[at, 0:HD] = kv_ref[s, kv_rows : 2 * kv_rows, :]
        values[at, HD : 2 * HD] = ones

    factor = math.log2(math.e) / math.sqrt(HD)
    for n in range(peers):
        scores = lax.dot_general(
            q_ref[n], keys[...], (((1,), (1,)), ((), ())), preferred_element_type=jnp.float32
        )
        highest = jnp.max(scores, axis=1, keepdims=True)
        powered = jnp.exp2((scores - highest) * factor).astype(jnp.bfloat16)
        sums = jnp.dot(powered, values[...], preferred_element_type=jnp.float32)
        out_ref[n] = (sums[:, 0:HD] / sums[:, HD : HD + 1]).astype(jnp.bfloat16)


def attention(queries, q_at, key_values, r, rows, kv_rows, per_dev, earlier=()):
    peers = queries.shape[0]
    return pl.pallas_call(
        attention_kernel,
        grid=(1,),
        in_specs=[
            pl.BlockSpec((peers, rows, HD), lambda i: (0, q_at, 0)),
            pl.BlockSpec((peers, 2 * kv_rows, HD), lambda i: (0, r, 0)),
        ]
        + [pl.BlockSpec(memory_space=pl.ANY)] * len(earlier),
        out_specs=pl.BlockSpec((peers, rows, HD), lambda i: (0, r, 0)),
        out_shape=jax.ShapeDtypeStruct((peers, per_dev * rows, HD), jnp.bfloat16),
        scratch_shapes=[
            pltpu.VMEM((peers * kv_rows, HD), jnp.bfloat16),
            pltpu.VMEM((peers * kv_rows, 2 * HD), jnp.bfloat16),
        ],
        input_output_aliases={2: 0} if earlier else {},
        compiler_params=pltpu.CompilerParams(vmem_limit_bytes=FULL_VMEM_BYTES),
        cost_estimate=pl.CostEstimate(
            flops=8 * peers * rows * peers * kv_rows * HD,
            bytes_accessed=2 * peers * (2 * rows + 2 * kv_rows) * HD,
            transcendentals=peers * rows * peers * kv_rows,
        ),
        name=f"attention{r}",
    )(queries, key_values, *earlier)


SPANS = ((0, 0), (0, 1), (1, 0), (1, 1), (3, 0), (3, 1), (2, 0), (2, 1), (2, 2))


def hidden_kernel(place, heads_ref, state_any, mods_any, final_any, *rest):
    pieces = rest[: 2 * len(SPANS)]
    hidden_ref, velocity_ref, flat, mixed, weights, state_ref, mods_ref, final_ref, sems = rest[
        2 * len(SPANS) :
    ]
    x_at, zh_at, y_at, c_at = place[0], place[1], place[2], place[3]
    per_dev, rows = state_ref.shape[1], state_ref.shape[2]
    width = weights.shape[2]
    part = weights.shape[1] // X

    def begin(source, target, n):
        copy = pltpu.make_async_copy(source, target, sems.at[n])
        copy.start()
        return copy

    copies = []
    for n, piece in enumerate(pieces):
        core, (turn, first) = n // len(SPANS), SPANS[n % len(SPANS)]
        target = weights.at[core * Y + turn, pl.ds(first * part, piece.shape[0])]
        copies.append(begin(piece, target, n))
        if n == 1:
            mods_copy = begin(mods_any, mods_ref, len(pieces))
            state_copy = begin(state_any, state_ref, len(pieces) + 1)
    final_copy = begin(final_any, final_ref, len(pieces) + 2)
    for i in range(X):
        for j in range(ZH):
            head = lax.rem(x_at + i, X) * ZH + lax.rem(zh_at + j, ZH)
            k = i * ZH + j
            flat[:, k * HD : (k + 1) * HD] = heads_ref[head]
    row_sum = jnp.zeros((per_dev * rows, 1), jnp.float32)
    square_sum = jnp.zeros((per_dev * rows, 1), jnp.float32)
    for core in range(2):
        core_at = c_at if core == 0 else 1 - c_at
        for turn in (0, 1, 3, 2):
            for n, (of_turn, _) in enumerate(SPANS):
                if of_turn == turn:
                    copies[core * len(SPANS) + n].wait()
            at = pl.ds(pl.multiple_of((lax.rem(y_at + turn, Y) * ZL + core_at) * width, 128), width)
            projected = jnp.dot(
                flat[...], weights[core * Y + turn], preferred_element_type=jnp.float32
            )
            if core == 0 and turn == 0:
                mods_copy.wait()
                state_copy.wait()
            for r in range(per_dev):
                gate = mods_ref[0, r : r + 1, at].astype(jnp.float32)
                mixed[r * rows : (r + 1) * rows, at] = (
                    state_ref[0, r, :, at].astype(jnp.float32)
                    + gate * projected[r * rows : (r + 1) * rows]
                )
            block = mixed[:, at]
            row_sum = row_sum + jnp.sum(block, axis=1, keepdims=True)
            square_sum = square_sum + jnp.sum(block * block, axis=1, keepdims=True)
    width_all = mixed.shape[1]
    center = row_sum / width_all
    square = square_sum / width_all
    inverse = lax.rsqrt(square - center * center + norm_eps)
    for r in range(per_dev):
        at = slice(r * rows, (r + 1) * rows)
        scale = 1.0 + mods_ref[2, r : r + 1, :].astype(jnp.float32)
        shift = mods_ref[1, r : r + 1, :].astype(jnp.float32)
        hidden_ref[at, :] = (
            (mixed[at, :] - center[at]) * inverse[at] * scale + shift
        ).astype(jnp.bfloat16)
    final_copy.wait()
    velocity_ref[...] = lax.dot_general(
        final_ref[...], hidden_ref[...], (((1,), (1,)), ((), ())), preferred_element_type=jnp.float32
    )


def hidden_rows(place, heads_part, image_state, modulation, final_weight, pieces):
    heads, all_rows, _ = heads_part.shape
    width_all = image_state.shape[3]
    vmem = pl.BlockSpec(memory_space=pltpu.VMEM)
    return pl.pallas_call(
        hidden_kernel,
        in_specs=[pl.BlockSpec(memory_space=pltpu.SMEM)]
        + [vmem]
        + [pl.BlockSpec(memory_space=pl.ANY)] * (3 + len(pieces)),
        out_specs=[vmem] * 2,
        out_shape=[
            jax.ShapeDtypeStruct((all_rows, width_all), jnp.bfloat16),
            jax.ShapeDtypeStruct((C, all_rows), jnp.float32),
        ],
        scratch_shapes=[
            pltpu.VMEM((all_rows, heads * HD), jnp.bfloat16),
            pltpu.VMEM((all_rows, width_all), jnp.float32),
            pltpu.VMEM((8, heads * HD, pieces[0].shape[1]), jnp.bfloat16),
            pltpu.VMEM(image_state.shape, jnp.bfloat16),
            pltpu.VMEM(modulation.shape, jnp.bfloat16),
            pltpu.VMEM(final_weight.shape, jnp.bfloat16),
            pltpu.SemaphoreType.DMA((len(pieces) + 3,)),
        ],
        compiler_params=pltpu.CompilerParams(vmem_limit_bytes=HIDDEN_VMEM_BYTES),
        cost_estimate=pl.CostEstimate(
            flops=2 * all_rows * heads * HD * width_all,
            bytes_accessed=2 * heads * HD * width_all,
            transcendentals=0,
        ),
        name="hidden",
    )(place, heads_part, image_state, modulation, final_weight, *pieces)


def step_kernel(
    place, terms, own_ref, partner_ref, latent_ref, next_ref, hidden_ref, keep_ref, send_ref, squares_ref
):
    first = place[3] == 0
    own, partner = own_ref[...], partner_ref[...]
    conditional = jnp.where(first, own, partner)
    unconditional = jnp.where(first, partner, own)
    guided = unconditional + cfg_scale * (conditional - unconditional)
    per_dev, _, rows = latent_ref.shape
    row = lax.broadcasted_iota(jnp.int32, squares_ref.shape, 0)
    squares = jnp.zeros(squares_ref.shape, jnp.float32)
    slopes = []
    for r in range(per_dev):
        step_mean = (
            latent_ref[r] * terms[0, r] - guided[:, r * rows : (r + 1) * rows] * terms[1, r]
        )
        residue = next_ref[r] - step_mean
        squares = jnp.where(row == r, jnp.sum(residue * residue), squares)
        slopes.append(terms[2, r] * residue)
    squares_ref[...] = squares
    own_slopes = jnp.where(first, cfg_scale, 1.0 - cfg_scale) * jnp.concatenate(slopes, axis=1)
    half = own_slopes.shape[0] // 2
    low, high = own_slopes[:half], own_slopes[half:]
    ordered = jnp.concatenate([jnp.where(first, low, high), jnp.where(first, high, low)], axis=0)
    partial = jnp.dot(
        ordered.astype(jnp.bfloat16), hidden_ref[...], preferred_element_type=jnp.float32
    )
    width = keep_ref.shape[2]
    for n in range(keep_ref.shape[0]):
        cols = slice(n * width, (n + 1) * width)
        keep_ref[n] = partial[:half, cols]
        send_ref[n] = partial[half:, cols]


def step(place, terms, own, partner, latent, next_latent, hidden, data_count):
    rows, width_all = hidden.shape
    cut = (data_count, C // 2, width_all // data_count)
    smem = pl.BlockSpec(memory_space=pltpu.SMEM)
    vmem = pl.BlockSpec(memory_space=pltpu.VMEM)
    return pl.pallas_call(
        step_kernel,
        in_specs=[smem] * 2 + [vmem] * 5,
        out_specs=[vmem] * 3,
        out_shape=[
            jax.ShapeDtypeStruct(cut, jnp.float32),
            jax.ShapeDtypeStruct(cut, jnp.float32),
            jax.ShapeDtypeStruct((8, 128), jnp.float32),
        ],
        compiler_params=pltpu.CompilerParams(vmem_limit_bytes=VMEM_BYTES),
        cost_estimate=pl.CostEstimate(
            flops=2 * rows * C * width_all, bytes_accessed=2 * rows * width_all, transcendentals=0
        ),
        name="step",
    )(place, terms, own, partner, latent, next_latent, hidden)


def fold_kernel(parts_ref, squares_ref, out_ref):
    count, width = parts_ref.shape[1], parts_ref.shape[2]
    out_ref[0:count, :] = jnp.sum(parts_ref[...], axis=0)
    out_ref[count : count + 8, 128:width] = jnp.zeros((8, width - 128), jnp.float32)
    out_ref[count : count + 8, 0:128] = squares_ref[...]


def fold(parts, squares):
    _, count, width = parts.shape
    vmem = pl.BlockSpec(memory_space=pltpu.VMEM)
    return pl.pallas_call(
        fold_kernel,
        in_specs=[vmem] * 2,
        out_specs=vmem,
        out_shape=jax.ShapeDtypeStruct((count + 8, width), jnp.float32),
        name="fold",
    )(parts, squares)


def exchange(send):
    return lax.all_to_all(send, "seq", split_axis=0, concat_axis=0, tiled=True)


def per_device(
    image_projections,
    text_projections,
    output_weight,
    image_state,
    modulation,
    final_weight,
    latent,
    next_latent,
    timestep,
    rewards,
    group_index,
):
    seq_count = lax.axis_size("seq")
    data_count = lax.axis_size("dp")
    per_dev = image_projections.shape[1]
    image_count = image_projections.shape[2]
    width_all = image_state.shape[3]
    rollouts = per_dev * data_count
    seq_at, dp_at, c_at = lax.axis_index("seq"), lax.axis_index("dp"), lax.axis_index("cfg")
    x_at, zh_at, y_at = seq_at // ZH, seq_at % ZH, dp_at // ZL
    place = jnp.stack([x_at, zh_at, y_at, c_at]).astype(jnp.int32)

    kv_rows = image_count + text_projections.shape[2]

    group_count = rollouts // GROUP_SIZE
    member = (group_index[:, None] == jnp.arange(group_count, dtype=jnp.int32)[None, :]).astype(
        jnp.float32
    )
    packed = pack(image_projections, text_projections)
    columns = after(output_weight, packed)
    column = jnp.concatenate([from_column(columns, d) for d in range(ZH)], axis=0)
    first_part = exchange(after(packed, column))
    depth = column.shape[0]
    ahead_own, behind_own = from_y(column, 1), from_y(column, -1)
    others = jnp.concatenate([from_x(column, d) for d in range(1, X)], axis=0)
    far_own = from_y(ahead_own, 1)
    totals = jnp.sum(member * rewards[:, None], axis=0)
    totals = ring_sum(totals, from_y)
    all_totals = totals + from_zl(totals)
    advantage = rewards - jnp.sum(member * all_totals[None, :], axis=1) / GROUP_SIZE
    rest = after(others, ahead_own, behind_own, totals)
    ahead, behind = from_y(rest, 1), from_y(rest, -1)
    early = [from_cfg(piece) for piece in (column, ahead_own, behind_own, far_own)]
    second_part = exchange(
        after(pack_queries(image_projections, 1), first_part, all_totals, *early, ahead, behind)
    )
    far_first = from_y(ahead[:depth], 1)
    far_second = from_y(behind[depth:], -1)
    late = [from_cfg(piece) for piece in (others, ahead, behind, far_first, far_second)]
    pieces = [column, others, ahead_own, ahead, behind_own, behind, far_own, far_first, far_second]
    pieces += [early[0], late[0], early[1], late[1], early[2], late[2], early[3], late[3], late[4]]

    spread = noise_level * jnp.sqrt(timestep / (1.0 - timestep))
    drift_gain = 1.0 + spread * spread * (1.0 - timestep) / (2.0 * timestep)
    deviation = spread * math.sqrt(step_width)
    terms = jnp.stack(
        [
            1.0 - spread * spread / (2.0 * timestep) * step_width,
            drift_gain * step_width,
            advantage / (rollouts * C) * drift_gain * step_width / (deviation * deviation),
        ]
    )

    queries_at = per_dev * 2 * kv_rows // image_count
    attended = attention(first_part, queries_at, first_part, 0, image_count, kv_rows, per_dev)
    attended = attention(
        second_part, 0, first_part, 1, image_count, kv_rows, per_dev, (attended,)
    )
    returned = after(exchange(after(attended, far_first, far_second)), terms)
    hidden, velocity = hidden_rows(
        place, returned, image_state, modulation[0].transpose(1, 0, 2), final_weight.T, pieces
    )
    keep, send, squares = step(
        place,
        terms,
        velocity,
        from_cfg(velocity),
        latent.transpose(0, 2, 1),
        next_latent.transpose(0, 2, 1),
        hidden,
        data_count,
    )

    kept = keep + from_cfg(send)
    share = fold(lax.all_to_all(kept, "dp", split_axis=0, concat_axis=0, tiled=True), squares)
    share = ring_sum(ring_sum(share, from_zh), from_x)
    other = from_cfg(share)
    first = c_at == 0
    half = C // 2
    gradient = jnp.concatenate(
        [jnp.where(first, share, other)[:half], jnp.where(first, other, share)[:half]], axis=0
    ).T
    square_mean = share[half : half + per_dev, 0] / (seq_count * image_count * C)
    log_prob = (
        -square_mean / (2.0 * deviation * deviation)
        - jnp.log(deviation)
        - 0.5 * math.log(2.0 * math.pi)
    )
    return (gradient, log_prob)


def solution(mesh):
    in_specs = (
        P("cfg", "dp", "seq", None),
        P("cfg", "dp", "seq", None),
        P("seq", "dp"),
        P("cfg", "dp", "seq", None),
        P("cfg", "dp", None, None),
        P(),
        P("dp", "seq", None),
        P("dp", "seq", None),
        P("dp"),
        P("dp"),
        P("dp"),
    )
    out_specs = (P("dp", None), P("dp"))
    return jax.shard_map(
        per_device, mesh=mesh, in_specs=in_specs, out_specs=out_specs, check_vma=False
    )
```

```python
import functools
import math

import jax
import jax.numpy as jnp
from jax import lax
from jax.experimental import pallas as pl
from jax.experimental.pallas import tpu as pltpu
from jax.sharding import PartitionSpec as P

C = 64
HD = 128
GROUP_SIZE = 2

cfg_scale = 4.5
noise_level = 0.7
step_width = 0.02
norm_eps = 1e-06

X, ZH, Y, ZL = 4, 4, 4, 2
VMEM_BYTES = 32 * 1024 * 1024
HIDDEN_VMEM_BYTES = 50 * 1024 * 1024
FULL_VMEM_BYTES = 61 * 1024 * 1024


def from_x(value, d):
    pairs = [(((x + d) % X) * ZH + z, x * ZH + z) for x in range(X) for z in range(ZH)]
    return lax.ppermute(value, "seq", pairs)


def from_column(value, d):
    def at(core, x, z, y, zl):
        return ((core * X + x) * ZH + z) * (Y * ZL) + y * ZL + zl

    pairs = [
        (at(core if zl == core else 1 - core, x, (z + d) % ZH, y, core), at(core, x, z, y, zl))
        for core in range(2)
        for x in range(X)
        for z in range(ZH)
        for y in range(Y)
        for zl in range(ZL)
    ]
    return lax.ppermute(value, ("cfg", "seq", "dp"), pairs)


def from_zh(value, d):
    pairs = [(x * ZH + (z + d) % ZH, x * ZH + z) for x in range(X) for z in range(ZH)]
    return lax.ppermute(value, "seq", pairs)


def from_y(value, d):
    pairs = [(((y + d) % Y) * ZL + z, y * ZL + z) for y in range(Y) for z in range(ZL)]
    return lax.ppermute(value, "dp", pairs)


def from_zl(value):
    pairs = [(y * ZL + 1 - z, y * ZL + z) for y in range(Y) for z in range(ZL)]
    return lax.ppermute(value, "dp", pairs)


def from_cfg(value):
    return lax.ppermute(value, "cfg", [(0, 1), (1, 0)])


def after(value, *others):
    return lax.optimization_barrier((value,) + others)[0]


def ring_sum(value, fetch):
    first, second, third = (fetch(value, d) for d in (1, 2, 3))
    return (value + second) + (first + third)


def pack_kernel(k_ref, v_ref, kt_ref, vt_ref, q_ref, out_ref):
    rows, text = k_ref.shape[2], kt_ref.shape[2]
    for h in range(out_ref.shape[0]):
        cols = slice(h * HD, (h + 1) * HD)
        at = 0
        for r in range(k_ref.shape[1]):
            for ref, count in ((k_ref, rows), (kt_ref, text), (v_ref, rows), (vt_ref, text)):
                out_ref[h, at : at + count, :] = ref[0, r, :, cols]
                at += count
        out_ref[h, at : at + rows, :] = q_ref[0, 0, :, cols]


def pack_queries_kernel(q_ref, out_ref):
    for h in range(out_ref.shape[0]):
        out_ref[h] = q_ref[0, 0, :, h * HD : (h + 1) * HD]


def pack(image_projections, text_projections):
    _, per_dev, rows, width = image_projections.shape
    text = text_projections.shape[2]
    heads = width // (3 * HD)
    per = 4
    steps = heads // per
    total = per_dev * 2 * (rows + text) + rows

    def spec(rollouts, count, part):
        return pl.BlockSpec((1, rollouts, count, per * HD), lambda h: (0, 0, 0, part * steps + h))

    return pl.pallas_call(
        pack_kernel,
        grid=(steps,),
        in_specs=[
            spec(per_dev, rows, 1),
            spec(per_dev, rows, 2),
            spec(per_dev, text, 0),
            spec(per_dev, text, 1),
            spec(1, rows, 0),
        ],
        out_specs=pl.BlockSpec((per, total, HD), lambda h: (h, 0, 0)),
        out_shape=jax.ShapeDtypeStruct((heads, total, HD), jnp.bfloat16),
        compiler_params=pltpu.CompilerParams(vmem_limit_bytes=FULL_VMEM_BYTES),
        cost_estimate=pl.CostEstimate(
            flops=0, bytes_accessed=2 * heads * total * HD * 2, transcendentals=0
        ),
        name="pack",
    )(image_projections, image_projections, text_projections, text_projections, image_projections)


def pack_queries(image_projections, r):
    _, _, rows, width = image_projections.shape
    heads = width // (3 * HD)
    return pl.pallas_call(
        pack_queries_kernel,
        grid=(1,),
        in_specs=[pl.BlockSpec((1, 1, rows, heads * HD), lambda i: (0, r, 0, 0))],
        out_specs=pl.BlockSpec((heads, rows, HD), lambda i: (0, 0, 0)),
        out_shape=jax.ShapeDtypeStruct((heads, rows, HD), jnp.bfloat16),
        compiler_params=pltpu.CompilerParams(vmem_limit_bytes=VMEM_BYTES),
        cost_estimate=pl.CostEstimate(
            flops=0, bytes_accessed=2 * heads * rows * HD * 2, transcendentals=0
        ),
        name="pack_queries",
    )(image_projections)


def attention_kernel(q_ref, kv_ref, *rest):
    out_ref, keys, values = rest[-3:]
    peers, kv_rows = kv_ref.shape[0], kv_ref.shape[1] // 2
    ones = jnp.ones((kv_rows, HD), jnp.bfloat16)
    for s in range(peers):
        at = slice(s * kv_rows, (s + 1) * kv_rows)
        keys[at, :] = kv_ref[s, 0:kv_rows, :]
        values[at, 0:HD] = kv_ref[s, kv_rows : 2 * kv_rows, :]
        values[at, HD : 2 * HD] = ones

    factor = math.log2(math.e) / math.sqrt(HD)
    for n in range(peers):
        scores = lax.dot_general(
            q_ref[n], keys[...], (((1,), (1,)), ((), ())), preferred_element_type=jnp.float32
        )
        highest = jnp.max(scores, axis=1, keepdims=True)
        powered = jnp.exp2((scores - highest) * factor).astype(jnp.bfloat16)
        sums = jnp.dot(powered, values[...], preferred_element_type=jnp.float32)
        out_ref[n] = (sums[:, 0:HD] / sums[:, HD : HD + 1]).astype(jnp.bfloat16)


def attention(queries, q_at, key_values, r, rows, kv_rows, per_dev, earlier=()):
    peers = queries.shape[0]
    return pl.pallas_call(
        attention_kernel,
        grid=(1,),
        in_specs=[
            pl.BlockSpec((peers, rows, HD), lambda i: (0, q_at, 0)),
            pl.BlockSpec((peers, 2 * kv_rows, HD), lambda i: (0, r, 0)),
        ]
        + [pl.BlockSpec(memory_space=pl.ANY)] * len(earlier),
        out_specs=pl.BlockSpec((peers, rows, HD), lambda i: (0, r, 0)),
        out_shape=jax.ShapeDtypeStruct((peers, per_dev * rows, HD), jnp.bfloat16),
        scratch_shapes=[
            pltpu.VMEM((peers * kv_rows, HD), jnp.bfloat16),
            pltpu.VMEM((peers * kv_rows, 2 * HD), jnp.bfloat16),
        ],
        input_output_aliases={2: 0} if earlier else {},
        compiler_params=pltpu.CompilerParams(vmem_limit_bytes=FULL_VMEM_BYTES),
        cost_estimate=pl.CostEstimate(
            flops=8 * peers * rows * peers * kv_rows * HD,
            bytes_accessed=2 * peers * (2 * rows + 2 * kv_rows) * HD,
            transcendentals=peers * rows * peers * kv_rows,
        ),
        name=f"attention{r}",
    )(queries, key_values, *earlier)


SPANS = ((0, 0), (1, 0), (3, 0), (2, 0), (2, 2))


def hidden_kernel(place, heads_ref, state_any, mods_any, final_any, *rest):
    pieces = rest[: 2 * len(SPANS)]
    hidden_ref, velocity_ref, flat, mixed, weights, state_ref, mods_ref, final_ref, sems = rest[
        2 * len(SPANS) :
    ]
    x_at, zh_at, y_at, c_at = place[0], place[1], place[2], place[3]
    per_dev, rows = state_ref.shape[1], state_ref.shape[2]
    width = weights.shape[2]
    part = weights.shape[1] // X

    def begin(source, target, n):
        copy = pltpu.make_async_copy(source, target, sems.at[n])
        copy.start()
        return copy

    copies = []
    for n, piece in enumerate(pieces):
        core, (turn, first) = n // len(SPANS), SPANS[n % len(SPANS)]
        target = weights.at[core * Y + turn, pl.ds(first * part, piece.shape[0])]
        copies.append(begin(piece, target, n))
        if n == 1:
            mods_copy = begin(mods_any, mods_ref, len(pieces))
            state_copy = begin(state_any, state_ref, len(pieces) + 1)
    final_copy = begin(final_any, final_ref, len(pieces) + 2)
    for i in range(X):
        for j in range(ZH):
            head = lax.rem(x_at + i, X) * ZH + lax.rem(zh_at + j, ZH)
            k = i * ZH + j
            flat[:, k * HD : (k + 1) * HD] = heads_ref[head]
    row_sum = jnp.zeros((per_dev * rows, 1), jnp.float32)
    square_sum = jnp.zeros((per_dev * rows, 1), jnp.float32)
    for core in range(2):
        core_at = c_at if core == 0 else 1 - c_at
        for turn in (0, 1, 3, 2):
            for n, (of_turn, _) in enumerate(SPANS):
                if of_turn == turn:
                    copies[core * len(SPANS) + n].wait()
            at = pl.ds(pl.multiple_of((lax.rem(y_at + turn, Y) * ZL + core_at) * width, 128), width)
            projected = jnp.dot(
                flat[...], weights[core * Y + turn], preferred_element_type=jnp.float32
            )
            if core == 0 and turn == 0:
                mods_copy.wait()
                state_copy.wait()
            for r in range(per_dev):
                gate = mods_ref[0, r : r + 1, at].astype(jnp.float32)
                mixed[r * rows : (r + 1) * rows, at] = (
                    state_ref[0, r, :, at].astype(jnp.float32)
                    + gate * projected[r * rows : (r + 1) * rows]
                )
            block = mixed[:, at]
            row_sum = row_sum + jnp.sum(block, axis=1, keepdims=True)
            square_sum = square_sum + jnp.sum(block * block, axis=1, keepdims=True)
    width_all = mixed.shape[1]
    center = row_sum / width_all
    square = square_sum / width_all
    inverse = lax.rsqrt(square - center * center + norm_eps)
    for r in range(per_dev):
        at = slice(r * rows, (r + 1) * rows)
        scale = 1.0 + mods_ref[2, r : r + 1, :].astype(jnp.float32)
        shift = mods_ref[1, r : r + 1, :].astype(jnp.float32)
        hidden_ref[at, :] = (
            (mixed[at, :] - center[at]) * inverse[at] * scale + shift
        ).astype(jnp.bfloat16)
    final_copy.wait()
    velocity_ref[...] = lax.dot_general(
        final_ref[...], hidden_ref[...], (((1,), (1,)), ((), ())), preferred_element_type=jnp.float32
    )


def hidden_rows(place, heads_part, image_state, modulation, final_weight, pieces):
    heads, all_rows, _ = heads_part.shape
    width_all = image_state.shape[3]
    vmem = pl.BlockSpec(memory_space=pltpu.VMEM)
    return pl.pallas_call(
        hidden_kernel,
        in_specs=[pl.BlockSpec(memory_space=pltpu.SMEM)]
        + [vmem]
        + [pl.BlockSpec(memory_space=pl.ANY)] * (3 + len(pieces)),
        out_specs=[vmem] * 2,
        out_shape=[
            jax.ShapeDtypeStruct((all_rows, width_all), jnp.bfloat16),
            jax.ShapeDtypeStruct((C, all_rows), jnp.float32),
        ],
        scratch_shapes=[
            pltpu.VMEM((all_rows, heads * HD), jnp.bfloat16),
            pltpu.VMEM((all_rows, width_all), jnp.float32),
            pltpu.VMEM((8, heads * HD, pieces[0].shape[1]), jnp.bfloat16),
            pltpu.VMEM(image_state.shape, jnp.bfloat16),
            pltpu.VMEM(modulation.shape, jnp.bfloat16),
            pltpu.VMEM(final_weight.shape, jnp.bfloat16),
            pltpu.SemaphoreType.DMA((len(pieces) + 3,)),
        ],
        compiler_params=pltpu.CompilerParams(vmem_limit_bytes=HIDDEN_VMEM_BYTES),
        cost_estimate=pl.CostEstimate(
            flops=2 * all_rows * heads * HD * width_all,
            bytes_accessed=2 * heads * HD * width_all,
            transcendentals=0,
        ),
        name="hidden",
    )(place, heads_part, image_state, modulation, final_weight, *pieces)


def step_kernel(
    place, terms, own_ref, partner_ref, latent_ref, next_ref, hidden_ref, keep_ref, send_ref, squares_ref
):
    first = place[3] == 0
    own, partner = own_ref[...], partner_ref[...]
    conditional = jnp.where(first, own, partner)
    unconditional = jnp.where(first, partner, own)
    guided = unconditional + cfg_scale * (conditional - unconditional)
    per_dev, _, rows = latent_ref.shape
    row = lax.broadcasted_iota(jnp.int32, squares_ref.shape, 0)
    squares = jnp.zeros(squares_ref.shape, jnp.float32)
    slopes = []
    for r in range(per_dev):
        step_mean = (
            latent_ref[r] * terms[0, r] - guided[:, r * rows : (r + 1) * rows] * terms[1, r]
        )
        residue = next_ref[r] - step_mean
        squares = jnp.where(row == r, jnp.sum(residue * residue), squares)
        slopes.append(terms[2, r] * residue)
    squares_ref[...] = squares
    own_slopes = jnp.where(first, cfg_scale, 1.0 - cfg_scale) * jnp.concatenate(slopes, axis=1)
    half = own_slopes.shape[0] // 2
    low, high = own_slopes[:half], own_slopes[half:]
    ordered = jnp.concatenate([jnp.where(first, low, high), jnp.where(first, high, low)], axis=0)
    partial = jnp.dot(
        ordered.astype(jnp.bfloat16), hidden_ref[...], preferred_element_type=jnp.float32
    )
    width = keep_ref.shape[2]
    for n in range(keep_ref.shape[0]):
        cols = slice(n * width, (n + 1) * width)
        keep_ref[n] = partial[:half, cols]
        send_ref[n] = partial[half:, cols]


def step(place, terms, own, partner, latent, next_latent, hidden, data_count):
    rows, width_all = hidden.shape
    cut = (data_count, C // 2, width_all // data_count)
    smem = pl.BlockSpec(memory_space=pltpu.SMEM)
    vmem = pl.BlockSpec(memory_space=pltpu.VMEM)
    return pl.pallas_call(
        step_kernel,
        in_specs=[smem] * 2 + [vmem] * 5,
        out_specs=[vmem] * 3,
        out_shape=[
            jax.ShapeDtypeStruct(cut, jnp.float32),
            jax.ShapeDtypeStruct(cut, jnp.float32),
            jax.ShapeDtypeStruct((8, 128), jnp.float32),
        ],
        compiler_params=pltpu.CompilerParams(vmem_limit_bytes=VMEM_BYTES),
        cost_estimate=pl.CostEstimate(
            flops=2 * rows * C * width_all, bytes_accessed=2 * rows * width_all, transcendentals=0
        ),
        name="step",
    )(place, terms, own, partner, latent, next_latent, hidden)


def fold_kernel(parts_ref, squares_ref, out_ref):
    count, width = parts_ref.shape[1], parts_ref.shape[2]
    out_ref[0:count, :] = jnp.sum(parts_ref[...], axis=0)
    out_ref[count : count + 8, 128:width] = jnp.zeros((8, width - 128), jnp.float32)
    out_ref[count : count + 8, 0:128] = squares_ref[...]


def fold(parts, squares):
    _, count, width = parts.shape
    vmem = pl.BlockSpec(memory_space=pltpu.VMEM)
    return pl.pallas_call(
        fold_kernel,
        in_specs=[vmem] * 2,
        out_specs=vmem,
        out_shape=jax.ShapeDtypeStruct((count + 8, width), jnp.float32),
        name="fold",
    )(parts, squares)


def exchange(send):
    return lax.all_to_all(send, "seq", split_axis=0, concat_axis=0, tiled=True)


def per_device(
    image_projections,
    text_projections,
    output_weight,
    image_state,
    modulation,
    final_weight,
    latent,
    next_latent,
    timestep,
    rewards,
    group_index,
):
    seq_count = lax.axis_size("seq")
    data_count = lax.axis_size("dp")
    per_dev = image_projections.shape[1]
    image_count = image_projections.shape[2]
    width_all = image_state.shape[3]
    rollouts = per_dev * data_count
    seq_at, dp_at, c_at = lax.axis_index("seq"), lax.axis_index("dp"), lax.axis_index("cfg")
    x_at, zh_at, y_at = seq_at // ZH, seq_at % ZH, dp_at // ZL
    place = jnp.stack([x_at, zh_at, y_at, c_at]).astype(jnp.int32)

    kv_rows = image_count + text_projections.shape[2]

    group_count = rollouts // GROUP_SIZE
    member = (group_index[:, None] == jnp.arange(group_count, dtype=jnp.int32)[None, :]).astype(
        jnp.float32
    )
    column = jnp.concatenate([from_column(output_weight, d) for d in range(ZH)], axis=0)
    totals = jnp.sum(member * rewards[:, None], axis=0)
    first_part = exchange(after(pack(image_projections, text_projections), column))
    totals = ring_sum(totals, from_y)
    column = after(column, totals)
    all_totals = totals + from_zl(totals)
    advantage = rewards - jnp.sum(member * all_totals[None, :], axis=1) / GROUP_SIZE
    plane = jnp.concatenate([column] + [from_x(column, d) for d in range(1, X)], axis=0)
    cut = plane.shape[0] // 2
    ahead, behind = from_y(plane, 1), from_y(plane, -1)
    plane_other = from_cfg(plane)
    second_part = exchange(
        after(pack_queries(image_projections, 1), plane_other, first_part, all_totals)
    )
    far_first = from_y(ahead[:cut], 1)
    far_second = from_y(behind[cut:], -1)
    own = [plane, ahead, behind, far_first, far_second]
    pieces = own + [plane_other] + [from_cfg(piece) for piece in own[1:]]

    spread = noise_level * jnp.sqrt(timestep / (1.0 - timestep))
    drift_gain = 1.0 + spread * spread * (1.0 - timestep) / (2.0 * timestep)
    deviation = spread * math.sqrt(step_width)
    terms = jnp.stack(
        [
            1.0 - spread * spread / (2.0 * timestep) * step_width,
            drift_gain * step_width,
            advantage / (rollouts * C) * drift_gain * step_width / (deviation * deviation),
        ]
    )

    queries_at = per_dev * 2 * kv_rows // image_count
    first_part = after(first_part, ahead, behind)
    attended = attention(first_part, queries_at, first_part, 0, image_count, kv_rows, per_dev)
    attended = attention(
        second_part, 0, first_part, 1, image_count, kv_rows, per_dev, (attended,)
    )
    returned = after(exchange(after(attended, far_first, far_second)), terms)
    hidden, velocity = hidden_rows(
        place, returned, image_state, modulation[0].transpose(1, 0, 2), final_weight.T, pieces
    )
    keep, send, squares = step(
        place,
        terms,
        velocity,
        from_cfg(velocity),
        latent.transpose(0, 2, 1),
        next_latent.transpose(0, 2, 1),
        hidden,
        data_count,
    )

    kept = keep + from_cfg(send)
    share = fold(lax.all_to_all(kept, "dp", split_axis=0, concat_axis=0, tiled=True), squares)
    share = ring_sum(ring_sum(share, from_zh), from_x)
    other = from_cfg(share)
    first = c_at == 0
    half = C // 2
    gradient = jnp.concatenate(
        [jnp.where(first, share, other)[:half], jnp.where(first, other, share)[:half]], axis=0
    ).T
    square_mean = share[half : half + per_dev, 0] / (seq_count * image_count * C)
    log_prob = (
        -square_mean / (2.0 * deviation * deviation)
        - jnp.log(deviation)
        - 0.5 * math.log(2.0 * math.pi)
    )
    return (gradient, log_prob)


def solution(mesh):
    in_specs = (
        P("cfg", "dp", "seq", None),
        P("cfg", "dp", "seq", None),
        P("seq", "dp"),
        P("cfg", "dp", "seq", None),
        P("cfg", "dp", None, None),
        P(),
        P("dp", "seq", None),
        P("dp", "seq", None),
        P("dp"),
        P("dp"),
        P("dp"),
    )
    out_specs = (P("dp", None), P("dp"))
    return jax.shard_map(
        per_device, mesh=mesh, in_specs=in_specs, out_specs=out_specs, check_vma=False
    )
```

```python
import functools
import math

import jax
import jax.numpy as jnp
from jax import lax
from jax.experimental import pallas as pl
from jax.experimental.pallas import tpu as pltpu
from jax.sharding import PartitionSpec as P

C = 64
HD = 128
GROUP_SIZE = 2

cfg_scale = 4.5
noise_level = 0.7
step_width = 0.02
norm_eps = 1e-06

X, ZH, Y, ZL = 4, 4, 4, 2
VMEM_BYTES = 32 * 1024 * 1024
HIDDEN_VMEM_BYTES = 50 * 1024 * 1024
FULL_VMEM_BYTES = 61 * 1024 * 1024


def from_x(value, d):
    pairs = [(((x + d) % X) * ZH + z, x * ZH + z) for x in range(X) for z in range(ZH)]
    return lax.ppermute(value, "seq", pairs)


def from_column(value, d):
    def at(core, x, z, y, zl):
        return ((core * X + x) * ZH + z) * (Y * ZL) + y * ZL + zl

    pairs = [
        (at(core if zl == core else 1 - core, x, (z + d) % ZH, y, core), at(core, x, z, y, zl))
        for core in range(2)
        for x in range(X)
        for z in range(ZH)
        for y in range(Y)
        for zl in range(ZL)
    ]
    return lax.ppermute(value, ("cfg", "seq", "dp"), pairs)


def from_zh(value, d):
    pairs = [(x * ZH + (z + d) % ZH, x * ZH + z) for x in range(X) for z in range(ZH)]
    return lax.ppermute(value, "seq", pairs)


def from_y(value, d):
    pairs = [(((y + d) % Y) * ZL + z, y * ZL + z) for y in range(Y) for z in range(ZL)]
    return lax.ppermute(value, "dp", pairs)


def from_zl(value):
    pairs = [(y * ZL + 1 - z, y * ZL + z) for y in range(Y) for z in range(ZL)]
    return lax.ppermute(value, "dp", pairs)


def from_cfg(value):
    return lax.ppermute(value, "cfg", [(0, 1), (1, 0)])


def after(value, *others):
    return lax.optimization_barrier((value,) + others)[0]


def ring_sum(value, fetch):
    first, second, third = (fetch(value, d) for d in (1, 2, 3))
    return (value + second) + (first + third)


def pack_kernel(k_ref, v_ref, kt_ref, vt_ref, q_ref, out_ref):
    rows, text = k_ref.shape[2], kt_ref.shape[2]
    for h in range(out_ref.shape[0]):
        cols = slice(h * HD, (h + 1) * HD)
        at = 0
        for r in range(k_ref.shape[1]):
            for ref, count in ((k_ref, rows), (kt_ref, text), (v_ref, rows), (vt_ref, text)):
                out_ref[h, at : at + count, :] = ref[0, r, :, cols]
                at += count
        out_ref[h, at : at + rows, :] = q_ref[0, 0, :, cols]


def pack_queries_kernel(q_ref, out_ref):
    for h in range(out_ref.shape[0]):
        out_ref[h] = q_ref[0, 0, :, h * HD : (h + 1) * HD]


def pack(image_projections, text_projections):
    _, per_dev, rows, width = image_projections.shape
    text = text_projections.shape[2]
    heads = width // (3 * HD)
    per = 4
    steps = heads // per
    total = per_dev * 2 * (rows + text) + rows

    def spec(rollouts, count, part):
        return pl.BlockSpec((1, rollouts, count, per * HD), lambda h: (0, 0, 0, part * steps + h))

    return pl.pallas_call(
        pack_kernel,
        grid=(steps,),
        in_specs=[
            spec(per_dev, rows, 1),
            spec(per_dev, rows, 2),
            spec(per_dev, text, 0),
            spec(per_dev, text, 1),
            spec(1, rows, 0),
        ],
        out_specs=pl.BlockSpec((per, total, HD), lambda h: (h, 0, 0)),
        out_shape=jax.ShapeDtypeStruct((heads, total, HD), jnp.bfloat16),
        compiler_params=pltpu.CompilerParams(vmem_limit_bytes=FULL_VMEM_BYTES),
        cost_estimate=pl.CostEstimate(
            flops=0, bytes_accessed=2 * heads * total * HD * 2, transcendentals=0
        ),
        name="pack",
    )(image_projections, image_projections, text_projections, text_projections, image_projections)


def pack_queries(image_projections, r):
    _, _, rows, width = image_projections.shape
    heads = width // (3 * HD)
    return pl.pallas_call(
        pack_queries_kernel,
        grid=(1,),
        in_specs=[pl.BlockSpec((1, 1, rows, heads * HD), lambda i: (0, r, 0, 0))],
        out_specs=pl.BlockSpec((heads, rows, HD), lambda i: (0, 0, 0)),
        out_shape=jax.ShapeDtypeStruct((heads, rows, HD), jnp.bfloat16),
        compiler_params=pltpu.CompilerParams(vmem_limit_bytes=VMEM_BYTES),
        cost_estimate=pl.CostEstimate(
            flops=0, bytes_accessed=2 * heads * rows * HD * 2, transcendentals=0
        ),
        name="pack_queries",
    )(image_projections)


def attention_kernel(q_ref, kv_ref, *rest):
    out_ref, keys, values = rest[-3:]
    peers, kv_rows = kv_ref.shape[0], kv_ref.shape[1] // 2
    ones = jnp.ones((kv_rows, HD), jnp.bfloat16)
    for s in range(peers):
        at = slice(s * kv_rows, (s + 1) * kv_rows)
        keys[at, :] = kv_ref[s, 0:kv_rows, :]
        values[at, 0:HD] = kv_ref[s, kv_rows : 2 * kv_rows, :]
        values[at, HD : 2 * HD] = ones

    factor = math.log2(math.e) / math.sqrt(HD)
    for n in range(peers):
        scores = lax.dot_general(
            q_ref[n], keys[...], (((1,), (1,)), ((), ())), preferred_element_type=jnp.float32
        )
        highest = jnp.max(scores, axis=1, keepdims=True)
        powered = jnp.exp2((scores - highest) * factor).astype(jnp.bfloat16)
        sums = jnp.dot(powered, values[...], preferred_element_type=jnp.float32)
        out_ref[n] = (sums[:, 0:HD] / sums[:, HD : HD + 1]).astype(jnp.bfloat16)


def attention(queries, q_at, key_values, r, rows, kv_rows, per_dev, earlier=()):
    peers = queries.shape[0]
    return pl.pallas_call(
        attention_kernel,
        grid=(1,),
        in_specs=[
            pl.BlockSpec((peers, rows, HD), lambda i: (0, q_at, 0)),
            pl.BlockSpec((peers, 2 * kv_rows, HD), lambda i: (0, r, 0)),
        ]
        + [pl.BlockSpec(memory_space=pl.ANY)] * len(earlier),
        out_specs=pl.BlockSpec((peers, rows, HD), lambda i: (0, r, 0)),
        out_shape=jax.ShapeDtypeStruct((peers, per_dev * rows, HD), jnp.bfloat16),
        scratch_shapes=[
            pltpu.VMEM((peers * kv_rows, HD), jnp.bfloat16),
            pltpu.VMEM((peers * kv_rows, 2 * HD), jnp.bfloat16),
        ],
        input_output_aliases={2: 0} if earlier else {},
        compiler_params=pltpu.CompilerParams(vmem_limit_bytes=FULL_VMEM_BYTES),
        cost_estimate=pl.CostEstimate(
            flops=8 * peers * rows * peers * kv_rows * HD,
            bytes_accessed=2 * peers * (2 * rows + 2 * kv_rows) * HD,
            transcendentals=peers * rows * peers * kv_rows,
        ),
        name=f"attention{r}",
    )(queries, key_values, *earlier)


SPANS = ((0, 0), (0, 2), (1, 0), (1, 2), (3, 0), (3, 2), (2, 0), (2, 2))


def hidden_kernel(place, heads_ref, state_any, mods_any, final_any, *rest):
    pieces = rest[: 2 * len(SPANS)]
    hidden_ref, velocity_ref, flat, mixed, weights, state_ref, mods_ref, final_ref, sems = rest[
        2 * len(SPANS) :
    ]
    x_at, zh_at, y_at, c_at = place[0], place[1], place[2], place[3]
    per_dev, rows = state_ref.shape[1], state_ref.shape[2]
    width = weights.shape[2]
    part = weights.shape[1] // X

    def begin(source, target, n):
        copy = pltpu.make_async_copy(source, target, sems.at[n])
        copy.start()
        return copy

    copies = []
    for n, piece in enumerate(pieces):
        core, (turn, first) = n // len(SPANS), SPANS[n % len(SPANS)]
        target = weights.at[core * Y + turn, pl.ds(first * part, piece.shape[0])]
        copies.append(begin(piece, target, n))
        if n == 1:
            mods_copy = begin(mods_any, mods_ref, len(pieces))
            state_copy = begin(state_any, state_ref, len(pieces) + 1)
    final_copy = begin(final_any, final_ref, len(pieces) + 2)
    for i in range(X):
        for j in range(ZH):
            head = lax.rem(x_at + i, X) * ZH + lax.rem(zh_at + j, ZH)
            k = i * ZH + j
            flat[:, k * HD : (k + 1) * HD] = heads_ref[head]
    row_sum = jnp.zeros((per_dev * rows, 1), jnp.float32)
    square_sum = jnp.zeros((per_dev * rows, 1), jnp.float32)
    for core in range(2):
        core_at = c_at if core == 0 else 1 - c_at
        for turn in (0, 1, 3, 2):
            for n, (of_turn, _) in enumerate(SPANS):
                if of_turn == turn:
                    copies[core * len(SPANS) + n].wait()
            at = pl.ds(pl.multiple_of((lax.rem(y_at + turn, Y) * ZL + core_at) * width, 128), width)
            projected = jnp.dot(
                flat[...], weights[core * Y + turn], preferred_element_type=jnp.float32
            )
            if core == 0 and turn == 0:
                mods_copy.wait()
                state_copy.wait()
            for r in range(per_dev):
                gate = mods_ref[0, r : r + 1, at].astype(jnp.float32)
                mixed[r * rows : (r + 1) * rows, at] = (
                    state_ref[0, r, :, at].astype(jnp.float32)
                    + gate * projected[r * rows : (r + 1) * rows]
                )
            block = mixed[:, at]
            row_sum = row_sum + jnp.sum(block, axis=1, keepdims=True)
            square_sum = square_sum + jnp.sum(block * block, axis=1, keepdims=True)
    width_all = mixed.shape[1]
    center = row_sum / width_all
    square = square_sum / width_all
    inverse = lax.rsqrt(square - center * center + norm_eps)
    for r in range(per_dev):
        at = slice(r * rows, (r + 1) * rows)
        scale = 1.0 + mods_ref[2, r : r + 1, :].astype(jnp.float32)
        shift = mods_ref[1, r : r + 1, :].astype(jnp.float32)
        hidden_ref[at, :] = (
            (mixed[at, :] - center[at]) * inverse[at] * scale + shift
        ).astype(jnp.bfloat16)
    final_copy.wait()
    velocity_ref[...] = lax.dot_general(
        final_ref[...], hidden_ref[...], (((1,), (1,)), ((), ())), preferred_element_type=jnp.float32
    )


def hidden_rows(place, heads_part, image_state, modulation, final_weight, pieces):
    heads, all_rows, _ = heads_part.shape
    width_all = image_state.shape[3]
    vmem = pl.BlockSpec(memory_space=pltpu.VMEM)
    return pl.pallas_call(
        hidden_kernel,
        in_specs=[pl.BlockSpec(memory_space=pltpu.SMEM)]
        + [vmem]
        + [pl.BlockSpec(memory_space=pl.ANY)] * (3 + len(pieces)),
        out_specs=[vmem] * 2,
        out_shape=[
            jax.ShapeDtypeStruct((all_rows, width_all), jnp.bfloat16),
            jax.ShapeDtypeStruct((C, all_rows), jnp.float32),
        ],
        scratch_shapes=[
            pltpu.VMEM((all_rows, heads * HD), jnp.bfloat16),
            pltpu.VMEM((all_rows, width_all), jnp.float32),
            pltpu.VMEM((8, heads * HD, pieces[0].shape[1]), jnp.bfloat16),
            pltpu.VMEM(image_state.shape, jnp.bfloat16),
            pltpu.VMEM(modulation.shape, jnp.bfloat16),
            pltpu.VMEM(final_weight.shape, jnp.bfloat16),
            pltpu.SemaphoreType.DMA((len(pieces) + 3,)),
        ],
        compiler_params=pltpu.CompilerParams(vmem_limit_bytes=HIDDEN_VMEM_BYTES),
        cost_estimate=pl.CostEstimate(
            flops=2 * all_rows * heads * HD * width_all,
            bytes_accessed=2 * heads * HD * width_all,
            transcendentals=0,
        ),
        name="hidden",
    )(place, heads_part, image_state, modulation, final_weight, *pieces)


def step_kernel(
    place,
    terms,
    own_ref,
    partner_ref,
    latent_ref,
    next_ref,
    hidden_any,
    keep_ref,
    send_ref,
    squares_ref,
    hidden_ref,
    sem,
):
    copy = pltpu.make_async_copy(hidden_any, hidden_ref, sem)
    copy.start()
    first = place[3] == 0
    own, partner = own_ref[...], partner_ref[...]
    conditional = jnp.where(first, own, partner)
    unconditional = jnp.where(first, partner, own)
    guided = unconditional + cfg_scale * (conditional - unconditional)
    per_dev, _, rows = latent_ref.shape
    row = lax.broadcasted_iota(jnp.int32, squares_ref.shape, 0)
    squares = jnp.zeros(squares_ref.shape, jnp.float32)
    slopes = []
    for r in range(per_dev):
        step_mean = (
            latent_ref[r] * terms[0, r] - guided[:, r * rows : (r + 1) * rows] * terms[1, r]
        )
        residue = next_ref[r] - step_mean
        squares = jnp.where(row == r, jnp.sum(residue * residue), squares)
        slopes.append(terms[2, r] * residue)
    squares_ref[...] = squares
    own_slopes = jnp.where(first, cfg_scale, 1.0 - cfg_scale) * jnp.concatenate(slopes, axis=1)
    half = own_slopes.shape[0] // 2
    low, high = own_slopes[:half], own_slopes[half:]
    ordered = jnp.concatenate([jnp.where(first, low, high), jnp.where(first, high, low)], axis=0)
    copy.wait()
    partial = jnp.dot(
        ordered.astype(jnp.bfloat16), hidden_ref[...], preferred_element_type=jnp.float32
    )
    width = keep_ref.shape[2]
    for n in range(keep_ref.shape[0]):
        cols = slice(n * width, (n + 1) * width)
        keep_ref[n] = partial[:half, cols]
        send_ref[n] = partial[half:, cols]


def step(place, terms, own, partner, latent, next_latent, hidden, data_count):
    rows, width_all = hidden.shape
    cut = (data_count, C // 2, width_all // data_count)
    smem = pl.BlockSpec(memory_space=pltpu.SMEM)
    vmem = pl.BlockSpec(memory_space=pltpu.VMEM)
    return pl.pallas_call(
        step_kernel,
        in_specs=[smem] * 2 + [vmem] * 4 + [pl.BlockSpec(memory_space=pl.ANY)],
        out_specs=[vmem] * 3,
        scratch_shapes=[pltpu.VMEM(hidden.shape, jnp.bfloat16), pltpu.SemaphoreType.DMA],
        out_shape=[
            jax.ShapeDtypeStruct(cut, jnp.float32),
            jax.ShapeDtypeStruct(cut, jnp.float32),
            jax.ShapeDtypeStruct((8, 128), jnp.float32),
        ],
        compiler_params=pltpu.CompilerParams(vmem_limit_bytes=VMEM_BYTES),
        cost_estimate=pl.CostEstimate(
            flops=2 * rows * C * width_all, bytes_accessed=2 * rows * width_all, transcendentals=0
        ),
        name="step",
    )(place, terms, own, partner, latent, next_latent, hidden)


def fold_kernel(parts_ref, squares_ref, out_ref):
    count, width = parts_ref.shape[1], parts_ref.shape[2]
    out_ref[0:count, :] = jnp.sum(parts_ref[...], axis=0)
    out_ref[count : count + 8, 128:width] = jnp.zeros((8, width - 128), jnp.float32)
    out_ref[count : count + 8, 0:128] = squares_ref[...]


def fold(parts, squares):
    _, count, width = parts.shape
    vmem = pl.BlockSpec(memory_space=pltpu.VMEM)
    return pl.pallas_call(
        fold_kernel,
        in_specs=[vmem] * 2,
        out_specs=vmem,
        out_shape=jax.ShapeDtypeStruct((count + 8, width), jnp.float32),
        name="fold",
    )(parts, squares)


def exchange(send):
    return lax.all_to_all(send, "seq", split_axis=0, concat_axis=0, tiled=True)


def per_device(
    image_projections,
    text_projections,
    output_weight,
    image_state,
    modulation,
    final_weight,
    latent,
    next_latent,
    timestep,
    rewards,
    group_index,
):
    seq_count = lax.axis_size("seq")
    data_count = lax.axis_size("dp")
    per_dev = image_projections.shape[1]
    image_count = image_projections.shape[2]
    width_all = image_state.shape[3]
    rollouts = per_dev * data_count
    seq_at, dp_at, c_at = lax.axis_index("seq"), lax.axis_index("dp"), lax.axis_index("cfg")
    x_at, zh_at, y_at = seq_at // ZH, seq_at % ZH, dp_at // ZL
    place = jnp.stack([x_at, zh_at, y_at, c_at]).astype(jnp.int32)

    kv_rows = image_count + text_projections.shape[2]

    group_count = rollouts // GROUP_SIZE
    member = (group_index[:, None] == jnp.arange(group_count, dtype=jnp.int32)[None, :]).astype(
        jnp.float32
    )
    column = jnp.concatenate([from_column(output_weight, d) for d in range(ZH)], axis=0)
    totals = jnp.sum(member * rewards[:, None], axis=0)
    first_part = exchange(after(pack(image_projections, text_projections), column))
    totals = ring_sum(totals, from_y)
    column = after(column, totals)
    x_parts = [from_x(column, d) for d in range(1, X)]
    first_half = jnp.concatenate([column, x_parts[0]], axis=0)
    second_half = jnp.concatenate(x_parts[1:], axis=0)
    ahead_first, behind_second = from_y(first_half, 1), from_y(second_half, -1)
    ahead_second, behind_first = from_y(second_half, 1), from_y(first_half, -1)
    plane_other = [from_cfg(first_half), from_cfg(second_half)]
    second_part = exchange(
        after(
            pack_queries(image_projections, 1),
            first_part,
            ahead_first,
            behind_second,
            *plane_other,
        )
    )
    far_first, far_second = from_y(ahead_first, 1), from_y(behind_second, -1)
    moved = [ahead_first, ahead_second, behind_first, behind_second, far_first, far_second]
    pieces = [first_half, second_half] + moved + plane_other + [from_cfg(piece) for piece in moved]

    queries_at = per_dev * 2 * kv_rows // image_count
    first_part = after(first_part, ahead_second, behind_first)
    attended = attention(first_part, queries_at, first_part, 0, image_count, kv_rows, per_dev)
    all_totals = totals + from_zl(after(totals, attended))
    advantage = rewards - jnp.sum(member * all_totals[None, :], axis=1) / GROUP_SIZE
    attended = attention(
        second_part, 0, first_part, 1, image_count, kv_rows, per_dev, (attended,)
    )
    spread = noise_level * jnp.sqrt(timestep / (1.0 - timestep))
    drift_gain = 1.0 + spread * spread * (1.0 - timestep) / (2.0 * timestep)
    deviation = spread * math.sqrt(step_width)
    terms = jnp.stack(
        [
            1.0 - spread * spread / (2.0 * timestep) * step_width,
            drift_gain * step_width,
            advantage / (rollouts * C) * drift_gain * step_width / (deviation * deviation),
        ]
    )

    returned = after(exchange(after(attended, far_first, far_second, all_totals)), terms)
    hidden, velocity = hidden_rows(
        place, returned, image_state, modulation[0].transpose(1, 0, 2), final_weight.T, pieces
    )
    keep, send, squares = step(
        place,
        terms,
        velocity,
        from_cfg(velocity),
        latent.transpose(0, 2, 1),
        next_latent.transpose(0, 2, 1),
        hidden,
        data_count,
    )

    kept = keep + from_cfg(send)
    share = fold(lax.all_to_all(kept, "dp", split_axis=0, concat_axis=0, tiled=True), squares)
    share = ring_sum(ring_sum(share, from_zh), from_x)
    other = from_cfg(share)
    first = c_at == 0
    half = C // 2
    gradient = jnp.concatenate(
        [jnp.where(first, share, other)[:half], jnp.where(first, other, share)[:half]], axis=0
    ).T
    square_mean = share[half : half + per_dev, 0] / (seq_count * image_count * C)
    log_prob = (
        -square_mean / (2.0 * deviation * deviation)
        - jnp.log(deviation)
        - 0.5 * math.log(2.0 * math.pi)
    )
    return (gradient, log_prob)


def solution(mesh):
    in_specs = (
        P("cfg", "dp", "seq", None),
        P("cfg", "dp", "seq", None),
        P("seq", "dp"),
        P("cfg", "dp", "seq", None),
        P("cfg", "dp", None, None),
        P(),
        P("dp", "seq", None),
        P("dp", "seq", None),
        P("dp"),
        P("dp"),
        P("dp"),
    )
    out_specs = (P("dp", None), P("dp"))
    return jax.shard_map(
        per_device, mesh=mesh, in_specs=in_specs, out_specs=out_specs, check_vma=False
    )
```

```python
import functools
import math

import jax
import jax.numpy as jnp
from jax import lax
from jax.experimental import pallas as pl
from jax.experimental.pallas import tpu as pltpu
from jax.sharding import PartitionSpec as P

C = 64
HD = 128
GROUP_SIZE = 2

cfg_scale = 4.5
noise_level = 0.7
step_width = 0.02
norm_eps = 1e-06

X, ZH, Y, ZL = 4, 4, 4, 2
VMEM_BYTES = 32 * 1024 * 1024
HIDDEN_VMEM_BYTES = 50 * 1024 * 1024
FULL_VMEM_BYTES = 61 * 1024 * 1024


def from_x(value, d):
    pairs = [(((x + d) % X) * ZH + z, x * ZH + z) for x in range(X) for z in range(ZH)]
    return lax.ppermute(value, "seq", pairs)


def from_column(value, d):
    def at(core, x, z, y, zl):
        return ((core * X + x) * ZH + z) * (Y * ZL) + y * ZL + zl

    pairs = [
        (at(core if zl == core else 1 - core, x, (z + d) % ZH, y, core), at(core, x, z, y, zl))
        for core in range(2)
        for x in range(X)
        for z in range(ZH)
        for y in range(Y)
        for zl in range(ZL)
    ]
    return lax.ppermute(value, ("cfg", "seq", "dp"), pairs)


def from_zh(value, d):
    pairs = [(x * ZH + (z + d) % ZH, x * ZH + z) for x in range(X) for z in range(ZH)]
    return lax.ppermute(value, "seq", pairs)


def from_y(value, d):
    pairs = [(((y + d) % Y) * ZL + z, y * ZL + z) for y in range(Y) for z in range(ZL)]
    return lax.ppermute(value, "dp", pairs)


def from_zl(value):
    pairs = [(y * ZL + 1 - z, y * ZL + z) for y in range(Y) for z in range(ZL)]
    return lax.ppermute(value, "dp", pairs)


def from_cfg(value):
    return lax.ppermute(value, "cfg", [(0, 1), (1, 0)])


def after(value, *others):
    return lax.optimization_barrier((value,) + others)[0]


def ring_sum(value, fetch):
    first, second, third = (fetch(value, d) for d in (1, 2, 3))
    return (value + second) + (first + third)


def pack_kernel(k_ref, v_ref, kt_ref, vt_ref, q_ref, out_ref):
    rows, text = k_ref.shape[2], kt_ref.shape[2]
    for h in range(out_ref.shape[0]):
        cols = slice(h * HD, (h + 1) * HD)
        at = 0
        for r in range(k_ref.shape[1]):
            for ref, count in ((k_ref, rows), (kt_ref, text), (v_ref, rows), (vt_ref, text)):
                out_ref[h, at : at + count, :] = ref[0, r, :, cols]
                at += count
        out_ref[h, at : at + rows, :] = q_ref[0, 0, :, cols]


def pack_queries_kernel(q_ref, out_ref):
    for h in range(out_ref.shape[0]):
        out_ref[h] = q_ref[0, 0, :, h * HD : (h + 1) * HD]


def pack(image_projections, text_projections):
    _, per_dev, rows, width = image_projections.shape
    text = text_projections.shape[2]
    heads = width // (3 * HD)
    per = 4
    steps = heads // per
    total = per_dev * 2 * (rows + text) + rows

    def spec(rollouts, count, part):
        return pl.BlockSpec((1, rollouts, count, per * HD), lambda h: (0, 0, 0, part * steps + h))

    return pl.pallas_call(
        pack_kernel,
        grid=(steps,),
        in_specs=[
            spec(per_dev, rows, 1),
            spec(per_dev, rows, 2),
            spec(per_dev, text, 0),
            spec(per_dev, text, 1),
            spec(1, rows, 0),
        ],
        out_specs=pl.BlockSpec((per, total, HD), lambda h: (h, 0, 0)),
        out_shape=jax.ShapeDtypeStruct((heads, total, HD), jnp.bfloat16),
        compiler_params=pltpu.CompilerParams(vmem_limit_bytes=FULL_VMEM_BYTES),
        cost_estimate=pl.CostEstimate(
            flops=0, bytes_accessed=2 * heads * total * HD * 2, transcendentals=0
        ),
        name="pack",
    )(image_projections, image_projections, text_projections, text_projections, image_projections)


def pack_queries(image_projections, r):
    _, _, rows, width = image_projections.shape
    heads = width // (3 * HD)
    return pl.pallas_call(
        pack_queries_kernel,
        grid=(1,),
        in_specs=[pl.BlockSpec((1, 1, rows, heads * HD), lambda i: (0, r, 0, 0))],
        out_specs=pl.BlockSpec((heads, rows, HD), lambda i: (0, 0, 0)),
        out_shape=jax.ShapeDtypeStruct((heads, rows, HD), jnp.bfloat16),
        compiler_params=pltpu.CompilerParams(vmem_limit_bytes=VMEM_BYTES),
        cost_estimate=pl.CostEstimate(
            flops=0, bytes_accessed=2 * heads * rows * HD * 2, transcendentals=0
        ),
        name="pack_queries",
    )(image_projections)


def attention_kernel(q_ref, kv_ref, *rest):
    out_ref, keys, values = rest[-3:]
    peers, kv_rows = kv_ref.shape[0], kv_ref.shape[1] // 2
    ones = jnp.ones((kv_rows, HD), jnp.bfloat16)
    for s in range(peers):
        at = slice(s * kv_rows, (s + 1) * kv_rows)
        keys[at, :] = kv_ref[s, 0:kv_rows, :]
        values[at, 0:HD] = kv_ref[s, kv_rows : 2 * kv_rows, :]
        values[at, HD : 2 * HD] = ones

    factor = math.log2(math.e) / math.sqrt(HD)
    for n in range(peers):
        scores = lax.dot_general(
            q_ref[n], keys[...], (((1,), (1,)), ((), ())), preferred_element_type=jnp.float32
        )
        highest = jnp.max(scores, axis=1, keepdims=True)
        powered = jnp.exp2((scores - highest) * factor).astype(jnp.bfloat16)
        sums = jnp.dot(powered, values[...], preferred_element_type=jnp.float32)
        out_ref[n] = (sums[:, 0:HD] / sums[:, HD : HD + 1]).astype(jnp.bfloat16)


def attention(queries, q_at, key_values, r, rows, kv_rows, per_dev, earlier=()):
    peers = queries.shape[0]
    return pl.pallas_call(
        attention_kernel,
        grid=(1,),
        in_specs=[
            pl.BlockSpec((peers, rows, HD), lambda i: (0, q_at, 0)),
            pl.BlockSpec((peers, 2 * kv_rows, HD), lambda i: (0, r, 0)),
        ]
        + [pl.BlockSpec(memory_space=pl.ANY)] * len(earlier),
        out_specs=pl.BlockSpec((peers, rows, HD), lambda i: (0, r, 0)),
        out_shape=jax.ShapeDtypeStruct((peers, per_dev * rows, HD), jnp.bfloat16),
        scratch_shapes=[
            pltpu.VMEM((peers * kv_rows, HD), jnp.bfloat16),
            pltpu.VMEM((peers * kv_rows, 2 * HD), jnp.bfloat16),
        ],
        input_output_aliases={2: 0} if earlier else {},
        compiler_params=pltpu.CompilerParams(vmem_limit_bytes=FULL_VMEM_BYTES),
        cost_estimate=pl.CostEstimate(
            flops=8 * peers * rows * peers * kv_rows * HD,
            bytes_accessed=2 * peers * (2 * rows + 2 * kv_rows) * HD,
            transcendentals=peers * rows * peers * kv_rows,
        ),
        name=f"attention{r}",
    )(queries, key_values, *earlier)


SPANS = ((0, 0), (0, 2), (1, 0), (1, 2), (3, 0), (3, 2), (2, 0), (2, 2))


def hidden_kernel(place, heads_ref, state_any, mods_any, final_any, *rest):
    pieces = rest[: 2 * len(SPANS)]
    hidden_ref, velocity_ref, flat, mixed, weights, state_ref, mods_ref, final_ref, sems = rest[
        2 * len(SPANS) :
    ]
    x_at, zh_at, y_at, c_at = place[0], place[1], place[2], place[3]
    per_dev, rows = state_ref.shape[1], state_ref.shape[2]
    width = weights.shape[2]
    part = weights.shape[1] // X

    def begin(source, target, n):
        copy = pltpu.make_async_copy(source, target, sems.at[n])
        copy.start()
        return copy

    copies = []
    for n, piece in enumerate(pieces):
        core, (turn, first) = n // len(SPANS), SPANS[n % len(SPANS)]
        target = weights.at[core * Y + turn, pl.ds(first * part, piece.shape[0])]
        copies.append(begin(piece, target, n))
        if n == 1:
            mods_copy = begin(mods_any, mods_ref, len(pieces))
            state_copy = begin(state_any, state_ref, len(pieces) + 1)
    final_copy = begin(final_any, final_ref, len(pieces) + 2)
    for i in range(X):
        for j in range(ZH):
            head = lax.rem(x_at + i, X) * ZH + lax.rem(zh_at + j, ZH)
            k = i * ZH + j
            flat[:, k * HD : (k + 1) * HD] = heads_ref[head]
    row_sum = jnp.zeros((per_dev * rows, 1), jnp.float32)
    square_sum = jnp.zeros((per_dev * rows, 1), jnp.float32)
    for core in range(2):
        core_at = c_at if core == 0 else 1 - c_at
        for turn in (0, 1, 3, 2):
            for n, (of_turn, _) in enumerate(SPANS):
                if of_turn == turn:
                    copies[core * len(SPANS) + n].wait()
            at = pl.ds(pl.multiple_of((lax.rem(y_at + turn, Y) * ZL + core_at) * width, 128), width)
            projected = jnp.dot(
                flat[...], weights[core * Y + turn], preferred_element_type=jnp.float32
            )
            if core == 0 and turn == 0:
                mods_copy.wait()
                state_copy.wait()
            for r in range(per_dev):
                gate = mods_ref[0, r : r + 1, at].astype(jnp.float32)
                mixed[r * rows : (r + 1) * rows, at] = (
                    state_ref[0, r, :, at].astype(jnp.float32)
                    + gate * projected[r * rows : (r + 1) * rows]
                )
            block = mixed[:, at]
            row_sum = row_sum + jnp.sum(block, axis=1, keepdims=True)
            square_sum = square_sum + jnp.sum(block * block, axis=1, keepdims=True)
    width_all = mixed.shape[1]
    center = row_sum / width_all
    square = square_sum / width_all
    inverse = lax.rsqrt(square - center * center + norm_eps)
    for r in range(per_dev):
        at = slice(r * rows, (r + 1) * rows)
        scale = 1.0 + mods_ref[2, r : r + 1, :].astype(jnp.float32)
        shift = mods_ref[1, r : r + 1, :].astype(jnp.float32)
        hidden_ref[at, :] = (
            (mixed[at, :] - center[at]) * inverse[at] * scale + shift
        ).astype(jnp.bfloat16)
    final_copy.wait()
    velocity_ref[...] = lax.dot_general(
        final_ref[...], hidden_ref[...], (((1,), (1,)), ((), ())), preferred_element_type=jnp.float32
    )


def hidden_rows(place, heads_part, image_state, modulation, final_weight, pieces):
    heads, all_rows, _ = heads_part.shape
    width_all = image_state.shape[3]
    vmem = pl.BlockSpec(memory_space=pltpu.VMEM)
    return pl.pallas_call(
        hidden_kernel,
        in_specs=[pl.BlockSpec(memory_space=pltpu.SMEM)]
        + [vmem]
        + [pl.BlockSpec(memory_space=pl.ANY)] * (3 + len(pieces)),
        out_specs=[vmem] * 2,
        out_shape=[
            jax.ShapeDtypeStruct((all_rows, width_all), jnp.bfloat16),
            jax.ShapeDtypeStruct((C, all_rows), jnp.float32),
        ],
        scratch_shapes=[
            pltpu.VMEM((all_rows, heads * HD), jnp.bfloat16),
            pltpu.VMEM((all_rows, width_all), jnp.float32),
            pltpu.VMEM((8, heads * HD, pieces[0].shape[1]), jnp.bfloat16),
            pltpu.VMEM(image_state.shape, jnp.bfloat16),
            pltpu.VMEM(modulation.shape, jnp.bfloat16),
            pltpu.VMEM(final_weight.shape, jnp.bfloat16),
            pltpu.SemaphoreType.DMA((len(pieces) + 3,)),
        ],
        compiler_params=pltpu.CompilerParams(vmem_limit_bytes=HIDDEN_VMEM_BYTES),
        cost_estimate=pl.CostEstimate(
            flops=2 * all_rows * heads * HD * width_all,
            bytes_accessed=2 * heads * HD * width_all,
            transcendentals=0,
        ),
        name="hidden",
    )(place, heads_part, image_state, modulation, final_weight, *pieces)


def step_kernel(
    place,
    terms,
    own_ref,
    partner_ref,
    latent_ref,
    next_ref,
    hidden_any,
    keep_ref,
    send_ref,
    squares_ref,
    hidden_ref,
    sem,
):
    copy = pltpu.make_async_copy(hidden_any, hidden_ref, sem)
    copy.start()
    first = place[3] == 0
    own, partner = own_ref[...], partner_ref[...]
    conditional = jnp.where(first, own, partner)
    unconditional = jnp.where(first, partner, own)
    guided = unconditional + cfg_scale * (conditional - unconditional)
    per_dev, _, rows = latent_ref.shape
    row = lax.broadcasted_iota(jnp.int32, squares_ref.shape, 0)
    squares = jnp.zeros(squares_ref.shape, jnp.float32)
    slopes = []
    for r in range(per_dev):
        step_mean = (
            latent_ref[r] * terms[0, r] - guided[:, r * rows : (r + 1) * rows] * terms[1, r]
        )
        residue = next_ref[r] - step_mean
        squares = jnp.where(row == r, jnp.sum(residue * residue), squares)
        slopes.append(terms[2, r] * residue)
    squares_ref[...] = squares
    own_slopes = jnp.where(first, cfg_scale, 1.0 - cfg_scale) * jnp.concatenate(slopes, axis=1)
    half = own_slopes.shape[0] // 2
    low, high = own_slopes[:half], own_slopes[half:]
    ordered = jnp.concatenate([jnp.where(first, low, high), jnp.where(first, high, low)], axis=0)
    copy.wait()
    partial = jnp.dot(
        ordered.astype(jnp.bfloat16), hidden_ref[...], preferred_element_type=jnp.float32
    )
    width = keep_ref.shape[2]
    for n in range(keep_ref.shape[0]):
        cols = slice(n * width, (n + 1) * width)
        keep_ref[n] = partial[:half, cols]
        send_ref[n] = partial[half:, cols]


def step(place, terms, own, partner, latent, next_latent, hidden, data_count):
    rows, width_all = hidden.shape
    cut = (data_count, C // 2, width_all // data_count)
    smem = pl.BlockSpec(memory_space=pltpu.SMEM)
    vmem = pl.BlockSpec(memory_space=pltpu.VMEM)
    return pl.pallas_call(
        step_kernel,
        in_specs=[smem] * 2 + [vmem] * 4 + [pl.BlockSpec(memory_space=pl.ANY)],
        out_specs=[vmem] * 3,
        scratch_shapes=[pltpu.VMEM(hidden.shape, jnp.bfloat16), pltpu.SemaphoreType.DMA],
        out_shape=[
            jax.ShapeDtypeStruct(cut, jnp.float32),
            jax.ShapeDtypeStruct(cut, jnp.float32),
            jax.ShapeDtypeStruct((8, 128), jnp.float32),
        ],
        compiler_params=pltpu.CompilerParams(vmem_limit_bytes=FULL_VMEM_BYTES),
        cost_estimate=pl.CostEstimate(
            flops=2 * rows * C * width_all, bytes_accessed=2 * rows * width_all, transcendentals=0
        ),
        name="step",
    )(place, terms, own, partner, latent, next_latent, hidden)


def fold_kernel(parts_ref, squares_ref, out_ref):
    count, width = parts_ref.shape[1], parts_ref.shape[2]
    out_ref[0:count, :] = jnp.sum(parts_ref[...], axis=0)
    out_ref[count : count + 8, 128:width] = jnp.zeros((8, width - 128), jnp.float32)
    out_ref[count : count + 8, 0:128] = squares_ref[...]


def fold(parts, squares):
    _, count, width = parts.shape
    vmem = pl.BlockSpec(memory_space=pltpu.VMEM)
    return pl.pallas_call(
        fold_kernel,
        in_specs=[vmem] * 2,
        out_specs=vmem,
        out_shape=jax.ShapeDtypeStruct((count + 8, width), jnp.float32),
        name="fold",
    )(parts, squares)


def exchange(send):
    return lax.all_to_all(send, "seq", split_axis=0, concat_axis=0, tiled=True)


def per_device(
    image_projections,
    text_projections,
    output_weight,
    image_state,
    modulation,
    final_weight,
    latent,
    next_latent,
    timestep,
    rewards,
    group_index,
):
    seq_count = lax.axis_size("seq")
    data_count = lax.axis_size("dp")
    per_dev = image_projections.shape[1]
    image_count = image_projections.shape[2]
    width_all = image_state.shape[3]
    rollouts = per_dev * data_count
    seq_at, dp_at, c_at = lax.axis_index("seq"), lax.axis_index("dp"), lax.axis_index("cfg")
    x_at, zh_at, y_at = seq_at // ZH, seq_at % ZH, dp_at // ZL
    place = jnp.stack([x_at, zh_at, y_at, c_at]).astype(jnp.int32)

    kv_rows = image_count + text_projections.shape[2]

    group_count = rollouts // GROUP_SIZE
    member = (group_index[:, None] == jnp.arange(group_count, dtype=jnp.int32)[None, :]).astype(
        jnp.float32
    )
    column = jnp.concatenate([from_column(output_weight, d) for d in range(ZH)], axis=0)
    totals = jnp.sum(member * rewards[:, None], axis=0)
    totals = totals + from_zl(totals)
    first_part = exchange(after(pack(image_projections, text_projections), column, totals))
    totals = ring_sum(totals, from_y)
    advantage = rewards - jnp.sum(member * totals[None, :], axis=1) / GROUP_SIZE
    column = after(column, totals)
    x_parts = [from_x(column, d) for d in range(1, X)]
    first_half = jnp.concatenate([column, x_parts[0]], axis=0)
    second_half = jnp.concatenate(x_parts[1:], axis=0)
    ahead_first, behind_second = from_y(first_half, 1), from_y(second_half, -1)
    ahead_second, behind_first = from_y(second_half, 1), from_y(first_half, -1)
    plane_other = [from_cfg(first_half), from_cfg(second_half)]
    second_part = exchange(
        after(
            pack_queries(image_projections, 1),
            first_part,
            ahead_first,
            behind_second,
            *plane_other,
        )
    )
    far_first, far_second = from_y(ahead_first, 1), from_y(behind_second, -1)
    moved = [ahead_first, ahead_second, behind_first, behind_second, far_first, far_second]
    pieces = [first_half, second_half] + moved + plane_other + [from_cfg(piece) for piece in moved]

    queries_at = per_dev * 2 * kv_rows // image_count
    first_part = after(first_part, ahead_second, behind_first)
    attended = attention(first_part, queries_at, first_part, 0, image_count, kv_rows, per_dev)
    attended = attention(
        second_part, 0, first_part, 1, image_count, kv_rows, per_dev, (attended,)
    )
    spread = noise_level * jnp.sqrt(timestep / (1.0 - timestep))
    drift_gain = 1.0 + spread * spread * (1.0 - timestep) / (2.0 * timestep)
    deviation = spread * math.sqrt(step_width)
    terms = jnp.stack(
        [
            1.0 - spread * spread / (2.0 * timestep) * step_width,
            drift_gain * step_width,
            advantage / (rollouts * C) * drift_gain * step_width / (deviation * deviation),
        ]
    )

    returned = after(exchange(attended), terms)
    hidden, velocity = hidden_rows(
        place, returned, image_state, modulation[0].transpose(1, 0, 2), final_weight.T, pieces
    )
    keep, send, squares = step(
        place,
        terms,
        velocity,
        from_cfg(velocity),
        latent.transpose(0, 2, 1),
        next_latent.transpose(0, 2, 1),
        hidden,
        data_count,
    )

    kept = keep + from_cfg(send)
    share = fold(lax.all_to_all(kept, "dp", split_axis=0, concat_axis=0, tiled=True), squares)
    share = ring_sum(ring_sum(share, from_zh), from_x)
    other = from_cfg(share)
    first = c_at == 0
    half = C // 2
    gradient = jnp.concatenate(
        [jnp.where(first, share, other)[:half], jnp.where(first, other, share)[:half]], axis=0
    ).T
    square_mean = share[half : half + per_dev, 0] / (seq_count * image_count * C)
    log_prob = (
        -square_mean / (2.0 * deviation * deviation)
        - jnp.log(deviation)
        - 0.5 * math.log(2.0 * math.pi)
    )
    return (gradient, log_prob)


def solution(mesh):
    in_specs = (
        P("cfg", "dp", "seq", None),
        P("cfg", "dp", "seq", None),
        P("seq", "dp"),
        P("cfg", "dp", "seq", None),
        P("cfg", "dp", None, None),
        P(),
        P("dp", "seq", None),
        P("dp", "seq", None),
        P("dp"),
        P("dp"),
        P("dp"),
    )
    out_specs = (P("dp", None), P("dp"))
    return jax.shard_map(
        per_device, mesh=mesh, in_specs=in_specs, out_specs=out_specs, check_vma=False
    )
```

```python
import functools
import math

import jax
import jax.numpy as jnp
from jax import lax
from jax.experimental import pallas as pl
from jax.experimental.pallas import tpu as pltpu
from jax.sharding import PartitionSpec as P

C = 64
HD = 128
GROUP_SIZE = 2

cfg_scale = 4.5
noise_level = 0.7
step_width = 0.02
norm_eps = 1e-06

X, ZH, Y, ZL = 4, 4, 4, 2
VMEM_BYTES = 32 * 1024 * 1024
HIDDEN_VMEM_BYTES = 50 * 1024 * 1024
ATTENTION_STEPS = 4
FULL_VMEM_BYTES = 61 * 1024 * 1024


def from_x(value, d):
    pairs = [(((x + d) % X) * ZH + z, x * ZH + z) for x in range(X) for z in range(ZH)]
    return lax.ppermute(value, "seq", pairs)


def from_column(value, d):
    def at(core, x, z, y, zl):
        return ((core * X + x) * ZH + z) * (Y * ZL) + y * ZL + zl

    pairs = [
        (at(core if zl == core else 1 - core, x, (z + d) % ZH, y, core), at(core, x, z, y, zl))
        for core in range(2)
        for x in range(X)
        for z in range(ZH)
        for y in range(Y)
        for zl in range(ZL)
    ]
    return lax.ppermute(value, ("cfg", "seq", "dp"), pairs)


def from_zh(value, d):
    pairs = [(x * ZH + (z + d) % ZH, x * ZH + z) for x in range(X) for z in range(ZH)]
    return lax.ppermute(value, "seq", pairs)


def from_y(value, d):
    pairs = [(((y + d) % Y) * ZL + z, y * ZL + z) for y in range(Y) for z in range(ZL)]
    return lax.ppermute(value, "dp", pairs)


def from_zl(value):
    pairs = [(y * ZL + 1 - z, y * ZL + z) for y in range(Y) for z in range(ZL)]
    return lax.ppermute(value, "dp", pairs)


def from_cfg(value):
    return lax.ppermute(value, "cfg", [(0, 1), (1, 0)])


def after(value, *others):
    return lax.optimization_barrier((value,) + others)[0]


def ring_sum(value, fetch):
    first, second, third = (fetch(value, d) for d in (1, 2, 3))
    return (value + second) + (first + third)


def pack_kernel(k_ref, v_ref, kt_ref, vt_ref, q_ref, out_ref):
    rows, text = k_ref.shape[2], kt_ref.shape[2]

    def pack_head(h, carry):
        cols = pl.ds(pl.multiple_of(h * HD, HD), HD)
        at = 0
        for r in range(k_ref.shape[1]):
            for ref, count in ((k_ref, rows), (kt_ref, text), (v_ref, rows), (vt_ref, text)):
                out_ref[h, at : at + count, :] = ref[0, r, :, cols]
                at += count
        out_ref[h, at : at + rows, :] = q_ref[0, 0, :, cols]
        return carry

    lax.fori_loop(0, out_ref.shape[0], pack_head, 0)


def pack_queries_kernel(q_ref, out_ref):
    def pack_head(h, carry):
        out_ref[h] = q_ref[0, 0, :, pl.ds(pl.multiple_of(h * HD, HD), HD)]
        return carry

    lax.fori_loop(0, out_ref.shape[0], pack_head, 0)


def pack(image_projections, text_projections):
    _, per_dev, rows, width = image_projections.shape
    text = text_projections.shape[2]
    heads = width // (3 * HD)
    per = 4
    steps = heads // per
    total = per_dev * 2 * (rows + text) + rows

    def spec(rollouts, count, part):
        return pl.BlockSpec((1, rollouts, count, per * HD), lambda h: (0, 0, 0, part * steps + h))

    return pl.pallas_call(
        pack_kernel,
        grid=(steps,),
        in_specs=[
            spec(per_dev, rows, 1),
            spec(per_dev, rows, 2),
            spec(per_dev, text, 0),
            spec(per_dev, text, 1),
            spec(1, rows, 0),
        ],
        out_specs=pl.BlockSpec((per, total, HD), lambda h: (h, 0, 0)),
        out_shape=jax.ShapeDtypeStruct((heads, total, HD), jnp.bfloat16),
        compiler_params=pltpu.CompilerParams(vmem_limit_bytes=FULL_VMEM_BYTES),
        cost_estimate=pl.CostEstimate(
            flops=0, bytes_accessed=2 * heads * total * HD * 2, transcendentals=0
        ),
        name="pack",
    )(image_projections, image_projections, text_projections, text_projections, image_projections)


def pack_queries(image_projections, r):
    _, _, rows, width = image_projections.shape
    heads = width // (3 * HD)
    return pl.pallas_call(
        pack_queries_kernel,
        grid=(1,),
        in_specs=[pl.BlockSpec((1, 1, rows, heads * HD), lambda i: (0, r, 0, 0))],
        out_specs=pl.BlockSpec((heads, rows, HD), lambda i: (0, 0, 0)),
        out_shape=jax.ShapeDtypeStruct((heads, rows, HD), jnp.bfloat16),
        compiler_params=pltpu.CompilerParams(vmem_limit_bytes=VMEM_BYTES),
        cost_estimate=pl.CostEstimate(
            flops=0, bytes_accessed=2 * heads * rows * HD * 2, transcendentals=0
        ),
        name="pack_queries",
    )(image_projections)


def attention_kernel(q_ref, kv_ref, *rest):
    out_ref, keys, values = rest[-3:]
    peers, kv_rows = kv_ref.shape[0], kv_ref.shape[1] // 2

    @pl.when(pl.program_id(0) == 0)
    def _():
        ones = jnp.ones((kv_rows, HD), jnp.bfloat16)

        def place_peer(s, carry):
            at = pl.ds(pl.multiple_of(s * kv_rows, kv_rows), kv_rows)
            keys[at, :] = kv_ref[s, 0:kv_rows, :]
            values[at, 0:HD] = kv_ref[s, kv_rows : 2 * kv_rows, :]
            values[at, HD : 2 * HD] = ones
            return carry

        lax.fori_loop(0, peers, place_peer, 0)

    factor = math.log2(math.e) / math.sqrt(HD)
    for n in range(q_ref.shape[0]):
        scores = lax.dot_general(
            q_ref[n], keys[...], (((1,), (1,)), ((), ())), preferred_element_type=jnp.float32
        )
        highest = jnp.max(scores, axis=1, keepdims=True)
        powered = jnp.exp2((scores - highest) * factor).astype(jnp.bfloat16)
        sums = jnp.dot(powered, values[...], preferred_element_type=jnp.float32)
        out_ref[n] = (sums[:, 0:HD] / sums[:, HD : HD + 1]).astype(jnp.bfloat16)


def attention(queries, q_at, key_values, r, rows, kv_rows, per_dev, earlier=()):
    peers = queries.shape[0]
    return pl.pallas_call(
        attention_kernel,
        grid=(ATTENTION_STEPS,),
        in_specs=[
            pl.BlockSpec((peers // ATTENTION_STEPS, rows, HD), lambda i: (i, q_at, 0)),
            pl.BlockSpec((peers, 2 * kv_rows, HD), lambda i: (0, r, 0)),
        ]
        + [pl.BlockSpec(memory_space=pl.ANY)] * len(earlier),
        out_specs=pl.BlockSpec((peers // ATTENTION_STEPS, rows, HD), lambda i: (i, r, 0)),
        out_shape=jax.ShapeDtypeStruct((peers, per_dev * rows, HD), jnp.bfloat16),
        scratch_shapes=[
            pltpu.VMEM((peers * kv_rows, HD), jnp.bfloat16),
            pltpu.VMEM((peers * kv_rows, 2 * HD), jnp.bfloat16),
        ],
        input_output_aliases={2: 0} if earlier else {},
        compiler_params=pltpu.CompilerParams(vmem_limit_bytes=FULL_VMEM_BYTES),
        cost_estimate=pl.CostEstimate(
            flops=8 * peers * rows * peers * kv_rows * HD,
            bytes_accessed=2 * peers * (2 * rows + 2 * kv_rows) * HD,
            transcendentals=peers * rows * peers * kv_rows,
        ),
        name=f"attention{r}",
    )(queries, key_values, *earlier)


SPANS = ((0, 0), (0, 2), (1, 0), (1, 2), (3, 0), (3, 2), (2, 0), (2, 2))


def hidden_kernel(place, heads_ref, state_any, mods_any, final_any, *rest):
    pieces = rest[: 2 * len(SPANS)]
    hidden_ref, velocity_ref, flat, mixed, weights, state_ref, mods_ref, final_ref, sems = rest[
        2 * len(SPANS) :
    ]
    x_at, zh_at, y_at, c_at = place[0], place[1], place[2], place[3]
    per_dev, rows = state_ref.shape[1], state_ref.shape[2]
    width = weights.shape[2]
    part = weights.shape[1] // X

    def begin(source, target, n):
        copy = pltpu.make_async_copy(source, target, sems.at[n])
        copy.start()
        return copy

    copies = []
    for n, piece in enumerate(pieces):
        core, (turn, first) = n // len(SPANS), SPANS[n % len(SPANS)]
        target = weights.at[core * Y + turn, pl.ds(first * part, piece.shape[0])]
        copies.append(begin(piece, target, n))
        if n == 1:
            mods_copy = begin(mods_any, mods_ref, len(pieces))
            state_copy = begin(state_any, state_ref, len(pieces) + 1)
    final_copy = begin(final_any, final_ref, len(pieces) + 2)
    for i in range(X):
        for j in range(ZH):
            head = lax.rem(x_at + i, X) * ZH + lax.rem(zh_at + j, ZH)
            k = i * ZH + j
            flat[:, k * HD : (k + 1) * HD] = heads_ref[head]
    row_sum = jnp.zeros((per_dev * rows, 1), jnp.float32)
    square_sum = jnp.zeros((per_dev * rows, 1), jnp.float32)
    for core in range(2):
        core_at = c_at if core == 0 else 1 - c_at
        for turn in (0, 1, 3, 2):
            for n, (of_turn, _) in enumerate(SPANS):
                if of_turn == turn:
                    copies[core * len(SPANS) + n].wait()
            at = pl.ds(pl.multiple_of((lax.rem(y_at + turn, Y) * ZL + core_at) * width, 128), width)
            projected = jnp.dot(
                flat[...], weights[core * Y + turn], preferred_element_type=jnp.float32
            )
            if core == 0 and turn == 0:
                mods_copy.wait()
                state_copy.wait()
            for r in range(per_dev):
                gate = mods_ref[0, r : r + 1, at].astype(jnp.float32)
                mixed[r * rows : (r + 1) * rows, at] = (
                    state_ref[0, r, :, at].astype(jnp.float32)
                    + gate * projected[r * rows : (r + 1) * rows]
                )
            block = mixed[:, at]
            row_sum = row_sum + jnp.sum(block, axis=1, keepdims=True)
            square_sum = square_sum + jnp.sum(block * block, axis=1, keepdims=True)
    width_all = mixed.shape[1]
    center = row_sum / width_all
    square = square_sum / width_all
    inverse = lax.rsqrt(square - center * center + norm_eps)
    for r in range(per_dev):
        at = slice(r * rows, (r + 1) * rows)
        scale = 1.0 + mods_ref[2, r : r + 1, :].astype(jnp.float32)
        shift = mods_ref[1, r : r + 1, :].astype(jnp.float32)
        hidden_ref[at, :] = (
            (mixed[at, :] - center[at]) * inverse[at] * scale + shift
        ).astype(jnp.bfloat16)
    final_copy.wait()
    velocity_ref[...] = lax.dot_general(
        final_ref[...], hidden_ref[...], (((1,), (1,)), ((), ())), preferred_element_type=jnp.float32
    )


def hidden_rows(place, heads_part, image_state, modulation, final_weight, pieces):
    heads, all_rows, _ = heads_part.shape
    width_all = image_state.shape[3]
    vmem = pl.BlockSpec(memory_space=pltpu.VMEM)
    return pl.pallas_call(
        hidden_kernel,
        in_specs=[pl.BlockSpec(memory_space=pltpu.SMEM)]
        + [vmem]
        + [pl.BlockSpec(memory_space=pl.ANY)] * (3 + len(pieces)),
        out_specs=[vmem] * 2,
        out_shape=[
            jax.ShapeDtypeStruct((all_rows, width_all), jnp.bfloat16),
            jax.ShapeDtypeStruct((C, all_rows), jnp.float32),
        ],
        scratch_shapes=[
            pltpu.VMEM((all_rows, heads * HD), jnp.bfloat16),
            pltpu.VMEM((all_rows, width_all), jnp.float32),
            pltpu.VMEM((8, heads * HD, pieces[0].shape[1]), jnp.bfloat16),
            pltpu.VMEM(image_state.shape, jnp.bfloat16),
            pltpu.VMEM(modulation.shape, jnp.bfloat16),
            pltpu.VMEM(final_weight.shape, jnp.bfloat16),
            pltpu.SemaphoreType.DMA((len(pieces) + 3,)),
        ],
        compiler_params=pltpu.CompilerParams(vmem_limit_bytes=HIDDEN_VMEM_BYTES),
        cost_estimate=pl.CostEstimate(
            flops=2 * all_rows * heads * HD * width_all,
            bytes_accessed=2 * heads * HD * width_all,
            transcendentals=0,
        ),
        name="hidden",
    )(place, heads_part, image_state, modulation, final_weight, *pieces)


def step_kernel(
    place,
    terms,
    own_ref,
    partner_ref,
    latent_ref,
    next_ref,
    hidden_ref,
    keep_ref,
    send_ref,
    squares_ref,
):
    first = place[3] == 0
    own, partner = own_ref[...], partner_ref[...]
    conditional = jnp.where(first, own, partner)
    unconditional = jnp.where(first, partner, own)
    guided = unconditional + cfg_scale * (conditional - unconditional)
    per_dev, _, rows = latent_ref.shape
    row = lax.broadcasted_iota(jnp.int32, squares_ref.shape, 0)
    squares = jnp.zeros(squares_ref.shape, jnp.float32)
    slopes = []
    for r in range(per_dev):
        step_mean = (
            latent_ref[r] * terms[0, r] - guided[:, r * rows : (r + 1) * rows] * terms[1, r]
        )
        residue = next_ref[r] - step_mean
        squares = jnp.where(row == r, jnp.sum(residue * residue), squares)
        slopes.append(terms[2, r] * residue)
    squares_ref[...] = squares
    own_slopes = jnp.where(first, cfg_scale, 1.0 - cfg_scale) * jnp.concatenate(slopes, axis=1)
    half = own_slopes.shape[0] // 2
    low, high = own_slopes[:half], own_slopes[half:]
    ordered = jnp.concatenate([jnp.where(first, low, high), jnp.where(first, high, low)], axis=0)
    partial = jnp.dot(
        ordered.astype(jnp.bfloat16), hidden_ref[...], preferred_element_type=jnp.float32
    )
    width = keep_ref.shape[2]
    for n in range(keep_ref.shape[0]):
        cols = slice(n * width, (n + 1) * width)
        keep_ref[n] = partial[:half, cols]
        send_ref[n] = partial[half:, cols]


def step(place, terms, own, partner, latent, next_latent, hidden, data_count):
    rows, width_all = hidden.shape
    cut = (data_count, C // 2, width_all // data_count)
    smem = pl.BlockSpec(memory_space=pltpu.SMEM)
    vmem = pl.BlockSpec(memory_space=pltpu.VMEM)
    return pl.pallas_call(
        step_kernel,
        in_specs=[smem] * 2 + [vmem] * 5,
        out_specs=[vmem] * 3,
        out_shape=[
            jax.ShapeDtypeStruct(cut, jnp.float32),
            jax.ShapeDtypeStruct(cut, jnp.float32),
            jax.ShapeDtypeStruct((8, 128), jnp.float32),
        ],
        compiler_params=pltpu.CompilerParams(vmem_limit_bytes=VMEM_BYTES),
        cost_estimate=pl.CostEstimate(
            flops=2 * rows * C * width_all, bytes_accessed=2 * rows * width_all, transcendentals=0
        ),
        name="step",
    )(place, terms, own, partner, latent, next_latent, hidden)


def fold_kernel(parts_ref, squares_ref, out_ref):
    count, width = parts_ref.shape[1], parts_ref.shape[2]
    out_ref[0:count, :] = jnp.sum(parts_ref[...], axis=0)
    out_ref[count : count + 8, 128:width] = jnp.zeros((8, width - 128), jnp.float32)
    out_ref[count : count + 8, 0:128] = squares_ref[...]


def fold(parts, squares):
    _, count, width = parts.shape
    vmem = pl.BlockSpec(memory_space=pltpu.VMEM)
    return pl.pallas_call(
        fold_kernel,
        in_specs=[vmem] * 2,
        out_specs=vmem,
        out_shape=jax.ShapeDtypeStruct((count + 8, width), jnp.float32),
        name="fold",
    )(parts, squares)


def exchange(send):
    return lax.all_to_all(send, "seq", split_axis=0, concat_axis=0, tiled=True)


def per_device(
    image_projections,
    text_projections,
    output_weight,
    image_state,
    modulation,
    final_weight,
    latent,
    next_latent,
    timestep,
    rewards,
    group_index,
):
    seq_count = lax.axis_size("seq")
    data_count = lax.axis_size("dp")
    per_dev = image_projections.shape[1]
    image_count = image_projections.shape[2]
    width_all = image_state.shape[3]
    rollouts = per_dev * data_count
    seq_at, dp_at, c_at = lax.axis_index("seq"), lax.axis_index("dp"), lax.axis_index("cfg")
    x_at, zh_at, y_at = seq_at // ZH, seq_at % ZH, dp_at // ZL
    place = jnp.stack([x_at, zh_at, y_at, c_at]).astype(jnp.int32)

    kv_rows = image_count + text_projections.shape[2]

    group_count = rollouts // GROUP_SIZE
    member = (group_index[:, None] == jnp.arange(group_count, dtype=jnp.int32)[None, :]).astype(
        jnp.float32
    )
    column = jnp.concatenate([from_column(output_weight, d) for d in range(ZH)], axis=0)
    totals = jnp.sum(member * rewards[:, None], axis=0)
    totals = totals + from_zl(totals)
    first_part = exchange(after(pack(image_projections, text_projections), column, totals))
    totals = ring_sum(totals, from_y)
    advantage = rewards - jnp.sum(member * totals[None, :], axis=1) / GROUP_SIZE
    column = after(column, totals)
    x_parts = [from_x(column, d) for d in range(1, X)]
    first_half = jnp.concatenate([column, x_parts[0]], axis=0)
    second_half = jnp.concatenate(x_parts[1:], axis=0)
    ahead_first, behind_second = from_y(first_half, 1), from_y(second_half, -1)
    ahead_second, behind_first = from_y(second_half, 1), from_y(first_half, -1)
    plane_other = [from_cfg(first_half), from_cfg(second_half)]
    second_part = exchange(
        after(
            pack_queries(image_projections, 1),
            first_part,
            ahead_first,
            behind_second,
            *plane_other,
        )
    )
    far_first, far_second = from_y(ahead_first, 1), from_y(behind_second, -1)
    moved = [ahead_first, ahead_second, behind_first, behind_second, far_first, far_second]
    pieces = [first_half, second_half] + moved + plane_other + [from_cfg(piece) for piece in moved]

    queries_at = per_dev * 2 * kv_rows // image_count
    first_part = after(first_part, ahead_second, behind_first)
    attended = attention(first_part, queries_at, first_part, 0, image_count, kv_rows, per_dev)
    attended = attention(
        second_part, 0, first_part, 1, image_count, kv_rows, per_dev, (attended,)
    )
    spread = noise_level * jnp.sqrt(timestep / (1.0 - timestep))
    drift_gain = 1.0 + spread * spread * (1.0 - timestep) / (2.0 * timestep)
    deviation = spread * math.sqrt(step_width)
    terms = jnp.stack(
        [
            1.0 - spread * spread / (2.0 * timestep) * step_width,
            drift_gain * step_width,
            advantage / (rollouts * C) * drift_gain * step_width / (deviation * deviation),
        ]
    )

    returned = after(exchange(attended), terms)
    hidden, velocity = hidden_rows(
        place, returned, image_state, modulation[0].transpose(1, 0, 2), final_weight.T, pieces
    )
    keep, send, squares = step(
        place,
        terms,
        velocity,
        from_cfg(velocity),
        latent.transpose(0, 2, 1),
        next_latent.transpose(0, 2, 1),
        hidden,
        data_count,
    )

    kept = keep + from_cfg(send)
    share = fold(lax.all_to_all(kept, "dp", split_axis=0, concat_axis=0, tiled=True), squares)
    share = ring_sum(ring_sum(share, from_zh), from_x)
    other = from_cfg(share)
    first = c_at == 0
    half = C // 2
    gradient = jnp.concatenate(
        [jnp.where(first, share, other)[:half], jnp.where(first, other, share)[:half]], axis=0
    ).T
    square_mean = share[half : half + per_dev, 0] / (seq_count * image_count * C)
    log_prob = (
        -square_mean / (2.0 * deviation * deviation)
        - jnp.log(deviation)
        - 0.5 * math.log(2.0 * math.pi)
    )
    return (gradient, log_prob)


def solution(mesh):
    in_specs = (
        P("cfg", "dp", "seq", None),
        P("cfg", "dp", "seq", None),
        P("seq", "dp"),
        P("cfg", "dp", "seq", None),
        P("cfg", "dp", None, None),
        P(),
        P("dp", "seq", None),
        P("dp", "seq", None),
        P("dp"),
        P("dp"),
        P("dp"),
    )
    out_specs = (P("dp", None), P("dp"))
    return jax.shard_map(
        per_device, mesh=mesh, in_specs=in_specs, out_specs=out_specs, check_vma=False
    )
```

```python
import functools
import math

import jax
import jax.numpy as jnp
from jax import lax
from jax.experimental import pallas as pl
from jax.experimental.pallas import tpu as pltpu
from jax.sharding import PartitionSpec as P

C = 64
HD = 128
GROUP_SIZE = 2

cfg_scale = 4.5
noise_level = 0.7
step_width = 0.02
norm_eps = 1e-06

X, ZH, Y, ZL = 4, 4, 4, 2
VMEM_BYTES = 32 * 1024 * 1024
HIDDEN_VMEM_BYTES = 50 * 1024 * 1024
ATTENTION_STEPS = 4
FULL_VMEM_BYTES = 61 * 1024 * 1024


def from_x(value, d):
    pairs = [(((x + d) % X) * ZH + z, x * ZH + z) for x in range(X) for z in range(ZH)]
    return lax.ppermute(value, "seq", pairs)


def from_column(value, d):
    def at(core, x, z, y, zl):
        return ((core * X + x) * ZH + z) * (Y * ZL) + y * ZL + zl

    pairs = [
        (at(core if zl == core else 1 - core, x, (z + d) % ZH, y, core), at(core, x, z, y, zl))
        for core in range(2)
        for x in range(X)
        for z in range(ZH)
        for y in range(Y)
        for zl in range(ZL)
    ]
    return lax.ppermute(value, ("cfg", "seq", "dp"), pairs)


def from_zh(value, d):
    pairs = [(x * ZH + (z + d) % ZH, x * ZH + z) for x in range(X) for z in range(ZH)]
    return lax.ppermute(value, "seq", pairs)


def from_y(value, d):
    pairs = [(((y + d) % Y) * ZL + z, y * ZL + z) for y in range(Y) for z in range(ZL)]
    return lax.ppermute(value, "dp", pairs)


def from_zl(value):
    pairs = [(y * ZL + 1 - z, y * ZL + z) for y in range(Y) for z in range(ZL)]
    return lax.ppermute(value, "dp", pairs)


def from_cfg(value):
    return lax.ppermute(value, "cfg", [(0, 1), (1, 0)])


def after(value, *others):
    return lax.optimization_barrier((value,) + others)[0]


def ring_sum(value, fetch):
    first, second, third = (fetch(value, d) for d in (1, 2, 3))
    return (value + second) + (first + third)


def pack_kernel(k_ref, v_ref, kt_ref, vt_ref, q_ref, out_ref):
    rows, text = k_ref.shape[2], kt_ref.shape[2]

    def pack_head(h, carry):
        cols = pl.ds(pl.multiple_of(h * HD, HD), HD)
        at = 0
        for r in range(k_ref.shape[1]):
            for ref, count in ((k_ref, rows), (kt_ref, text), (v_ref, rows), (vt_ref, text)):
                out_ref[h, at : at + count, :] = ref[0, r, :, cols]
                at += count
        out_ref[h, at : at + rows, :] = q_ref[0, 0, :, cols]
        return carry

    lax.fori_loop(0, out_ref.shape[0], pack_head, 0)


def pack_queries_kernel(q_ref, out_ref):
    def pack_head(h, carry):
        out_ref[h] = q_ref[0, 0, :, pl.ds(pl.multiple_of(h * HD, HD), HD)]
        return carry

    lax.fori_loop(0, out_ref.shape[0], pack_head, 0)


def pack(image_projections, text_projections):
    _, per_dev, rows, width = image_projections.shape
    text = text_projections.shape[2]
    heads = width // (3 * HD)
    per = 4
    steps = heads // per
    total = per_dev * 2 * (rows + text) + rows

    def spec(rollouts, count, part):
        return pl.BlockSpec((1, rollouts, count, per * HD), lambda h: (0, 0, 0, part * steps + h))

    return pl.pallas_call(
        pack_kernel,
        grid=(steps,),
        in_specs=[
            spec(per_dev, rows, 1),
            spec(per_dev, rows, 2),
            spec(per_dev, text, 0),
            spec(per_dev, text, 1),
            spec(1, rows, 0),
        ],
        out_specs=pl.BlockSpec((per, total, HD), lambda h: (h, 0, 0)),
        out_shape=jax.ShapeDtypeStruct((heads, total, HD), jnp.bfloat16),
        compiler_params=pltpu.CompilerParams(vmem_limit_bytes=FULL_VMEM_BYTES),
        cost_estimate=pl.CostEstimate(
            flops=0, bytes_accessed=2 * heads * total * HD * 2, transcendentals=0
        ),
        name="pack",
    )(image_projections, image_projections, text_projections, text_projections, image_projections)


def pack_queries(image_projections, r):
    _, _, rows, width = image_projections.shape
    heads = width // (3 * HD)
    return pl.pallas_call(
        pack_queries_kernel,
        grid=(1,),
        in_specs=[pl.BlockSpec((1, 1, rows, heads * HD), lambda i: (0, r, 0, 0))],
        out_specs=pl.BlockSpec((heads, rows, HD), lambda i: (0, 0, 0)),
        out_shape=jax.ShapeDtypeStruct((heads, rows, HD), jnp.bfloat16),
        compiler_params=pltpu.CompilerParams(vmem_limit_bytes=VMEM_BYTES),
        cost_estimate=pl.CostEstimate(
            flops=0, bytes_accessed=2 * heads * rows * HD * 2, transcendentals=0
        ),
        name="pack_queries",
    )(image_projections)


def attention_kernel(q_ref, kv_ref, *rest):
    out_ref, keys, values = rest[-3:]
    peers, kv_rows = kv_ref.shape[0], kv_ref.shape[1] // 2

    @pl.when(pl.program_id(0) == 0)
    def _():
        ones = jnp.ones((kv_rows, HD), jnp.bfloat16)

        def place_peer(s, carry):
            at = pl.ds(pl.multiple_of(s * kv_rows, kv_rows), kv_rows)
            keys[at, :] = kv_ref[s, 0:kv_rows, :]
            values[at, 0:HD] = kv_ref[s, kv_rows : 2 * kv_rows, :]
            values[at, HD : 2 * HD] = ones
            return carry

        lax.fori_loop(0, peers, place_peer, 0)

    factor = math.log2(math.e) / math.sqrt(HD)
    for n in range(q_ref.shape[0]):
        scores = lax.dot_general(
            q_ref[n], keys[...], (((1,), (1,)), ((), ())), preferred_element_type=jnp.float32
        )
        highest = jnp.max(scores, axis=1, keepdims=True)
        powered = jnp.exp2((scores - highest) * factor).astype(jnp.bfloat16)
        sums = jnp.dot(powered, values[...], preferred_element_type=jnp.float32)
        out_ref[n] = (sums[:, 0:HD] / sums[:, HD : HD + 1]).astype(jnp.bfloat16)


def attention(queries, q_at, key_values, r, rows, kv_rows, per_dev, earlier=()):
    peers = queries.shape[0]
    return pl.pallas_call(
        attention_kernel,
        grid=(ATTENTION_STEPS,),
        in_specs=[
            pl.BlockSpec((peers // ATTENTION_STEPS, rows, HD), lambda i: (i, q_at, 0)),
            pl.BlockSpec((peers, 2 * kv_rows, HD), lambda i: (0, r, 0)),
        ]
        + [pl.BlockSpec(memory_space=pl.ANY)] * len(earlier),
        out_specs=pl.BlockSpec((peers // ATTENTION_STEPS, rows, HD), lambda i: (i, r, 0)),
        out_shape=jax.ShapeDtypeStruct((peers, per_dev * rows, HD), jnp.bfloat16),
        scratch_shapes=[
            pltpu.VMEM((peers * kv_rows, HD), jnp.bfloat16),
            pltpu.VMEM((peers * kv_rows, 2 * HD), jnp.bfloat16),
        ],
        input_output_aliases={2: 0} if earlier else {},
        compiler_params=pltpu.CompilerParams(vmem_limit_bytes=FULL_VMEM_BYTES),
        cost_estimate=pl.CostEstimate(
            flops=8 * peers * rows * peers * kv_rows * HD,
            bytes_accessed=2 * peers * (2 * rows + 2 * kv_rows) * HD,
            transcendentals=peers * rows * peers * kv_rows,
        ),
        name=f"attention{r}",
    )(queries, key_values, *earlier)


SPANS = ((0, 0), (0, 2), (1, 0), (1, 2), (3, 0), (3, 2), (2, 0), (2, 2))


def hidden_kernel(place, heads_ref, state_any, mods_any, final_any, *rest):
    pieces = rest[: 2 * len(SPANS)]
    hidden_ref, velocity_ref, flat, mixed, weights, state_ref, mods_ref, final_ref, sems = rest[
        2 * len(SPANS) :
    ]
    x_at, zh_at, y_at, c_at = place[0], place[1], place[2], place[3]
    per_dev, rows = state_ref.shape[1], state_ref.shape[2]
    width = weights.shape[2]
    part = weights.shape[1] // X

    def begin(source, target, n):
        copy = pltpu.make_async_copy(source, target, sems.at[n])
        copy.start()
        return copy

    copies = []
    for n, piece in enumerate(pieces):
        core, (turn, first) = n // len(SPANS), SPANS[n % len(SPANS)]
        target = weights.at[core * Y + turn, pl.ds(first * part, piece.shape[0])]
        copies.append(begin(piece, target, n))
        if n == 1:
            mods_copy = begin(mods_any, mods_ref, len(pieces))
            state_copy = begin(state_any, state_ref, len(pieces) + 1)
    final_copy = begin(final_any, final_ref, len(pieces) + 2)
    for i in range(X):
        for j in range(ZH):
            head = lax.rem(x_at + i, X) * ZH + lax.rem(zh_at + j, ZH)
            k = i * ZH + j
            flat[:, k * HD : (k + 1) * HD] = heads_ref[head]
    row_sum = jnp.zeros((per_dev * rows, 1), jnp.float32)
    square_sum = jnp.zeros((per_dev * rows, 1), jnp.float32)
    for core in range(2):
        core_at = c_at if core == 0 else 1 - c_at
        for turn in (0, 1, 3, 2):
            for n, (of_turn, _) in enumerate(SPANS):
                if of_turn == turn:
                    copies[core * len(SPANS) + n].wait()
            at = pl.ds(pl.multiple_of((lax.rem(y_at + turn, Y) * ZL + core_at) * width, 128), width)
            projected = jnp.dot(
                flat[...], weights[core * Y + turn], preferred_element_type=jnp.float32
            )
            if core == 0 and turn == 0:
                mods_copy.wait()
                state_copy.wait()
            for r in range(per_dev):
                gate = mods_ref[0, r : r + 1, at].astype(jnp.float32)
                mixed[r * rows : (r + 1) * rows, at] = (
                    state_ref[0, r, :, at].astype(jnp.float32)
                    + gate * projected[r * rows : (r + 1) * rows]
                )
            block = mixed[:, at]
            row_sum = row_sum + jnp.sum(block, axis=1, keepdims=True)
            square_sum = square_sum + jnp.sum(block * block, axis=1, keepdims=True)
    width_all = mixed.shape[1]
    center = row_sum / width_all
    square = square_sum / width_all
    inverse = lax.rsqrt(square - center * center + norm_eps)
    for r in range(per_dev):
        at = slice(r * rows, (r + 1) * rows)
        scale = 1.0 + mods_ref[2, r : r + 1, :].astype(jnp.float32)
        shift = mods_ref[1, r : r + 1, :].astype(jnp.float32)
        hidden_ref[at, :] = (
            (mixed[at, :] - center[at]) * inverse[at] * scale + shift
        ).astype(jnp.bfloat16)
    final_copy.wait()
    velocity_ref[...] = lax.dot_general(
        final_ref[...], hidden_ref[...], (((1,), (1,)), ((), ())), preferred_element_type=jnp.float32
    )


def hidden_rows(place, heads_part, image_state, modulation, final_weight, pieces):
    heads, all_rows, _ = heads_part.shape
    width_all = image_state.shape[3]
    vmem = pl.BlockSpec(memory_space=pltpu.VMEM)
    return pl.pallas_call(
        hidden_kernel,
        in_specs=[pl.BlockSpec(memory_space=pltpu.SMEM)]
        + [vmem]
        + [pl.BlockSpec(memory_space=pl.ANY)] * (3 + len(pieces)),
        out_specs=[vmem] * 2,
        out_shape=[
            jax.ShapeDtypeStruct((all_rows, width_all), jnp.bfloat16),
            jax.ShapeDtypeStruct((C, all_rows), jnp.float32),
        ],
        scratch_shapes=[
            pltpu.VMEM((all_rows, heads * HD), jnp.bfloat16),
            pltpu.VMEM((all_rows, width_all), jnp.float32),
            pltpu.VMEM((8, heads * HD, pieces[0].shape[1]), jnp.bfloat16),
            pltpu.VMEM(image_state.shape, jnp.bfloat16),
            pltpu.VMEM(modulation.shape, jnp.bfloat16),
            pltpu.VMEM(final_weight.shape, jnp.bfloat16),
            pltpu.SemaphoreType.DMA((len(pieces) + 3,)),
        ],
        compiler_params=pltpu.CompilerParams(vmem_limit_bytes=HIDDEN_VMEM_BYTES),
        cost_estimate=pl.CostEstimate(
            flops=2 * all_rows * heads * HD * width_all,
            bytes_accessed=2 * heads * HD * width_all,
            transcendentals=0,
        ),
        name="hidden",
    )(place, heads_part, image_state, modulation, final_weight, *pieces)


def step_kernel(
    place,
    terms,
    own_ref,
    partner_ref,
    latent_ref,
    next_ref,
    hidden_ref,
    keep_ref,
    send_ref,
    squares_ref,
):
    first = place[3] == 0
    own, partner = own_ref[...], partner_ref[...]
    conditional = jnp.where(first, own, partner)
    unconditional = jnp.where(first, partner, own)
    guided = unconditional + cfg_scale * (conditional - unconditional)
    per_dev, _, rows = latent_ref.shape
    row = lax.broadcasted_iota(jnp.int32, squares_ref.shape, 0)
    squares = jnp.zeros(squares_ref.shape, jnp.float32)
    slopes = []
    for r in range(per_dev):
        step_mean = (
            latent_ref[r] * terms[0, r] - guided[:, r * rows : (r + 1) * rows] * terms[1, r]
        )
        residue = next_ref[r] - step_mean
        squares = jnp.where(row == r, jnp.sum(residue * residue), squares)
        slopes.append(terms[2, r] * residue)
    squares_ref[...] = squares
    own_slopes = jnp.where(first, cfg_scale, 1.0 - cfg_scale) * jnp.concatenate(slopes, axis=1)
    half = own_slopes.shape[0] // 2
    low, high = own_slopes[:half], own_slopes[half:]
    ordered = jnp.concatenate([jnp.where(first, low, high), jnp.where(first, high, low)], axis=0)
    partial = jnp.dot(
        ordered.astype(jnp.bfloat16), hidden_ref[...], preferred_element_type=jnp.float32
    )
    width = keep_ref.shape[2]
    for n in range(keep_ref.shape[0]):
        cols = slice(n * width, (n + 1) * width)
        keep_ref[n] = partial[:half, cols]
        send_ref[n] = partial[half:, cols]


def step(place, terms, own, partner, latent, next_latent, hidden, data_count):
    rows, width_all = hidden.shape
    cut = (data_count, C // 2, width_all // data_count)
    smem = pl.BlockSpec(memory_space=pltpu.SMEM)
    vmem = pl.BlockSpec(memory_space=pltpu.VMEM)
    return pl.pallas_call(
        step_kernel,
        in_specs=[smem] * 2 + [vmem] * 5,
        out_specs=[vmem] * 3,
        out_shape=[
            jax.ShapeDtypeStruct(cut, jnp.float32),
            jax.ShapeDtypeStruct(cut, jnp.float32),
            jax.ShapeDtypeStruct((8, 128), jnp.float32),
        ],
        compiler_params=pltpu.CompilerParams(vmem_limit_bytes=VMEM_BYTES),
        cost_estimate=pl.CostEstimate(
            flops=2 * rows * C * width_all, bytes_accessed=2 * rows * width_all, transcendentals=0
        ),
        name="step",
    )(place, terms, own, partner, latent, next_latent, hidden)


def fold_kernel(parts_ref, squares_ref, out_ref):
    count, width = parts_ref.shape[1], parts_ref.shape[2]
    out_ref[0:count, :] = jnp.sum(parts_ref[...], axis=0)
    out_ref[count : count + 8, 128:width] = jnp.zeros((8, width - 128), jnp.float32)
    out_ref[count : count + 8, 0:128] = squares_ref[...]


def fold(parts, squares):
    _, count, width = parts.shape
    vmem = pl.BlockSpec(memory_space=pltpu.VMEM)
    return pl.pallas_call(
        fold_kernel,
        in_specs=[vmem] * 2,
        out_specs=vmem,
        out_shape=jax.ShapeDtypeStruct((count + 8, width), jnp.float32),
        name="fold",
    )(parts, squares)


def exchange(send):
    return lax.all_to_all(send, "seq", split_axis=0, concat_axis=0, tiled=True)


def per_device(
    image_projections,
    text_projections,
    output_weight,
    image_state,
    modulation,
    final_weight,
    latent,
    next_latent,
    timestep,
    rewards,
    group_index,
):
    seq_count = lax.axis_size("seq")
    data_count = lax.axis_size("dp")
    per_dev = image_projections.shape[1]
    image_count = image_projections.shape[2]
    width_all = image_state.shape[3]
    rollouts = per_dev * data_count
    seq_at, dp_at, c_at = lax.axis_index("seq"), lax.axis_index("dp"), lax.axis_index("cfg")
    x_at, zh_at, y_at = seq_at // ZH, seq_at % ZH, dp_at // ZL
    place = jnp.stack([x_at, zh_at, y_at, c_at]).astype(jnp.int32)

    kv_rows = image_count + text_projections.shape[2]

    group_count = rollouts // GROUP_SIZE
    member = (group_index[:, None] == jnp.arange(group_count, dtype=jnp.int32)[None, :]).astype(
        jnp.float32
    )
    column = jnp.concatenate([from_column(output_weight, d) for d in range(ZH)], axis=0)
    totals = jnp.sum(member * rewards[:, None], axis=0)
    totals = totals + from_zl(totals)
    first_part = exchange(after(pack(image_projections, text_projections), column, totals))
    totals = ring_sum(totals, from_y)
    advantage = rewards - jnp.sum(member * totals[None, :], axis=1) / GROUP_SIZE
    column = after(column, totals)
    x_parts = [from_x(column, d) for d in range(1, X)]
    first_half = jnp.concatenate([column, x_parts[0]], axis=0)
    second_half = jnp.concatenate(x_parts[1:], axis=0)
    ahead_first, behind_second = from_y(first_half, 1), from_y(second_half, -1)
    ahead_second, behind_first = from_y(second_half, 1), from_y(first_half, -1)
    plane_other = [from_cfg(first_half), from_cfg(second_half)]
    second_part = exchange(
        after(
            pack_queries(image_projections, 1),
            first_part,
            ahead_first,
            behind_second,
            *plane_other,
        )
    )
    far_first, far_second = from_y(ahead_first, 1), from_y(behind_second, -1)
    moved = [ahead_first, ahead_second, behind_first, behind_second, far_first, far_second]
    pieces = [first_half, second_half] + moved + plane_other + [from_cfg(piece) for piece in moved]

    queries_at = per_dev * 2 * kv_rows // image_count
    first_part = after(first_part, ahead_second, behind_first)
    attended = attention(first_part, queries_at, first_part, 0, image_count, kv_rows, per_dev)
    attended = attention(
        second_part, 0, first_part, 1, image_count, kv_rows, per_dev, (attended,)
    )
    spread = noise_level * jnp.sqrt(timestep / (1.0 - timestep))
    drift_gain = 1.0 + spread * spread * (1.0 - timestep) / (2.0 * timestep)
    deviation = spread * math.sqrt(step_width)
    terms = jnp.stack(
        [
            1.0 - spread * spread / (2.0 * timestep) * step_width,
            drift_gain * step_width,
            advantage / (rollouts * C) * drift_gain * step_width / (deviation * deviation),
        ]
    )

    returned = after(exchange(after(attended, far_first, far_second)), terms)
    hidden, velocity = hidden_rows(
        place, returned, image_state, modulation[0].transpose(1, 0, 2), final_weight.T, pieces
    )
    keep, send, squares = step(
        place,
        terms,
        velocity,
        from_cfg(velocity),
        latent.transpose(0, 2, 1),
        next_latent.transpose(0, 2, 1),
        hidden,
        data_count,
    )

    kept = keep + from_cfg(send)
    share = fold(lax.all_to_all(kept, "dp", split_axis=0, concat_axis=0, tiled=True), squares)
    share = ring_sum(ring_sum(share, from_zh), from_x)
    other = from_cfg(share)
    first = c_at == 0
    half = C // 2
    gradient = jnp.concatenate(
        [jnp.where(first, share, other)[:half], jnp.where(first, other, share)[:half]], axis=0
    ).T
    square_mean = share[half : half + per_dev, 0] / (seq_count * image_count * C)
    log_prob = (
        -square_mean / (2.0 * deviation * deviation)
        - jnp.log(deviation)
        - 0.5 * math.log(2.0 * math.pi)
    )
    return (gradient, log_prob)


def solution(mesh):
    in_specs = (
        P("cfg", "dp", "seq", None),
        P("cfg", "dp", "seq", None),
        P("seq", "dp"),
        P("cfg", "dp", "seq", None),
        P("cfg", "dp", None, None),
        P(),
        P("dp", "seq", None),
        P("dp", "seq", None),
        P("dp"),
        P("dp"),
        P("dp"),
    )
    out_specs = (P("dp", None), P("dp"))
    return jax.shard_map(
        per_device, mesh=mesh, in_specs=in_specs, out_specs=out_specs, check_vma=False
    )
```
